256 devices in a mesh: grp: 16 (over z_hi, y, core), dev: 16 (over z_lo, x).
Axes of the slice: x: 4, y: 4, z: 8 (z_hi: 2, z_lo: 4; z = z_hi * 4 + z_lo), core: 2. Of those that a mesh axis runs over, the one named last changes fastest.
Arguments:
- inputs: bfloat16 [1024, 32, 32, 128], P(('grp', 'dev')), may hold values from -6 to 6
- cotangent: bfloat16 [1024, 32, 32, 128], P(('grp', 'dev')), may hold values from -0.09375 to 0.09375
- weights: bfloat16 [2, 1152, 128], replicated, may hold values from -0.1875 to 0.1875
- master: float32 [2, 1152, 128], P(None, 'dev'), may hold values from -0.1875 to 0.1875
- first_moment: float32 [2, 1152, 128], P(None, 'dev'), may hold values from -2 to 2
- second_moment: float32 [2, 1152, 128], P(None, 'dev'), may hold values from 0.1 to 1
Outputs:
- new_weights: bfloat16 [2, 1152, 128], replicated
- new_master: float32 [2, 1152, 128], P(None, 'dev')
- new_first: float32 [2, 1152, 128], P(None, 'dev')
- new_second: float32 [2, 1152, 128], P(None, 'dev')
The draws below stay inside these ranges and needn't reach their ends.
All inputs are finite; a program needn't handle non-finite values.
Results may differ from the reference program's by a relative error of at most 0.0034.
Values may be sent and summed in bfloat16 or wider, within the bound.
A program may use at most 128 MiB of HBM per device.

```python
import math
import jax
import jax.numpy as jnp
from jax import lax

C = 128
LAYERS = 2
H = 32
W = 32
B_DEV = 4
STEP = 10
KC = 1152
SAMPLES = 1024
N_GRP = 16
N_DEV = 16


def steps_of(stream_key, extent, shards, least, top_value):
    factor_of = 1.0
    for axis_at, blocks in shards:
        steps = jax.random.uniform(jax.random.fold_in(jax.random.fold_in(stream_key, 6), axis_at), (blocks,), jnp.float32, least / len(shards), top_value / len(shards))
        factor_of = factor_of * jnp.repeat(jnp.exp(steps), extent[axis_at] // blocks).reshape((-1,) + (1,) * (len(extent) - 1 - axis_at))
    return factor_of


def normal_values(own_key, extent, scale, bound, split=(), dtype=jnp.bfloat16):
    level = steps_of(own_key, extent, split, -0.22, 0.18) if split else 1.0
    entries = jax.random.normal(own_key, extent, jnp.float32) * scale * level
    return jnp.minimum(jnp.maximum(entries, -bound), bound).astype(dtype)


def setup_inputs(seed: int = 0) -> dict:
    splits = jax.random.split(jax.random.key(seed), 7)
    return {
        "inputs": normal_values(splits[0], (SAMPLES, H, W, C), 1.0, 6.0, ((0, 256),)),
        "cotangent": normal_values(splits[1], (SAMPLES, H, W, C), (1.0 / (B_DEV * H * W) ** 0.5), 0.09375, ((0, 256),)),
        "weights": normal_values(splits[2], (LAYERS, KC, C), KC ** -0.5, 0.1875),
        "master": normal_values(splits[3], (LAYERS, KC, C), KC ** -0.5, 0.1875, ((1, 16),), jnp.float32),
        "first_moment": normal_values(splits[4], (LAYERS, KC, C), 0.3, 2.0, ((1, 16),), jnp.float32),
        "second_moment": jnp.clip(jnp.exp(math.log(1.0) - 2.3025851 * jax.random.uniform(splits[5], (LAYERS, KC, C), jnp.float32) ** steps_of(splits[5], (LAYERS, KC, C), ((1, 16),), -0.2, 0.2)), 0.1, 1.0),
    }


def patches(feat):
    height, width = (feat.shape[1], feat.shape[2])
    padded = jnp.pad(feat, ((0, 0), (1, 1), (1, 1), (0, 0)))
    taps = [padded[:, ti:ti + height, tj:tj + width, :] for ti in range(3) for tj in range(3)]
    return jnp.concatenate(taps, axis=-1).reshape(-1, 9 * feat.shape[3])

def back_taps(cot_rows, kernel, shape):
    batch, height, width, chans = shape
    kernel3 = kernel.reshape(9, chans, -1)
    padded = jnp.zeros((batch, height + 2, width + 2, chans), jnp.float32)
    for tap in range(9):
        ti, tj = (tap // 3, tap % 3)
        part = jnp.dot(cot_rows, kernel3[tap].T, preferred_element_type=jnp.float32)
        padded = padded.at[:, ti:ti + height, tj:tj + width, :].add(part.reshape(batch, height, width, chans))
    return padded[:, 1:-1, 1:-1, :]

def local_grads(feat, cot, kernel_one, kernel_two):
    shape = feat.shape
    rows = shape[0] * shape[1] * shape[2]
    cols_in = patches(feat)
    pre = jnp.dot(cols_in, kernel_one, preferred_element_type=jnp.float32)
    act = jax.nn.silu(pre).astype(jnp.bfloat16)
    cols_act = patches(act.reshape(shape))
    cot_rows = cot.reshape(rows, shape[3])
    grad_second = lax.dot_general(cols_act, cot_rows, (((0,), (0,)), ((), ())), preferred_element_type=jnp.float32)
    back = back_taps(cot_rows, kernel_two, shape).reshape(rows, shape[3])
    sig = jax.nn.sigmoid(pre)
    dpre = (back * sig * (1.0 + pre * (1.0 - sig))).astype(jnp.bfloat16)
    grad_first = lax.dot_general(cols_in, dpre, (((0,), (0,)), ((), ())), preferred_element_type=jnp.float32)
    return (grad_first, grad_second)

def adamw(grad, master_part, first_part, second_part, step_count):
    first_new = 0.9 * first_part + 0.1 * grad
    second_new = 0.95 * second_part + 0.05 * grad * grad
    corr_one = 1.0 - 0.9 ** step_count
    corr_two = 1.0 - 0.95 ** step_count
    update = first_new / corr_one / (jnp.sqrt(second_new / corr_two) + 1e-08)
    master_new = master_part - 0.001 * (update + 0.1 * master_part)
    return (master_new, first_new, second_new)

def reference(inputs, cotangent, weights, master, first_moment, second_moment):
    blocks = N_GRP * N_DEV
    feats = inputs.reshape(blocks, B_DEV, H, W, C)
    cots = cotangent.reshape(blocks, B_DEV, H, W, C)

    def accumulate(carry, pair):
        grad_first, grad_second = local_grads(pair[0], pair[1], weights[0], weights[1])
        return ((carry[0] + grad_first, carry[1] + grad_second), None)
    zeros = jnp.zeros((KC, C), jnp.float32)
    (grad_first, grad_second), unused = lax.scan(accumulate, (zeros, zeros), (feats, cots))
    grads = [grad_first, grad_second]
    masters, firsts, seconds = ([], [], [])
    for layer in range(LAYERS):
        result = adamw(grads[layer], master[layer], first_moment[layer], second_moment[layer], STEP)
        masters.append(result[0])
        firsts.append(result[1])
        seconds.append(result[2])
    new_master = jnp.stack(masters)
    return (new_master.astype(jnp.bfloat16), new_master, jnp.stack(firsts), jnp.stack(seconds))
```

```python
import jax
import jax.numpy as jnp
from jax import lax
from jax.experimental import pallas as pl
from jax.experimental.pallas import tpu as pltpu
from jax.sharding import PartitionSpec as P

STEP = 10
MESH = pl.DeviceIdType.MESH
N_DEV = 16
ROWS = 72
SLAB = 80


def patches(feat):
    height, width = (feat.shape[1], feat.shape[2])
    padded = jnp.pad(feat, ((0, 0), (1, 1), (1, 1), (0, 0)))
    taps = [padded[:, ti : ti + height, tj : tj + width, :] for ti in range(3) for tj in range(3)]
    return jnp.concatenate(taps, axis=-1).reshape(-1, 9 * feat.shape[3])


def flipped_kernel(kernel):
    chans = kernel.shape[1]
    blocks = kernel.reshape(9, chans, chans)[::-1]
    return blocks.transpose(0, 2, 1).reshape(9 * chans, chans)


def adamw(grad, master_part, first_part, second_part):
    first_new = 0.9 * first_part + 0.1 * grad
    second_new = 0.95 * second_part + 0.05 * grad * grad
    corr_one = 1.0 - 0.9**STEP
    corr_two = 1.0 - 0.95**STEP
    update = first_new / corr_one / (jnp.sqrt(second_new / corr_two) + 1e-08)
    master_new = master_part - 0.001 * (update + 0.1 * master_part)
    return (master_new, first_new, second_new)


def comm_kernel(grad_ref, master_ref, first_ref, second_ref,
                weights_ref, master_out, first_out, second_out,
                pair_recv, dev_send, dev_recv, own_sum, col_buf, col_sum, hi_recv, total, other, gathered,
                pair_ss, pair_rs, dev_ss, dev_rs, col_ss, col_rs, hi_ss, hi_rs, tot_ss, tot_rs,
                gat_ss, gat_rs, fwd_ss, fwd_rs):
    grp = lax.axis_index("grp")
    dev = lax.axis_index("dev")
    core = lax.rem(grp, 2)
    col = lax.rem(grp, 8) // 2
    high = grp // 8
    partner = (grp + 1 - 2 * core, dev)
    opposite = (lax.rem(grp + 8, 16), dev)

    def dev_peer(step):
        return (grp, lax.rem(dev + step, N_DEV))

    def col_peer(step):
        return (high * 8 + lax.rem(col + step, 4) * 2 + core, dev)

    def remote(src, dst, ss, rs, target):
        return pltpu.make_async_remote_copy(
            src_ref=src, dst_ref=dst, send_sem=ss, recv_sem=rs, device_id=target, device_id_type=MESH
        )

    barrier = pltpu.get_barrier_semaphore()
    peers = [partner, opposite] + [dev_peer(k) for k in range(1, N_DEV)] + [col_peer(k) for k in range(1, 4)]
    for peer in peers:
        pl.semaphore_signal(barrier, inc=1, device_id=peer, device_id_type=MESH)
    pl.semaphore_wait(barrier, len(peers))

    def shard_rows(step):
        start = lax.rem(dev + step, N_DEV) * ROWS
        return pl.ds(pl.multiple_of(start, 8), ROWS)

    order = list(range(1, N_DEV)) + [0]
    pair = {}
    for k in order:
        pair[k] = remote(grad_ref.at[1 - core, shard_rows(k), :], pair_recv.at[k], pair_ss.at[k], pair_rs.at[k], partner)
        pair[k].start()
    sends = []
    for k in order:
        pair[k].wait_recv()
        summed = grad_ref[core, shard_rows(k), :] + pair_recv[k]
        if k == 0:
            own_sum[...] = summed
        else:
            dev_send[k, 0:ROWS, :] = summed.astype(jnp.bfloat16)
            copy = remote(dev_send.at[k], dev_recv.at[k], dev_ss.at[k], dev_rs.at[k], dev_peer(k))
            copy.start()
            sends.append(copy)
    acc = own_sum[...]
    for copy, k in zip(sends, range(1, N_DEV)):
        copy.wait_recv()
        acc = acc + dev_recv[k, 0:ROWS, :].astype(jnp.float32)
    col_buf[col] = acc
    cols = []
    for k in range(1, 4):
        copy = remote(col_buf.at[col], col_buf.at[col], col_ss.at[k], col_rs.at[k], col_peer(k))
        copy.start()
        cols.append(copy)
    for k in range(1, 4):
        source = lax.rem(col + 4 - k, 4)
        remote(col_buf.at[source], col_buf.at[source], col_ss.at[k], col_rs.at[k], col_peer(k)).wait_recv()
    for copy in cols:
        copy.wait_send()
    col_sum[...] = (col_buf[0] + col_buf[1]) + (col_buf[2] + col_buf[3])
    hi = remote(col_sum, hi_recv, hi_ss, hi_rs, opposite)
    hi.start()
    hi.wait_recv()
    total[...] = col_sum[...] + hi_recv[...]
    tot = remote(total, other, tot_ss, tot_rs, partner)
    tot.start()
    master_new, first_new, second_new = adamw(total[...], master_ref[core], first_ref[core], second_ref[core])
    gathered[core, dev, 0:ROWS, :] = master_new.astype(jnp.bfloat16)
    mine = gathered.at[core, dev]
    gats = []
    for k in range(1, N_DEV):
        copy = remote(mine, mine, gat_ss.at[k], gat_rs.at[k], dev_peer(k))
        copy.start()
        gats.append(copy)
    fwds = [remote(mine, mine, fwd_ss.at[0], fwd_rs.at[0], partner)]
    fwds[0].start()
    master_out[core] = master_new
    first_out[core] = first_new
    second_out[core] = second_new
    tot.wait_recv()
    other_new = adamw(other[...], master_ref[1 - core], first_ref[1 - core], second_ref[1 - core])
    master_out[1 - core] = other_new[0]
    first_out[1 - core] = other_new[1]
    second_out[1 - core] = other_new[2]
    for k in range(1, N_DEV):
        source = lax.rem(dev + N_DEV - k, N_DEV)
        slot = gathered.at[core, source]
        remote(slot, slot, gat_ss.at[k], gat_rs.at[k], dev_peer(k)).wait_recv()
        fwd = remote(slot, slot, fwd_ss.at[k], fwd_rs.at[k], partner)
        fwd.start()
        fwds.append(fwd)
    for k in range(N_DEV):
        source = lax.rem(dev + N_DEV - k, N_DEV)
        slot = gathered.at[1 - core, source]
        remote(slot, slot, fwd_ss.at[k], fwd_rs.at[k], partner).wait_recv()
    for layer in range(2):
        for two in range(N_DEV // 2):
            even = gathered[layer, 2 * two, 0:ROWS, :].astype(jnp.float32)
            odd = gathered[layer, 2 * two + 1, 0:ROWS, :].astype(jnp.float32)
            both = jnp.concatenate([even, odd], axis=0).astype(jnp.bfloat16)
            weights_ref[layer, 2 * ROWS * two : 2 * ROWS * (two + 1), :] = both
    for copy in [pair[k] for k in order] + sends + gats + fwds + [hi, tot]:
        copy.wait_send()


def reduce_update(grads, master, first_moment, second_moment):
    whole = pl.BlockSpec(memory_space=pltpu.VMEM)
    state = jax.ShapeDtypeStruct(master.shape, jnp.float32)
    dma = pltpu.SemaphoreType.DMA
    return pl.pallas_call(
        comm_kernel,
        out_shape=(jax.ShapeDtypeStruct(grads.shape, jnp.bfloat16), state, state, state),
        in_specs=[whole] * 4,
        out_specs=(whole,) * 4,
        scratch_shapes=[
            pltpu.VMEM((N_DEV, ROWS, 128), jnp.float32),
            pltpu.VMEM((N_DEV, SLAB, 128), jnp.bfloat16),
            pltpu.VMEM((N_DEV, SLAB, 128), jnp.bfloat16),
            pltpu.VMEM((ROWS, 128), jnp.float32),
            pltpu.VMEM((4, ROWS, 128), jnp.float32),
            pltpu.VMEM((ROWS, 128), jnp.float32),
            pltpu.VMEM((ROWS, 128), jnp.float32),
            pltpu.VMEM((ROWS, 128), jnp.float32),
            pltpu.VMEM((ROWS, 128), jnp.float32),
            pltpu.VMEM((2, N_DEV, SLAB, 128), jnp.bfloat16),
            dma((N_DEV,)), dma((N_DEV,)), dma((N_DEV,)), dma((N_DEV,)),
            dma((4,)), dma((4,)), dma, dma, dma, dma,
            dma((N_DEV,)), dma((N_DEV,)), dma((N_DEV,)), dma((N_DEV,)),
        ],
        compiler_params=pltpu.CompilerParams(collective_id=0, has_side_effects=True, vmem_limit_bytes=32 * 2**20),
        name="reduce_update",
    )(grads, master, first_moment, second_moment)


def shards(inputs, cotangent, weights, master, first_moment, second_moment):
    shape = inputs.shape
    rows = shape[0] * shape[1] * shape[2]
    cols_in = patches(inputs)
    pre = jnp.dot(cols_in, weights[0], preferred_element_type=jnp.float32)
    act = jax.nn.silu(pre).astype(jnp.bfloat16)
    cols_act = patches(act.reshape(shape))
    cot_rows = cotangent.reshape(rows, shape[3])
    grad_second = lax.dot_general(
        cols_act, cot_rows, (((0,), (0,)), ((), ())), preferred_element_type=jnp.float32
    )
    cols_cot = patches(cotangent)
    back = jnp.dot(cols_cot, flipped_kernel(weights[1]), preferred_element_type=jnp.float32)
    sig = jax.nn.sigmoid(pre)
    dpre = (back * sig * (1.0 + pre * (1.0 - sig))).astype(jnp.bfloat16)
    grad_first = lax.dot_general(
        cols_in, dpre, (((0,), (0,)), ((), ())), preferred_element_type=jnp.float32
    )
    grads = jnp.stack([grad_first, grad_second])
    return reduce_update(grads, master, first_moment, second_moment)


def solution(mesh):
    placed = (
        P(("grp", "dev"), None, None, None),
        P(("grp", "dev"), None, None, None),
        P(),
        P(None, "dev", None),
        P(None, "dev", None),
        P(None, "dev", None),
    )
    return jax.shard_map(
        shards,
        mesh=mesh,
        in_specs=placed,
        out_specs=(P(), P(None, "dev", None), P(None, "dev", None), P(None, "dev", None)),
        check_vma=False,
    )
```

```python
import jax
import jax.numpy as jnp
from jax import lax
from jax.experimental import pallas as pl
from jax.experimental.pallas import tpu as pltpu
from jax.sharding import PartitionSpec as P

STEP = 10
MESH = pl.DeviceIdType.MESH
BF16, F32 = jnp.bfloat16, jnp.float32
BATCH, CHANS = 4, 128
ROWS = 72
SLAB = 80
PART = 9
PAD = 16


def adamw(grad, master_part, first_part, second_part):
    first_new = 0.9 * first_part + 0.1 * grad
    second_new = 0.95 * second_part + 0.05 * grad * grad
    corr_one = 1.0 - 0.9**STEP
    corr_two = 1.0 - 0.95**STEP
    update = first_new / corr_one / (jnp.sqrt(second_new / corr_two) + 1e-08)
    master_new = master_part - 0.001 * (update + 0.1 * master_part)
    return (master_new, first_new, second_new)


def swap_pairs(tiles):
    row = lax.broadcasted_iota(jnp.int32, tiles[0].shape, 1)
    low = row < 4
    half = [
        jnp.where(low, tiles[0], pltpu.roll(tiles[2], 4, 1)),
        jnp.where(low, tiles[1], pltpu.roll(tiles[3], 4, 1)),
        jnp.where(low, pltpu.roll(tiles[0], 4, 1), tiles[2]),
        jnp.where(low, pltpu.roll(tiles[1], 4, 1), tiles[3]),
    ]
    even = lax.rem(row, 4) < 2
    return [
        jnp.where(even, half[0], pltpu.roll(half[1], 2, 1)),
        jnp.where(even, pltpu.roll(half[0], 6, 1), half[1]),
        jnp.where(even, half[2], pltpu.roll(half[3], 2, 1)),
        jnp.where(even, pltpu.roll(half[2], 6, 1), half[3]),
    ]


def shift_store(src_ref, dst_ref, image):
    col = lax.broadcasted_iota(jnp.int32, (16, 32, CHANS), 1)
    for odd in range(2):
        rows = src_ref[image, :, odd]
        wide = rows.astype(F32)
        left = jnp.where(col == 0, 0.0, pltpu.roll(wide, 1, 1)).astype(BF16)
        right = jnp.where(col == 31, 0.0, pltpu.roll(wide, 31, 1)).astype(BF16)
        place = pl.ds(odd, 16)
        dst_ref[image, 1 - odd, place, :, 0:128] = left
        dst_ref[image, 1 - odd, place, :, 128:256] = rows
        dst_ref[image, 1 - odd, place, :, 256:384] = right
    zero = jnp.zeros((32, 3 * CHANS), BF16)
    dst_ref[image, 0, 0] = zero
    dst_ref[image, 1, 16] = zero


def four_rows(ref, image):
    return jnp.concatenate(
        [ref[image, k % 2, pl.ds(k // 2, 16)].reshape(512, 3 * CHANS) for k in range(4)], axis=1
    )


def pair_weights(w_ref, forward_ref, backward_ref):
    zero = jnp.zeros((CHANS, CHANS), BF16)
    for k in range(4):
        for tj in range(3):
            rows = pl.ds((k * 3 + tj) * CHANS, CHANS)
            for odd in range(2):
                cols = pl.ds(odd * CHANS, CHANS)
                if 0 <= k - odd <= 2:
                    tap = (k - odd) * 3 + tj
                    forward_ref[rows, cols] = w_ref[0, tap * CHANS : (tap + 1) * CHANS, :]
                    tap = (odd - k + 2) * 3 + 2 - tj
                    block = w_ref[1, tap * CHANS : (tap + 1) * CHANS, :]
                    backward_ref[rows, cols] = block.astype(F32).T.astype(BF16)
                else:
                    forward_ref[rows, cols] = zero
                    backward_ref[rows, cols] = zero


def outer_sum(lhs_ref, ref):
    rhs = jnp.concatenate([four_rows(ref, image) for image in range(BATCH)], axis=0)
    lhs = lhs_ref[...].reshape(BATCH * 512, 2 * CHANS)
    return lax.dot_general(lhs, rhs, (((0,), (0,)), ((), ())), preferred_element_type=F32)


def step_kernel(x_ref, c_ref, w_ref, master_ref, first_ref, second_ref,
                gathered_out, totals_out,
                x3, c3, forward_w, backward_w, act, slope, dpre, grads,
                pair_recv, xy_send, xy_recv, xy_own, sums, z_send, z_recv, part, new_part,
                w_parts, t_parts, whole_w, totals, gathered,
                pair_ss, pair_rs, xy_ss, xy_rs, z_ss, z_rs, w_ss, w_rs, t_ss, t_rs, tot_ss, tot_rs,
                gat_ss, gat_rs, fwd_ss, fwd_rs):
    grp = lax.axis_index("grp")
    dev = lax.axis_index("dev")
    core = lax.rem(grp, 2)
    y = lax.rem(grp, 8) // 2
    z_hi = grp // 8
    x = lax.rem(dev, 4)
    z_lo = dev // 4
    z = z_hi * 4 + z_lo
    partner = (grp + 1 - 2 * core, dev)

    def xy_peer(kx, ky):
        return (z_hi * 8 + lax.rem(y + ky, 4) * 2 + core, z_lo * 4 + lax.rem(x + kx, 4))

    def z_peer(kz):
        other = lax.rem(z + kz, 8)
        return (other // 4 * 8 + y * 2 + core, lax.rem(other, 4) * 4 + x)

    def z_slot(place):
        return lax.rem(place, 4) * 2 + place // 4

    def t_peer(ky, kh):
        return (lax.rem(z_hi + kh, 2) * 8 + lax.rem(y + ky, 4) * 2 + core, dev)

    def remote(src, dst, ss, rs, target):
        return pltpu.make_async_remote_copy(
            src_ref=src, dst_ref=dst, send_sem=ss, recv_sem=rs, device_id=target, device_id_type=MESH
        )

    xy_steps = [(kx, ky) for kx in (1, 2, 3, 0) for ky in (1, 2, 3, 0) if kx or ky]
    t_steps = [(ky, kh) for ky in range(4) for kh in range(2) if ky or kh]
    peers = [partner] + [xy_peer(*k) for k in xy_steps] + [z_peer(k) for k in range(1, 8)]
    peers += [t_peer(k, 1) for k in range(1, 4)]
    barrier = pltpu.get_barrier_semaphore()
    for peer in peers:
        pl.semaphore_signal(barrier, inc=1, device_id=peer, device_id_type=MESH)

    def shard_rows(kx, lo):
        start = (lo * 4 + lax.rem(x + kx, 4)) * ROWS
        return pl.ds(pl.multiple_of(start, 8), ROWS)

    def pair_copy(layer, kx, lo):
        slot = kx * 4 + lo
        return remote(grads.at[layer, shard_rows(kx, lo), :], pair_recv.at[slot], pair_ss.at[slot], pair_rs.at[slot], partner)

    def xy_copy(kx, ky):
        slot = kx * 4 + ky
        return remote(xy_send.at[kx, lax.rem(y + ky, 4)], xy_recv.at[slot], xy_ss.at[slot], xy_rs.at[slot], xy_peer(kx, ky))

    def send_pair(layer):
        for kx in (1, 2, 3, 0):
            for lo in range(4):
                pair_copy(layer, kx, lo).start()

    def sum_pair(layer):
        for kx in (1, 2, 3, 0):
            tiles = []
            for lo in range(4):
                pair_copy(layer, kx, lo).wait_recv()
                both = grads[layer, shard_rows(kx, lo), :] + pair_recv[kx * 4 + lo]
                tiles.append(both.reshape(PART, 8, CHANS))
            for ky, tile in enumerate(swap_pairs(tiles)):
                tile = tile.reshape(ROWS, CHANS)
                if kx == 0:
                    xy_own[ky] = tile
                xy_send[kx, ky, 0:ROWS, :] = tile.astype(BF16)
            for ky in (1, 2, 3, 0):
                if kx or ky:
                    xy_copy(kx, ky).start()

    pair_weights(w_ref, forward_w, backward_w)
    for image in range(BATCH):
        shift_store(x_ref, x3, image)
        pre = jnp.dot(four_rows(x3, image), forward_w[...], preferred_element_type=F32)
        sig = 1.0 / (1.0 + jnp.exp(-pre))
        act[image] = (pre * sig).astype(BF16)
        slope[image] = sig * (1.0 + pre * (1.0 - sig))
        shift_store(c_ref, c3, image)
    out = outer_sum(act, c3)
    for ti in range(3):
        for tj in range(3):
            tap = ti * 3 + tj
            parts = [out[o * 128 : (o + 1) * 128, ((o + 2 - ti) * 3 + 2 - tj) * 128 :][:, :128] for o in range(2)]
            grads[1, tap * 128 : (tap + 1) * 128, :] = parts[0] + parts[1]

    pl.semaphore_wait(barrier, len(peers))

    @pl.when(core == 0)
    def _():
        send_pair(1)

    for image in range(BATCH):
        back = jnp.dot(four_rows(c3, image), backward_w[...], preferred_element_type=F32)
        dpre[image] = (back * slope[image]).astype(BF16)

    @pl.when(core == 1)
    def _():
        sum_pair(1)

    out = outer_sum(dpre, x3)
    for ti in range(3):
        for tj in range(3):
            tap = ti * 3 + tj
            parts = [out[o * 128 : (o + 1) * 128, ((ti + o) * 3 + tj) * 128 :][:, :128] for o in range(2)]
            grads[0, tap * 128 : (tap + 1) * 128, :] = (parts[0] + parts[1]).T

    @pl.when(core == 1)
    def _():
        send_pair(0)

    @pl.when(core == 0)
    def _():
        sum_pair(0)

    acc = xy_own[y]
    for kx, ky in xy_steps:
        xy_copy(kx, ky).wait_recv()
        acc = acc + xy_recv[kx * 4 + ky, 0:ROWS, :].astype(F32)
    sums[...] = acc
    for place in range(8):
        z_send[place, 0:PART, :] = sums[pl.ds(place, PART, stride=8), :]

    def z_copy(kz):
        return remote(z_send.at[z_slot(lax.rem(z + kz, 8))], z_recv.at[kz], z_ss.at[kz], z_rs.at[kz], z_peer(kz))

    for kz in (4, 3, 5, 2, 6, 1, 7):
        z_copy(kz).start()
    mine = z_send[z_slot(z), 0:PART, :]
    for kz in (1, 7, 2, 6, 3, 5, 4):
        z_copy(kz).wait_recv()
        mine = mine + z_recv[kz, 0:PART, :]

    own = y * 2 + z_hi
    t_parts[own, 0:PART, :] = mine
    held = pl.ds(own, PART, stride=8)
    state = [ref.at[core][held, :] for ref in (master_ref, first_ref, second_ref)]
    w_parts[z_slot(z), 0:PART, :] = adamw(mine, *state)[0]

    def w_copy(kz, place):
        slot = w_parts.at[z_slot(place)]
        return remote(slot, slot, w_ss.at[kz], w_rs.at[kz], z_peer(kz))

    def t_copy(ky, kh, place):
        slot = t_parts.at[place]
        k = ky * 2 + kh
        return remote(slot, slot, t_ss.at[k], t_rs.at[k], t_peer(ky, kh))

    for kz in (4, 3, 5, 2, 6, 1, 7):
        w_copy(kz, z).start()
    for ky, kh in t_steps:
        t_copy(ky, kh, own).start()
    for kz in range(1, 8):
        w_copy(kz, lax.rem(z + 8 - kz, 8)).wait_recv()
    for place in range(8):
        whole_w[pl.ds(place, PART, stride=8), :] = w_parts[place, 0:PART, :]
    gathered[core, x * 4 + y, 0:ROWS, :] = whole_w[...].astype(BF16)

    def gat_copy(kx, ky, slot):
        return remote(slot, slot, gat_ss.at[kx * 4 + ky], gat_rs.at[kx * 4 + ky], xy_peer(kx, ky))

    def source(layer, kx, ky):
        return gathered.at[layer, lax.rem(x + 4 - kx, 4) * 4 + lax.rem(y + 4 - ky, 4)]

    def fwd_copy(layer, kx, ky):
        slot = source(layer, kx, ky)
        return remote(slot, slot, fwd_ss.at[kx * 4 + ky], fwd_rs.at[kx * 4 + ky], partner)

    for kx, ky in xy_steps:
        gat_copy(kx, ky, source(core, 0, 0)).start()
    fwd_copy(core, 0, 0).start()
    for ky, kh in t_steps:
        place = lax.rem(y + 4 - ky, 4) * 2 + lax.rem(z_hi + kh, 2)
        t_copy(ky, kh, place).wait_recv()
    for place in range(8):
        new_part[pl.ds(place, PART, stride=8), :] = t_parts[place, 0:PART, :]
    totals[core] = new_part[...]
    tot = remote(totals.at[core], totals.at[core], tot_ss, tot_rs, partner)
    tot.start()
    for kx, ky in xy_steps:
        gat_copy(kx, ky, source(core, kx, ky)).wait_recv()
        fwd_copy(core, kx, ky).start()
    remote(totals.at[1 - core], totals.at[1 - core], tot_ss, tot_rs, partner).wait_recv()
    totals_out[...] = totals[...]
    for kx, ky in xy_steps + [(0, 0)]:
        fwd_copy(1 - core, kx, ky).wait_recv()
    gathered_out[...] = gathered[...]
    for kx in range(4):
        for k in range(4):
            pair_copy(1 - core, kx, k).wait_send()
            fwd_copy(core, kx, k).wait_send()
    for kx, ky in xy_steps:
        xy_copy(kx, ky).wait_send()
        gat_copy(kx, ky, source(core, 0, 0)).wait_send()
    for kz in range(1, 8):
        z_copy(kz).wait_send()
        w_copy(kz, z).wait_send()
    for ky, kh in t_steps:
        t_copy(ky, kh, own).wait_send()
    tot.wait_send()


def finish_kernel(gathered_ref, totals_ref, master_ref, first_ref, second_ref,
                  weights_out, master_out, first_out, second_out):
    for layer in range(2):
        new = adamw(totals_ref[layer], master_ref[layer], first_ref[layer], second_ref[layer])
        for ref, value in zip((master_out, first_out, second_out), new):
            ref[layer] = value
        shards_of = {}
        for x in range(4):
            tiles = [gathered_ref[layer, x * 4 + y, 0:ROWS, :].astype(F32).reshape(PART, 8, CHANS) for y in range(4)]
            for lo, tile in enumerate(swap_pairs(tiles)):
                shards_of[lo * 4 + x] = tile.reshape(ROWS, CHANS)
        for two in range(8):
            both = jnp.concatenate([shards_of[2 * two], shards_of[2 * two + 1]], axis=0)
            weights_out[layer, 2 * ROWS * two : 2 * ROWS * (two + 1), :] = both.astype(BF16)


def shards(inputs, cotangent, weights, master, first_moment, second_moment):
    whole = pl.BlockSpec(memory_space=pltpu.VMEM)
    dma = pltpu.SemaphoreType.DMA
    vmem = pltpu.VMEM
    by_pairs = (BATCH, 16, 2, 32, CHANS)
    gathered, totals = pl.pallas_call(
        step_kernel,
        out_shape=(
            jax.ShapeDtypeStruct((2, 16, SLAB, CHANS), BF16),
            jax.ShapeDtypeStruct((2, ROWS, CHANS), F32),
        ),
        in_specs=[whole] * 6,
        out_specs=(whole, whole),
        scratch_shapes=[
            vmem((BATCH, 2, 17, 32, 3 * CHANS), BF16),
            vmem((BATCH, 2, 17, 32, 3 * CHANS), BF16),
            vmem((12 * CHANS, 2 * CHANS), BF16),
            vmem((12 * CHANS, 2 * CHANS), BF16),
            vmem((BATCH, 512, 2 * CHANS), BF16),
            vmem((BATCH, 512, 2 * CHANS), F32),
            vmem((BATCH, 512, 2 * CHANS), BF16),
            vmem((2, 9 * CHANS, CHANS), F32),
            vmem((16, ROWS, CHANS), F32),
            vmem((4, 4, SLAB, CHANS), BF16),
            vmem((16, SLAB, CHANS), BF16),
            vmem((4, ROWS, CHANS), F32),
            vmem((ROWS, CHANS), F32),
            vmem((8, PAD, CHANS), F32),
            vmem((8, PAD, CHANS), F32),
            vmem((PAD, CHANS), F32),
            vmem((ROWS, CHANS), F32),
            vmem((8, PAD, CHANS), F32),
            vmem((8, PAD, CHANS), F32),
            vmem((ROWS, CHANS), F32),
            vmem((2, ROWS, CHANS), F32),
            vmem((2, 16, SLAB, CHANS), BF16),
            dma((16,)), dma((16,)), dma((16,)), dma((16,)), dma((8,)), dma((8,)), dma((8,)), dma((8,)),
            dma((8,)), dma((8,)), dma, dma, dma((16,)), dma((16,)), dma((16,)), dma((16,)),
        ],
        compiler_params=pltpu.CompilerParams(collective_id=0, has_side_effects=True, vmem_limit_bytes=56 * 2**20),
        name="step",
    )(inputs.reshape(by_pairs), cotangent.reshape(by_pairs), weights, master, first_moment, second_moment)
    state = jax.ShapeDtypeStruct(master.shape, F32)
    return pl.pallas_call(
        finish_kernel,
        out_shape=(jax.ShapeDtypeStruct(weights.shape, BF16), state, state, state),
        in_specs=[whole] * 5,
        out_specs=(whole,) * 4,
        compiler_params=pltpu.CompilerParams(vmem_limit_bytes=16 * 2**20),
        name="finish",
    )(gathered, totals, master, first_moment, second_moment)


def solution(mesh):
    placed = (
        P(("grp", "dev"), None, None, None),
        P(("grp", "dev"), None, None, None),
        P(),
        P(None, "dev", None),
        P(None, "dev", None),
        P(None, "dev", None),
    )
    return jax.shard_map(
        shards,
        mesh=mesh,
        in_specs=placed,
        out_specs=(P(), P(None, "dev", None), P(None, "dev", None), P(None, "dev", None)),
        check_vma=False,
    )
```

```python
import jax
import jax.numpy as jnp
from jax import lax
from jax.experimental import pallas as pl
from jax.experimental.pallas import tpu as pltpu
from jax.sharding import PartitionSpec as P

STEP = 10
MESH = pl.DeviceIdType.MESH
BF16, F32 = jnp.bfloat16, jnp.float32
BATCH, CHANS = 4, 128
ROWS = 72
SLAB = 80
PART = 9
PAD = 16


def adamw(grad, master_part, first_part, second_part):
    first_new = 0.9 * first_part + 0.1 * grad
    second_new = 0.95 * second_part + 0.05 * grad * grad
    corr_one = 1.0 - 0.9**STEP
    corr_two = 1.0 - 0.95**STEP
    update = first_new / corr_one / (jnp.sqrt(second_new / corr_two) + 1e-08)
    master_new = master_part - 0.001 * (update + 0.1 * master_part)
    return (master_new, first_new, second_new)


def swap_pairs(tiles):
    row = lax.broadcasted_iota(jnp.int32, tiles[0].shape, 1)
    low = row < 4
    half = [
        jnp.where(low, tiles[0], pltpu.roll(tiles[2], 4, 1)),
        jnp.where(low, tiles[1], pltpu.roll(tiles[3], 4, 1)),
        jnp.where(low, pltpu.roll(tiles[0], 4, 1), tiles[2]),
        jnp.where(low, pltpu.roll(tiles[1], 4, 1), tiles[3]),
    ]
    even = lax.rem(row, 4) < 2
    return [
        jnp.where(even, half[0], pltpu.roll(half[1], 2, 1)),
        jnp.where(even, pltpu.roll(half[0], 6, 1), half[1]),
        jnp.where(even, half[2], pltpu.roll(half[3], 2, 1)),
        jnp.where(even, pltpu.roll(half[2], 6, 1), half[3]),
    ]


def shift_store(src_ref, dst_ref, image):
    col = lax.broadcasted_iota(jnp.int32, (16, 32, CHANS), 1)
    for odd in range(2):
        rows = src_ref[image, :, odd]
        wide = rows.astype(F32)
        left = jnp.where(col == 0, 0.0, pltpu.roll(wide, 1, 1)).astype(BF16)
        right = jnp.where(col == 31, 0.0, pltpu.roll(wide, 31, 1)).astype(BF16)
        place = pl.ds(odd, 16)
        dst_ref[image, 1 - odd, place, :, 0:128] = left
        dst_ref[image, 1 - odd, place, :, 128:256] = rows
        dst_ref[image, 1 - odd, place, :, 256:384] = right
    zero = jnp.zeros((32, 3 * CHANS), BF16)
    dst_ref[image, 0, 0] = zero
    dst_ref[image, 1, 16] = zero


def four_rows(ref, image):
    return jnp.concatenate(
        [ref[image, k % 2, pl.ds(k // 2, 16)].reshape(512, 3 * CHANS) for k in range(4)], axis=1
    )


def pair_weights(w_ref, forward_ref, backward_ref):
    zero = jnp.zeros((CHANS, CHANS), BF16)
    for k in range(4):
        for tj in range(3):
            rows = pl.ds((k * 3 + tj) * CHANS, CHANS)
            for odd in range(2):
                cols = pl.ds(odd * CHANS, CHANS)
                if 0 <= k - odd <= 2:
                    tap = (k - odd) * 3 + tj
                    forward_ref[rows, cols] = w_ref[0, tap * CHANS : (tap + 1) * CHANS, :]
                    tap = (odd - k + 2) * 3 + 2 - tj
                    block = w_ref[1, tap * CHANS : (tap + 1) * CHANS, :]
                    backward_ref[rows, cols] = block.astype(F32).T.astype(BF16)
                else:
                    forward_ref[rows, cols] = zero
                    backward_ref[rows, cols] = zero


def outer_sum(lhs_ref, ref):
    rhs = jnp.concatenate([four_rows(ref, image) for image in range(BATCH)], axis=0)
    lhs = lhs_ref[...].reshape(BATCH * 512, 2 * CHANS)
    return lax.dot_general(lhs, rhs, (((0,), (0,)), ((), ())), preferred_element_type=F32)


def step_kernel(x_hbm, c_hbm, w_hbm, master_hbm, first_hbm, second_hbm,
                gathered_out, totals_out,
                x_ref, c_ref, w_ref, state_ref,
                x3, c3, forward_w, backward_w, act, slope, dpre, grads,
                pair_recv, xy_send, xy_recv, xy_own, z_parts, sums, held, held_whole,
                t_parts, new_part, totals, gathered,
                load_s, pair_ss, pair_rs, xy_ss, xy_rs, z_ss, z_rs, held_ss, held_rs, t_ss, t_rs, tot_ss, tot_rs,
                gat_ss, gat_rs, fwd_ss, fwd_rs):
    grp = lax.axis_index("grp")
    dev = lax.axis_index("dev")
    core = lax.rem(grp, 2)
    y = lax.rem(grp, 8) // 2
    z_hi = grp // 8
    x = lax.rem(dev, 4)
    z_lo = dev // 4
    z = z_hi * 4 + z_lo
    partner = (grp + 1 - 2 * core, dev)

    def xy_peer(kx, ky):
        return (z_hi * 8 + lax.rem(y + ky, 4) * 2 + core, z_lo * 4 + lax.rem(x + kx, 4))

    def z_peer(kz):
        other = lax.rem(z + kz, 8)
        return (other // 4 * 8 + y * 2 + core, lax.rem(other, 4) * 4 + x)

    def held_peer(k):
        return (grp, lax.rem(z_lo + k, 4) * 4 + x)

    def remote(src, dst, ss, rs, target):
        return pltpu.make_async_remote_copy(
            src_ref=src, dst_ref=dst, send_sem=ss, recv_sem=rs, device_id=target, device_id_type=MESH
        )

    loads = [
        pltpu.make_async_copy(src, dst, load_s.at[k])
        for k, (src, dst) in enumerate(
            [(x_hbm, x_ref), (w_hbm, w_ref), (c_hbm, c_ref), (master_hbm, state_ref.at[0]),
             (first_hbm, state_ref.at[1]), (second_hbm, state_ref.at[2])]
        )
    ]
    for copy in loads:
        copy.start()
    xy_order = [(kx, ky) for kx in (2, 1, 3, 0) for ky in (2, 1, 3, 0) if kx or ky]
    xy_steps = [(kx, ky) for kx in (0, 1, 3, 2) for ky in (0, 1, 3, 2) if kx or ky]
    z_order = (4, 3, 5, 2, 6, 1, 7)
    peers = [partner] + [xy_peer(*k) for k in xy_steps] + [z_peer(k) for k in z_order]
    barrier = pltpu.get_barrier_semaphore()
    for peer in peers:
        pl.semaphore_signal(barrier, inc=1, device_id=peer, device_id_type=MESH)

    def shard_rows(kx, lo):
        start = (lo * 4 + lax.rem(x + kx, 4)) * ROWS
        return pl.ds(pl.multiple_of(start, 8), ROWS)

    def pair_copy(layer, kx, lo):
        slot = kx * 4 + lo
        return remote(grads.at[layer, shard_rows(kx, lo), :], pair_recv.at[slot], pair_ss.at[slot], pair_rs.at[slot], partner)

    def xy_copy(kx, ky):
        slot = kx * 4 + ky
        return remote(xy_send.at[kx, lax.rem(y + ky, 4)], xy_recv.at[slot], xy_ss.at[slot], xy_rs.at[slot], xy_peer(kx, ky))

    def send_pair(layer):
        for kx in (2, 1, 3, 0):
            for lo in range(4):
                pair_copy(layer, kx, lo).start()

    def sum_pair(layer):
        for kx in (2, 1, 3, 0):
            tiles = []
            for lo in range(4):
                pair_copy(layer, kx, lo).wait_recv()
                both = grads[layer, shard_rows(kx, lo), :] + pair_recv[kx * 4 + lo]
                tiles.append(both.reshape(PART, 8, CHANS))
            for ky, tile in enumerate(swap_pairs(tiles)):
                tile = tile.reshape(ROWS, CHANS)
                if kx == 0:
                    xy_own[ky] = tile
                xy_send[kx, ky, 0:ROWS, :] = tile.astype(BF16)
            for ky in (2, 1, 3, 0):
                if kx or ky:
                    xy_copy(kx, ky).start()

    for copy in loads:
        copy.wait()
    pair_weights(w_ref, forward_w, backward_w)
    for image in range(BATCH):
        shift_store(x_ref, x3, image)
        pre = jnp.dot(four_rows(x3, image), forward_w[...], preferred_element_type=F32)
        sig = 1.0 / (1.0 + jnp.exp(-pre))
        act[image] = (pre * sig).astype(BF16)
        slope[image] = sig * (1.0 + pre * (1.0 - sig))
        shift_store(c_ref, c3, image)
    out = outer_sum(act, c3)
    for ti in range(3):
        for tj in range(3):
            tap = ti * 3 + tj
            parts = [out[o * 128 : (o + 1) * 128, ((o + 2 - ti) * 3 + 2 - tj) * 128 :][:, :128] for o in range(2)]
            grads[1, tap * 128 : (tap + 1) * 128, :] = parts[0] + parts[1]

    pl.semaphore_wait(barrier, len(peers))

    for k in range(3):
        for h in range(2):
            held[z_lo, k, h, 0:PART, :] = state_ref.at[k, core][pl.ds(y * 2 + h, PART, stride=8), :]

    def held_copy(k, place):
        return remote(held.at[place], held.at[place], held_ss.at[k], held_rs.at[k], held_peer(k))

    for k in range(1, 4):
        held_copy(k, z_lo).start()

    @pl.when(core == 0)
    def _():
        send_pair(1)

    for image in range(BATCH):
        back = jnp.dot(four_rows(c3, image), backward_w[...], preferred_element_type=F32)
        dpre[image] = (back * slope[image]).astype(BF16)

    @pl.when(core == 1)
    def _():
        sum_pair(1)

    out = outer_sum(dpre, x3)
    for ti in range(3):
        for tj in range(3):
            tap = ti * 3 + tj
            parts = [out[o * 128 : (o + 1) * 128, ((ti + o) * 3 + tj) * 128 :][:, :128] for o in range(2)]
            grads[0, tap * 128 : (tap + 1) * 128, :] = (parts[0] + parts[1]).T

    @pl.when(core == 1)
    def _():
        send_pair(0)

    @pl.when(core == 0)
    def _():
        sum_pair(0)

    for k in range(1, 4):
        held_copy(k, lax.rem(z_lo + 4 - k, 4)).wait_recv()
    for k in range(3):
        for lo in range(4):
            for h in range(2):
                held_whole[k, pl.ds(lo * 2 + h, PART, stride=8), :] = held[lo, k, h, 0:PART, :]
    acc = xy_own[y]
    for kx, ky in xy_steps:
        xy_copy(kx, ky).wait_recv()
        acc = acc + xy_recv[kx * 4 + ky, 0:ROWS, :].astype(F32)
    z_parts[z] = acc

    def z_copy(kz, place):
        return remote(z_parts.at[place], z_parts.at[place], z_ss.at[kz], z_rs.at[kz], z_peer(kz))

    for kz in z_order:
        z_copy(kz, z).start()
    for kz in z_order[::-1]:
        z_copy(kz, lax.rem(z + 8 - kz, 8)).wait_recv()
    halves = [(z_parts[k] + z_parts[k + 1]) + (z_parts[k + 2] + z_parts[k + 3]) for k in (0, 4)]
    whole = halves[0] + halves[1]
    sums[...] = whole
    gathered[core, x * 4 + y, 0:ROWS, :] = adamw(whole, held_whole[0], held_whole[1], held_whole[2])[0].astype(BF16)

    def gat_copy(kx, ky, slot):
        return remote(slot, slot, gat_ss.at[kx * 4 + ky], gat_rs.at[kx * 4 + ky], xy_peer(kx, ky))

    def source(layer, kx, ky):
        return gathered.at[layer, lax.rem(x + 4 - kx, 4) * 4 + lax.rem(y + 4 - ky, 4)]

    def fwd_copy(layer, kx, ky):
        slot = source(layer, kx, ky)
        return remote(slot, slot, fwd_ss.at[kx * 4 + ky], fwd_rs.at[kx * 4 + ky], partner)

    for kx, ky in xy_order:
        gat_copy(kx, ky, source(core, 0, 0)).start()
    fwd_copy(core, 0, 0).start()

    def t_copy(ky, place):
        return remote(t_parts.at[place], t_parts.at[place], t_ss.at[ky], t_rs.at[ky], xy_peer(0, ky))

    for h in range(2):
        t_parts[y, h, 0:PART, :] = sums[pl.ds(z_lo * 2 + h, PART, stride=8), :]
    for ky in (2, 1, 3):
        t_copy(ky, y).start()
    for ky in (1, 3, 2):
        t_copy(ky, lax.rem(y + 4 - ky, 4)).wait_recv()
    for place in range(4):
        for h in range(2):
            new_part[pl.ds(place * 2 + h, PART, stride=8), :] = t_parts[place, h, 0:PART, :]
    totals[core] = new_part[...]
    tot = remote(totals.at[core], totals.at[core], tot_ss, tot_rs, partner)
    tot.start()
    for kx, ky in xy_steps:
        gat_copy(kx, ky, source(core, kx, ky)).wait_recv()
        fwd_copy(core, kx, ky).start()
    remote(totals.at[1 - core], totals.at[1 - core], tot_ss, tot_rs, partner).wait_recv()
    totals_out[...] = totals[...]
    for kx, ky in xy_steps + [(0, 0)]:
        fwd_copy(1 - core, kx, ky).wait_recv()
    gathered_out[...] = gathered[...]
    for kx in range(4):
        for k in range(4):
            pair_copy(1 - core, kx, k).wait_send()
            fwd_copy(core, kx, k).wait_send()
    for kx, ky in xy_steps:
        xy_copy(kx, ky).wait_send()
        gat_copy(kx, ky, source(core, 0, 0)).wait_send()
    for kz in z_order:
        z_copy(kz, z).wait_send()
    for k in range(1, 4):
        held_copy(k, z_lo).wait_send()
        t_copy(k, y).wait_send()
    tot.wait_send()


def finish_kernel(gathered_ref, totals_ref, master_ref, first_ref, second_ref,
                  weights_out, master_out, first_out, second_out):
    for layer in range(2):
        new = adamw(totals_ref[layer], master_ref[layer], first_ref[layer], second_ref[layer])
        for ref, value in zip((master_out, first_out, second_out), new):
            ref[layer] = value
        shards_of = {}
        for x in range(4):
            tiles = [gathered_ref[layer, x * 4 + y, 0:ROWS, :].astype(F32).reshape(PART, 8, CHANS) for y in range(4)]
            for lo, tile in enumerate(swap_pairs(tiles)):
                shards_of[lo * 4 + x] = tile.reshape(ROWS, CHANS)
        for two in range(8):
            both = jnp.concatenate([shards_of[2 * two], shards_of[2 * two + 1]], axis=0)
            weights_out[layer, 2 * ROWS * two : 2 * ROWS * (two + 1), :] = both.astype(BF16)


def shards(inputs, cotangent, weights, master, first_moment, second_moment):
    whole = pl.BlockSpec(memory_space=pltpu.VMEM)
    dma = pltpu.SemaphoreType.DMA
    vmem = pltpu.VMEM
    by_pairs = (BATCH, 16, 2, 32, CHANS)
    gathered, totals = pl.pallas_call(
        step_kernel,
        out_shape=(
            jax.ShapeDtypeStruct((2, 16, SLAB, CHANS), BF16),
            jax.ShapeDtypeStruct((2, ROWS, CHANS), F32),
        ),
        in_specs=[pl.BlockSpec(memory_space=pltpu.HBM)] * 6,
        out_specs=(whole, whole),
        scratch_shapes=[
            vmem(by_pairs, BF16),
            vmem(by_pairs, BF16),
            vmem(weights.shape, BF16),
            vmem((3,) + master.shape, F32),
            vmem((BATCH, 2, 17, 32, 3 * CHANS), BF16),
            vmem((BATCH, 2, 17, 32, 3 * CHANS), BF16),
            vmem((12 * CHANS, 2 * CHANS), BF16),
            vmem((12 * CHANS, 2 * CHANS), BF16),
            vmem((BATCH, 512, 2 * CHANS), BF16),
            vmem((BATCH, 512, 2 * CHANS), F32),
            vmem((BATCH, 512, 2 * CHANS), BF16),
            vmem((2, 9 * CHANS, CHANS), F32),
            vmem((16, ROWS, CHANS), F32),
            vmem((4, 4, SLAB, CHANS), BF16),
            vmem((16, SLAB, CHANS), BF16),
            vmem((4, ROWS, CHANS), F32),
            vmem((8, ROWS, CHANS), F32),
            vmem((ROWS, CHANS), F32),
            vmem((4, 3, 2, PAD, CHANS), F32),
            vmem((3, ROWS, CHANS), F32),
            vmem((4, 2, PAD, CHANS), F32),
            vmem((ROWS, CHANS), F32),
            vmem((2, ROWS, CHANS), F32),
            vmem((2, 16, SLAB, CHANS), BF16),
            dma((6,)),
            dma((16,)), dma((16,)), dma((16,)), dma((16,)), dma((8,)), dma((8,)), dma((4,)), dma((4,)),
            dma((4,)), dma((4,)), dma, dma, dma((16,)), dma((16,)), dma((16,)), dma((16,)),
        ],
        compiler_params=pltpu.CompilerParams(collective_id=0, has_side_effects=True, vmem_limit_bytes=60 * 2**20),
        name="step",
    )(inputs.reshape(by_pairs), cotangent.reshape(by_pairs), weights, master, first_moment, second_moment)
    state = jax.ShapeDtypeStruct(master.shape, F32)
    return pl.pallas_call(
        finish_kernel,
        out_shape=(jax.ShapeDtypeStruct(weights.shape, BF16), state, state, state),
        in_specs=[whole] * 5,
        out_specs=(whole,) * 4,
        compiler_params=pltpu.CompilerParams(vmem_limit_bytes=60 * 2**20),
        name="finish",
    )(gathered, totals, master, first_moment, second_moment)


def solution(mesh):
    placed = (
        P(("grp", "dev"), None, None, None),
        P(("grp", "dev"), None, None, None),
        P(),
        P(None, "dev", None),
        P(None, "dev", None),
        P(None, "dev", None),
    )
    return jax.shard_map(
        shards,
        mesh=mesh,
        in_specs=placed,
        out_specs=(P(), P(None, "dev", None), P(None, "dev", None), P(None, "dev", None)),
        check_vma=False,
    )
```

```python
import jax
import jax.numpy as jnp
from jax import lax
from jax.experimental import pallas as pl
from jax.experimental.pallas import tpu as pltpu
from jax.sharding import PartitionSpec as P

STEP = 10
MESH = pl.DeviceIdType.MESH
BF16, F32 = jnp.bfloat16, jnp.float32
BATCH, CHANS = 4, 128
ROWS = 72
SLAB = 80


def adamw(grad, master_part, first_part, second_part):
    first_new = 0.9 * first_part + 0.1 * grad
    second_new = 0.95 * second_part + 0.05 * grad * grad
    corr_one = 1.0 - 0.9**STEP
    corr_two = 1.0 - 0.95**STEP
    update = first_new / corr_one / (jnp.sqrt(second_new / corr_two) + 1e-08)
    master_new = master_part - 0.001 * (update + 0.1 * master_part)
    return (master_new, first_new, second_new)


def shift_store(src_ref, dst_ref, image):
    edge = jnp.zeros((16, 1, CHANS), BF16)
    for odd in range(2):
        rows = src_ref[image, :, odd]
        place = pl.ds(odd, 16)
        dst_ref[image, 1 - odd, place, :, 0:128] = jnp.concatenate([edge, rows[:, :31]], axis=1)
        dst_ref[image, 1 - odd, place, :, 128:256] = rows
        dst_ref[image, 1 - odd, place, :, 256:384] = jnp.concatenate([rows[:, 1:], edge], axis=1)
    zero = jnp.zeros((32, 3 * CHANS), BF16)
    dst_ref[image, 0, 0] = zero
    dst_ref[image, 1, 16] = zero


def four_rows(ref, image):
    return jnp.concatenate(
        [ref[image, k % 2, pl.ds(k // 2, 16)].reshape(512, 3 * CHANS) for k in range(4)], axis=1
    )


def pair_forward(w_ref, out_ref):
    zero = jnp.zeros((CHANS, CHANS), BF16)
    for k in range(4):
        for tj in range(3):
            rows = pl.ds((k * 3 + tj) * CHANS, CHANS)
            for odd in range(2):
                tap = (k - odd) * 3 + tj
                block = w_ref[0, tap * CHANS : (tap + 1) * CHANS, :] if 0 <= k - odd <= 2 else zero
                out_ref[rows, odd * CHANS : (odd + 1) * CHANS] = block


def pair_backward(w_ref, out_ref):
    zero = jnp.zeros((CHANS, CHANS), BF16)
    for k in range(4):
        for tj in range(3):
            rows = pl.ds((k * 3 + tj) * CHANS, CHANS)
            for odd in range(2):
                tap = (odd - k + 2) * 3 + 2 - tj
                block = w_ref[1, tap * CHANS : (tap + 1) * CHANS, :].T if 0 <= k - odd <= 2 else zero
                out_ref[rows, odd * CHANS : (odd + 1) * CHANS] = block


def put_turned(ref, value, image):
    turned = value.astype(BF16).T
    for odd in range(2):
        start = odd * BATCH * 512 + image * 512
        ref[:, start : start + 512] = turned[odd * CHANS : (odd + 1) * CHANS]


def outer_sum(turned, ref):
    out = None
    for odd in range(2):
        for image in range(BATCH):
            near = jnp.concatenate(
                [ref[image, (k + odd) % 2, pl.ds((k + odd) // 2, 16)].reshape(512, 3 * CHANS) for k in range(3)], axis=1
            )
            start = odd * BATCH * 512 + image * 512
            part = jnp.dot(turned[:, start : start + 512], near, preferred_element_type=F32)
            out = part if out is None else out + part
    return out


def step_kernel(x_hbm, c_hbm, w_hbm, master_hbm, first_hbm, second_hbm,
                weights_out, totals_out,
                x_ref, c_ref, w_ref, state_ref,
                x3, c3, forward_w, backward_w, act, slope, dpre, grads,
                pair_recv, xy_send, xy_recv, xy_own, z_parts, held, totals, gathered,
                load_s, pair_ss, pair_rs, xy_ss, xy_rs, z_ss, z_rs, held_ss, held_rs, t_ss, t_rs, tot_ss, tot_rs,
                gat_ss, gat_rs, fwd_ss, fwd_rs):
    grp = lax.axis_index("grp")
    dev = lax.axis_index("dev")
    core = lax.rem(grp, 2)
    y = lax.rem(grp, 8) // 2
    z_hi = grp // 8
    x = lax.rem(dev, 4)
    z_lo = dev // 4
    z = z_hi * 4 + z_lo
    partner = (grp + 1 - 2 * core, dev)

    def xy_peer(kx, ky):
        return (z_hi * 8 + lax.rem(y + ky, 4) * 2 + core, z_lo * 4 + lax.rem(x + kx, 4))

    def z_peer(kz):
        other = lax.rem(z + kz, 8)
        return (other // 4 * 8 + y * 2 + core, lax.rem(other, 4) * 4 + x)

    def held_peer(k):
        return (grp, lax.rem(z_lo + k, 4) * 4 + x)

    def remote(src, dst, ss, rs, target):
        return pltpu.make_async_remote_copy(
            src_ref=src, dst_ref=dst, send_sem=ss, recv_sem=rs, device_id=target, device_id_type=MESH
        )

    loads = [
        pltpu.make_async_copy(src, dst, load_s.at[k])
        for k, (src, dst) in enumerate(
            [(x_hbm, x_ref), (w_hbm, w_ref), (c_hbm, c_ref)]
            + [(ref.at[layer], state_ref.at[layer, k])
               for k, ref in enumerate((master_hbm, first_hbm, second_hbm)) for layer in range(2)]
        )
    ]
    for copy in loads:
        copy.start()
    xy_order = [(kx, ky) for kx in (2, 1, 3, 0) for ky in (2, 1, 3, 0) if kx or ky]
    xy_steps = [(kx, ky) for kx in (0, 1, 3, 2) for ky in (0, 1, 3, 2) if kx or ky]
    z_order = (4, 3, 5, 2, 6, 1, 7)
    peers = [partner] + [xy_peer(*k) for k in xy_steps] + [z_peer(k) for k in z_order]
    barrier = pltpu.get_barrier_semaphore()
    for peer in peers:
        pl.semaphore_signal(barrier, inc=1, device_id=peer, device_id_type=MESH)

    def shard_rows(kx, ky):
        start = (lax.rem(y + ky, 4) * 4 + lax.rem(x + kx, 4)) * ROWS
        return pl.ds(pl.multiple_of(start, 8), ROWS)

    def pair_copy(layer, kx, ky):
        slot = kx * 4 + ky
        return remote(grads.at[layer, shard_rows(kx, ky), :], pair_recv.at[slot], pair_ss.at[slot], pair_rs.at[slot], partner)

    def xy_copy(kx, ky):
        slot = kx * 4 + ky
        return remote(xy_send.at[slot], xy_recv.at[slot], xy_ss.at[slot], xy_rs.at[slot], xy_peer(kx, ky))

    def send_pair(layer):
        for kx, ky in xy_order + [(0, 0)]:
            pair_copy(layer, kx, ky).start()

    def sum_pair(layer):
        for kx, ky in xy_order + [(0, 0)]:
            slot = kx * 4 + ky
            pair_copy(layer, kx, ky).wait_recv()
            both = grads[layer, shard_rows(kx, ky), :] + pair_recv[slot]
            if slot:
                xy_send[slot, 0:ROWS, :] = both.astype(BF16)
                xy_copy(kx, ky).start()
            else:
                xy_own[...] = both

    for copy in loads:
        copy.wait()
    pair_forward(w_ref, forward_w)
    shift_store(x_ref, x3, 0)
    for image in range(BATCH):
        pre = jnp.dot(four_rows(x3, image), forward_w[...], preferred_element_type=F32)
        sig = 1.0 / (1.0 + jnp.exp(-pre))
        value = pre * sig
        put_turned(act, value, image)
        slope[image] = sig + value * (1.0 - sig)
        if image < BATCH - 1:
            shift_store(x_ref, x3, image + 1)
        shift_store(c_ref, c3, image)
    pair_backward(w_ref, backward_w)
    out = outer_sum(act, c3)
    for block in range(9):
        tap = 8 - block
        grads[1, tap * CHANS : (tap + 1) * CHANS, :] = out[:, block * CHANS : (block + 1) * CHANS]

    pl.semaphore_wait(barrier, len(peers))

    def held_copy(k, source_ref):
        return remote(source_ref, held, held_ss.at[k], held_rs, held_peer(k))

    @pl.when(z_lo == y)
    def _():
        held[...] = state_ref[core]
        for k in range(1, 4):
            held_copy(k, held).start()

    @pl.when(core == 0)
    def _():
        send_pair(1)

    for image in range(BATCH):
        back = jnp.dot(four_rows(c3, image), backward_w[...], preferred_element_type=F32)
        put_turned(dpre, back * slope[image], image)

    @pl.when(core == 1)
    def _():
        sum_pair(1)

    out = outer_sum(dpre, x3)
    for tap in range(9):
        grads[0, tap * CHANS : (tap + 1) * CHANS, :] = out[:, tap * CHANS : (tap + 1) * CHANS].T

    @pl.when(core == 1)
    def _():
        send_pair(0)

    @pl.when(core == 0)
    def _():
        sum_pair(0)

    @pl.when(z_lo != y)
    def _():
        held_copy(1, held).wait_recv()

    acc = xy_own[...]
    for kx, ky in xy_steps:
        xy_copy(kx, ky).wait_recv()
        acc = acc + xy_recv[kx * 4 + ky, 0:ROWS, :].astype(F32)
    z_parts[z] = acc

    def z_copy(kz, place):
        return remote(z_parts.at[place], z_parts.at[place], z_ss.at[kz], z_rs.at[kz], z_peer(kz))

    for kz in z_order:
        z_copy(kz, z).start()
    for kz in z_order[::-1]:
        z_copy(kz, lax.rem(z + 8 - kz, 8)).wait_recv()
    halves = [(z_parts[k] + z_parts[k + 1]) + (z_parts[k + 2] + z_parts[k + 3]) for k in (0, 4)]
    whole = halves[0] + halves[1]
    slab = adamw(whole, held[0], held[1], held[2])[0].astype(BF16)
    gathered[core, y * 4 + x, 0:ROWS, :] = slab

    def gat_copy(kx, ky, slot):
        return remote(slot, slot, gat_ss.at[kx * 4 + ky], gat_rs.at[kx * 4 + ky], xy_peer(kx, ky))

    def source(layer, kx, ky):
        return gathered.at[layer, lax.rem(y + 4 - ky, 4) * 4 + lax.rem(x + 4 - kx, 4)]

    def fwd_copy(layer, kx, ky):
        slot = source(layer, kx, ky)
        return remote(slot, slot, fwd_ss.at[kx * 4 + ky], fwd_rs.at[kx * 4 + ky], partner)

    for kx, ky in xy_order:
        gat_copy(kx, ky, source(core, 0, 0)).start()
    fwd_copy(core, 0, 0).start()

    def t_copy(ky):
        return remote(totals.at[core], totals.at[core], t_ss.at[ky], t_rs, xy_peer(0, ky))

    @pl.when(z_lo == y)
    def _():
        totals[core] = whole
        for ky in (2, 1, 3):
            t_copy(ky).start()

    @pl.when(z_lo != y)
    def _():
        t_copy(1).wait_recv()

    tot = remote(totals.at[core], totals.at[core], tot_ss, tot_rs, partner)
    tot.start()

    def assemble(layer):
        for two in range(8):
            both = [gathered[layer, 2 * two + k, 0:ROWS, :].astype(F32) for k in range(2)]
            weights_out[layer, 2 * ROWS * two : 2 * ROWS * (two + 1), :] = jnp.concatenate(both, axis=0).astype(BF16)

    for kx, ky in xy_steps:
        gat_copy(kx, ky, source(core, kx, ky)).wait_recv()
        fwd_copy(core, kx, ky).start()
    assemble(core)
    remote(totals.at[1 - core], totals.at[1 - core], tot_ss, tot_rs, partner).wait_recv()
    totals_out[...] = totals[...]
    for kx, ky in xy_steps + [(0, 0)]:
        fwd_copy(1 - core, kx, ky).wait_recv()
    assemble(1 - core)
    for kx in range(4):
        for k in range(4):
            pair_copy(1 - core, kx, k).wait_send()
            fwd_copy(core, kx, k).wait_send()
    for kx, ky in xy_steps:
        xy_copy(kx, ky).wait_send()
        gat_copy(kx, ky, source(core, 0, 0)).wait_send()
    for kz in z_order:
        z_copy(kz, z).wait_send()

    @pl.when(z_lo == y)
    def _():
        for k in range(1, 4):
            held_copy(k, held).wait_send()
            t_copy(k).wait_send()

    tot.wait_send()


def shards(inputs, cotangent, weights, master, first_moment, second_moment):
    whole = pl.BlockSpec(memory_space=pltpu.VMEM)
    dma = pltpu.SemaphoreType.DMA
    vmem = pltpu.VMEM
    by_pairs = (BATCH, 16, 2, 32, CHANS)
    new_weights, totals = pl.pallas_call(
        step_kernel,
        out_shape=(
            jax.ShapeDtypeStruct(weights.shape, BF16),
            jax.ShapeDtypeStruct((2, ROWS, CHANS), F32),
        ),
        in_specs=[pl.BlockSpec(memory_space=pltpu.HBM)] * 6,
        out_specs=(whole, whole),
        scratch_shapes=[
            vmem(by_pairs, BF16),
            vmem(by_pairs, BF16),
            vmem(weights.shape, BF16),
            vmem((2, 3, ROWS, CHANS), F32),
            vmem((BATCH, 2, 17, 32, 3 * CHANS), BF16),
            vmem((BATCH, 2, 17, 32, 3 * CHANS), BF16),
            vmem((12 * CHANS, 2 * CHANS), BF16),
            vmem((12 * CHANS, 2 * CHANS), BF16),
            vmem((CHANS, BATCH * 1024), BF16),
            vmem((BATCH, 512, 2 * CHANS), F32),
            vmem((CHANS, BATCH * 1024), BF16),
            vmem((2, 9 * CHANS, CHANS), F32),
            vmem((16, ROWS, CHANS), F32),
            vmem((16, SLAB, CHANS), BF16),
            vmem((16, SLAB, CHANS), BF16),
            vmem((ROWS, CHANS), F32),
            vmem((8, ROWS, CHANS), F32),
            vmem((3, ROWS, CHANS), F32),
            vmem((2, ROWS, CHANS), F32),
            vmem((2, 16, SLAB, CHANS), BF16),
            dma((9,)),
            dma((16,)), dma((16,)), dma((16,)), dma((16,)), dma((8,)), dma((8,)), dma((4,)), dma,
            dma((4,)), dma, dma, dma, dma((16,)), dma((16,)), dma((16,)), dma((16,)),
        ],
        compiler_params=pltpu.CompilerParams(collective_id=0, has_side_effects=True, vmem_limit_bytes=60 * 2**20),
        name="step",
    )(inputs.reshape(by_pairs), cotangent.reshape(by_pairs), weights, master, first_moment, second_moment)
    return (new_weights,) + adamw(totals, master, first_moment, second_moment)


def solution(mesh):
    placed = (
        P(("grp", "dev"), None, None, None),
        P(("grp", "dev"), None, None, None),
        P(),
        P(None, "dev", None),
        P(None, "dev", None),
        P(None, "dev", None),
    )
    return jax.shard_map(
        shards,
        mesh=mesh,
        in_specs=placed,
        out_specs=(P(), P(None, "dev", None), P(None, "dev", None), P(None, "dev", None)),
        check_vma=False,
    )
```

```python
import jax
import jax.numpy as jnp
from jax import lax
from jax.experimental import pallas as pl
from jax.experimental.pallas import tpu as pltpu
from jax.sharding import PartitionSpec as P

STEP = 10
MESH = pl.DeviceIdType.MESH
BF16, F32 = jnp.bfloat16, jnp.float32
BATCH, CHANS = 4, 128
ROWS = 72
SLAB = 80


def adamw(grad, master_part, first_part, second_part):
    first_new = 0.9 * first_part + 0.1 * grad
    second_new = 0.95 * second_part + 0.05 * grad * grad
    corr_one = 1.0 - 0.9**STEP
    corr_two = 1.0 - 0.95**STEP
    update = first_new / corr_one / (jnp.sqrt(second_new / corr_two) + 1e-08)
    master_new = master_part - 0.001 * (update + 0.1 * master_part)
    return (master_new, first_new, second_new)


def shift_store(src_ref, dst_ref, image):
    edge = jnp.zeros((16, 1, CHANS), BF16)
    for odd in range(2):
        rows = src_ref[image, :, odd]
        place = pl.ds(odd, 16)
        dst_ref[image, 1 - odd, place, :, 0:128] = jnp.concatenate([edge, rows[:, :31]], axis=1)
        dst_ref[image, 1 - odd, place, :, 128:256] = rows
        dst_ref[image, 1 - odd, place, :, 256:384] = jnp.concatenate([rows[:, 1:], edge], axis=1)
    zero = jnp.zeros((32, 3 * CHANS), BF16)
    dst_ref[image, 0, 0] = zero
    dst_ref[image, 1, 16] = zero


def four_rows(ref, image):
    return jnp.concatenate(
        [ref[image, k % 2, pl.ds(k // 2, 16)].reshape(512, 3 * CHANS) for k in range(4)], axis=1
    )


def pair_forward(w_ref, out_ref):
    zero = jnp.zeros((CHANS, CHANS), BF16)
    for k in range(4):
        for tj in range(3):
            rows = pl.ds((k * 3 + tj) * CHANS, CHANS)
            for odd in range(2):
                tap = (k - odd) * 3 + tj
                block = w_ref[0, tap * CHANS : (tap + 1) * CHANS, :] if 0 <= k - odd <= 2 else zero
                out_ref[rows, odd * CHANS : (odd + 1) * CHANS] = block


def pair_backward(w_ref, out_ref):
    zero = jnp.zeros((CHANS, CHANS), BF16)
    for k in range(4):
        for tj in range(3):
            rows = pl.ds((k * 3 + tj) * CHANS, CHANS)
            for odd in range(2):
                tap = (odd - k + 2) * 3 + 2 - tj
                block = w_ref[1, tap * CHANS : (tap + 1) * CHANS, :].T if 0 <= k - odd <= 2 else zero
                out_ref[rows, odd * CHANS : (odd + 1) * CHANS] = block


def put_turned(ref, value, image):
    turned = value.astype(BF16).T
    for odd in range(2):
        start = odd * BATCH * 512 + image * 512
        ref[:, start : start + 512] = turned[odd * CHANS : (odd + 1) * CHANS]


def outer_sum(turned, ref):
    out = None
    for odd in range(2):
        for image in range(BATCH):
            near = jnp.concatenate(
                [ref[image, (k + odd) % 2, pl.ds((k + odd) // 2, 16)].reshape(512, 3 * CHANS) for k in range(3)], axis=1
            )
            start = odd * BATCH * 512 + image * 512
            part = jnp.dot(turned[:, start : start + 512], near, preferred_element_type=F32)
            out = part if out is None else out + part
    return out


def step_kernel(x_hbm, c_hbm, w_hbm, master_hbm, first_hbm, second_hbm,
                gathered_out, totals_out,
                x_ref, c_ref, w_ref, state_ref,
                x3, c3, forward_w, backward_w, act, slope, dpre, grads,
                pair_recv, xy_send, xy_recv, xy_own, z_parts, held, totals, gathered,
                load_s, pair_ss, pair_rs, xy_ss, xy_rs, z_ss, z_rs, held_ss, held_rs, t_ss, t_rs, tot_ss, tot_rs,
                gat_ss, gat_rs, fwd_ss, fwd_rs, put_s):
    grp = lax.axis_index("grp")
    dev = lax.axis_index("dev")
    core = lax.rem(grp, 2)
    y = lax.rem(grp, 8) // 2
    z_hi = grp // 8
    x = lax.rem(dev, 4)
    z_lo = dev // 4
    z = z_hi * 4 + z_lo
    partner = (grp + 1 - 2 * core, dev)

    def xy_peer(kx, ky):
        return (z_hi * 8 + lax.rem(y + ky, 4) * 2 + core, z_lo * 4 + lax.rem(x + kx, 4))

    def z_peer(kz):
        other = lax.rem(z + kz, 8)
        return (other // 4 * 8 + y * 2 + core, lax.rem(other, 4) * 4 + x)

    def held_peer(k):
        return (grp, lax.rem(z_lo + k, 4) * 4 + x)

    def remote(src, dst, ss, rs, target):
        return pltpu.make_async_remote_copy(
            src_ref=src, dst_ref=dst, send_sem=ss, recv_sem=rs, device_id=target, device_id_type=MESH
        )

    loads = [
        pltpu.make_async_copy(src, dst, load_s.at[k])
        for k, (src, dst) in enumerate(
            [(x_hbm, x_ref), (w_hbm, w_ref), (c_hbm, c_ref)]
            + [(ref.at[layer], state_ref.at[layer, k])
               for k, ref in enumerate((master_hbm, first_hbm, second_hbm)) for layer in range(2)]
        )
    ]
    for copy in loads:
        copy.start()
    xy_order = [(kx, ky) for kx in (2, 1, 3, 0) for ky in (2, 1, 3, 0) if kx or ky]
    xy_steps = [(kx, ky) for kx in (0, 1, 3, 2) for ky in (0, 1, 3, 2) if kx or ky]
    z_order = (4, 3, 5, 2, 6, 1, 7)
    peers = [partner] + [xy_peer(*k) for k in xy_steps] + [z_peer(k) for k in z_order]
    barrier = pltpu.get_barrier_semaphore()
    for peer in peers:
        pl.semaphore_signal(barrier, inc=1, device_id=peer, device_id_type=MESH)

    def shard_rows(kx, ky):
        start = (lax.rem(y + ky, 4) * 4 + lax.rem(x + kx, 4)) * ROWS
        return pl.ds(pl.multiple_of(start, 8), ROWS)

    def pair_copy(layer, kx, ky):
        slot = kx * 4 + ky
        return remote(grads.at[layer, shard_rows(kx, ky), :], pair_recv.at[slot], pair_ss.at[slot], pair_rs.at[slot], partner)

    def xy_copy(kx, ky):
        slot = kx * 4 + ky
        return remote(xy_send.at[slot], xy_recv.at[slot], xy_ss.at[slot], xy_rs.at[slot], xy_peer(kx, ky))

    def send_pair(layer):
        for kx, ky in xy_order + [(0, 0)]:
            pair_copy(layer, kx, ky).start()

    def sum_pair(layer):
        for kx, ky in xy_order + [(0, 0)]:
            slot = kx * 4 + ky
            pair_copy(layer, kx, ky).wait_recv()
            both = grads[layer, shard_rows(kx, ky), :] + pair_recv[slot]
            if slot:
                xy_send[slot, 0:ROWS, :] = both.astype(BF16)
                xy_copy(kx, ky).start()
            else:
                xy_own[...] = both

    for copy in loads:
        copy.wait()
    pair_forward(w_ref, forward_w)
    shift_store(x_ref, x3, 0)
    for image in range(BATCH):
        pre = jnp.dot(four_rows(x3, image), forward_w[...], preferred_element_type=F32)
        sig = 1.0 / (1.0 + jnp.exp(-pre))
        value = pre * sig
        put_turned(act, value, image)
        slope[image] = sig + value * (1.0 - sig)
        if image < BATCH - 1:
            shift_store(x_ref, x3, image + 1)
        shift_store(c_ref, c3, image)

    pl.semaphore_wait(barrier, len(peers))

    def held_copy(k, source_ref):
        return remote(source_ref, held, held_ss.at[k], held_rs, held_peer(k))

    @pl.when(z_lo == y)
    def _():
        held[...] = state_ref[core]
        for k in range(1, 4):
            held_copy(k, held).start()

    pair_backward(w_ref, backward_w)
    out = outer_sum(act, c3)
    for block in range(9):
        tap = 8 - block
        grads[1, tap * CHANS : (tap + 1) * CHANS, :] = out[:, block * CHANS : (block + 1) * CHANS]

    @pl.when(core == 0)
    def _():
        send_pair(1)

    for image in range(BATCH):
        back = jnp.dot(four_rows(c3, image), backward_w[...], preferred_element_type=F32)
        put_turned(dpre, back * slope[image], image)

    @pl.when(core == 1)
    def _():
        sum_pair(1)

    out = outer_sum(dpre, x3)
    for tap in range(9):
        grads[0, tap * CHANS : (tap + 1) * CHANS, :] = out[:, tap * CHANS : (tap + 1) * CHANS].T

    @pl.when(core == 1)
    def _():
        send_pair(0)

    @pl.when(core == 0)
    def _():
        sum_pair(0)

    acc = xy_own[...]
    for kx, ky in xy_steps:
        xy_copy(kx, ky).wait_recv()
        acc = acc + xy_recv[kx * 4 + ky, 0:ROWS, :].astype(F32)
    z_parts[z, 0:ROWS, :] = acc.astype(BF16)

    def z_copy(kz, place):
        return remote(z_parts.at[place], z_parts.at[place], z_ss.at[kz], z_rs.at[kz], z_peer(kz))

    for kz in z_order:
        z_copy(kz, z).start()
    for kz in z_order[::-1]:
        z_copy(kz, lax.rem(z + 8 - kz, 8)).wait_recv()
    z_part = [z_parts[k, 0:ROWS, :].astype(F32) for k in range(8)]
    halves = [(z_part[k] + z_part[k + 1]) + (z_part[k + 2] + z_part[k + 3]) for k in (0, 4)]
    whole = halves[0] + halves[1]
    @pl.when(z_lo != y)
    def _():
        held_copy(1, held).wait_recv()

    slab = adamw(whole, held[0], held[1], held[2])[0].astype(BF16)
    gathered[core, y * 4 + x, 0:ROWS, :] = slab

    def gat_copy(kx, ky, slot):
        return remote(slot, slot, gat_ss.at[kx * 4 + ky], gat_rs.at[kx * 4 + ky], xy_peer(kx, ky))

    def source(layer, kx, ky):
        return gathered.at[layer, lax.rem(y + 4 - ky, 4) * 4 + lax.rem(x + 4 - kx, 4)]

    def fwd_copy(layer, kx, ky):
        slot = source(layer, kx, ky)
        return remote(slot, slot, fwd_ss.at[kx * 4 + ky], fwd_rs.at[kx * 4 + ky], partner)

    for kx, ky in xy_order:
        gat_copy(kx, ky, source(core, 0, 0)).start()
    fwd_copy(core, 0, 0).start()

    def t_copy(ky):
        return remote(totals.at[core], totals.at[core], t_ss.at[ky], t_rs, xy_peer(0, ky))

    @pl.when(z_lo == y)
    def _():
        totals[core] = whole
        for ky in (2, 1, 3):
            t_copy(ky).start()

    @pl.when(z_lo != y)
    def _():
        t_copy(1).wait_recv()

    tot = remote(totals.at[core], totals.at[core], tot_ss, tot_rs, partner)
    tot.start()

    def put(layer):
        pairs = ((gathered.at[layer], gathered_out.at[layer]), (totals.at[layer], totals_out.at[layer]))
        return [pltpu.make_async_copy(src, dst, put_s.at[layer, k]) for k, (src, dst) in enumerate(pairs)]

    for kx, ky in xy_steps:
        gat_copy(kx, ky, source(core, kx, ky)).wait_recv()
        fwd_copy(core, kx, ky).start()
    for copy in put(core):
        copy.start()
    remote(totals.at[1 - core], totals.at[1 - core], tot_ss, tot_rs, partner).wait_recv()
    for kx, ky in xy_steps + [(0, 0)]:
        fwd_copy(1 - core, kx, ky).wait_recv()
    for copy in put(1 - core):
        copy.start()
    for kx in range(4):
        for k in range(4):
            pair_copy(1 - core, kx, k).wait_send()
            fwd_copy(core, kx, k).wait_send()
    for kx, ky in xy_steps:
        xy_copy(kx, ky).wait_send()
        gat_copy(kx, ky, source(core, 0, 0)).wait_send()
    for kz in z_order:
        z_copy(kz, z).wait_send()

    @pl.when(z_lo == y)
    def _():
        for k in range(1, 4):
            held_copy(k, held).wait_send()
            t_copy(k).wait_send()

    tot.wait_send()
    for copy in put(0) + put(1):
        copy.wait()


def finish_kernel(gathered_hbm, totals_hbm, master_hbm, first_hbm, second_hbm,
                  weights_hbm, master_out, first_out, second_out,
                  gathered, weights, held, new, load_s, state_s, store_s, new_s):
    loads, stores = [], []
    for k in range(4):
        layer, part = k // 2, pl.ds(k % 2 * 8, 8)
        loads.append(pltpu.make_async_copy(gathered_hbm.at[layer, part], gathered.at[layer, part], load_s.at[k]))
        rows = pl.ds(k % 2 * 8 * ROWS, 8 * ROWS)
        stores.append(pltpu.make_async_copy(weights.at[layer, rows], weights_hbm.at[layer, rows], store_s.at[k]))
    states = [
        pltpu.make_async_copy(src, held.at[k], state_s.at[k])
        for k, src in enumerate((totals_hbm, master_hbm, first_hbm, second_hbm))
    ]
    for copy in states + loads:
        copy.start()
    for copy in states:
        copy.wait()
    for k, value in enumerate(adamw(held[0], held[1], held[2], held[3])):
        new[k] = value
        store = pltpu.make_async_copy(new.at[k], (master_out, first_out, second_out)[k], new_s.at[k])
        store.start()
        stores.append(store)
    for k in range(4):
        loads[k].wait()
        for two in range(k % 2 * 4, k % 2 * 4 + 4):
            both = [gathered[k // 2, 2 * two + odd, 0:ROWS, :].astype(F32) for odd in range(2)]
            weights[k // 2, 2 * ROWS * two : 2 * ROWS * (two + 1), :] = jnp.concatenate(both, axis=0).astype(BF16)
        stores[k].start()
    for copy in stores:
        copy.wait()


def shards(inputs, cotangent, weights, master, first_moment, second_moment):
    far = pl.BlockSpec(memory_space=pltpu.HBM)
    dma = pltpu.SemaphoreType.DMA
    vmem = pltpu.VMEM
    by_pairs = (BATCH, 16, 2, 32, CHANS)
    gathered, totals = pl.pallas_call(
        step_kernel,
        out_shape=(
            jax.ShapeDtypeStruct((2, 16, SLAB, CHANS), BF16),
            jax.ShapeDtypeStruct((2, ROWS, CHANS), F32),
        ),
        in_specs=[far] * 6,
        out_specs=(far, far),
        scratch_shapes=[
            vmem(by_pairs, BF16),
            vmem(by_pairs, BF16),
            vmem(weights.shape, BF16),
            vmem((2, 3, ROWS, CHANS), F32),
            vmem((BATCH, 2, 17, 32, 3 * CHANS), BF16),
            vmem((BATCH, 2, 17, 32, 3 * CHANS), BF16),
            vmem((12 * CHANS, 2 * CHANS), BF16),
            vmem((12 * CHANS, 2 * CHANS), BF16),
            vmem((CHANS, BATCH * 1024), BF16),
            vmem((BATCH, 512, 2 * CHANS), F32),
            vmem((CHANS, BATCH * 1024), BF16),
            vmem((2, 9 * CHANS, CHANS), F32),
            vmem((16, ROWS, CHANS), F32),
            vmem((16, SLAB, CHANS), BF16),
            vmem((16, SLAB, CHANS), BF16),
            vmem((ROWS, CHANS), F32),
            vmem((8, SLAB, CHANS), BF16),
            vmem((3, ROWS, CHANS), F32),
            vmem((2, ROWS, CHANS), F32),
            vmem((2, 16, SLAB, CHANS), BF16),
            dma((9,)),
            dma((16,)), dma((16,)), dma((16,)), dma((16,)), dma((8,)), dma((8,)), dma((4,)), dma,
            dma((4,)), dma, dma, dma, dma((16,)), dma((16,)), dma((16,)), dma((16,)), dma((2, 2)),
        ],
        compiler_params=pltpu.CompilerParams(collective_id=0, has_side_effects=True, vmem_limit_bytes=60 * 2**20),
        name="step",
    )(inputs.reshape(by_pairs), cotangent.reshape(by_pairs), weights, master, first_moment, second_moment)
    state = jax.ShapeDtypeStruct(master.shape, F32)
    return pl.pallas_call(
        finish_kernel,
        out_shape=(jax.ShapeDtypeStruct(weights.shape, BF16), state, state, state),
        in_specs=[far] * 5,
        out_specs=(far,) * 4,
        scratch_shapes=[
            vmem((2, 16, SLAB, CHANS), BF16),
            vmem(weights.shape, BF16),
            vmem((4,) + master.shape, F32),
            vmem((3,) + master.shape, F32),
            dma((4,)), dma((4,)), dma((4,)), dma((3,)),
        ],
        compiler_params=pltpu.CompilerParams(vmem_limit_bytes=60 * 2**20),
        name="finish",
    )(gathered, totals, master, first_moment, second_moment)


def solution(mesh):
    placed = (
        P(("grp", "dev"), None, None, None),
        P(("grp", "dev"), None, None, None),
        P(),
        P(None, "dev", None),
        P(None, "dev", None),
        P(None, "dev", None),
    )
    return jax.shard_map(
        shards,
        mesh=mesh,
        in_specs=placed,
        out_specs=(P(), P(None, "dev", None), P(None, "dev", None), P(None, "dev", None)),
        check_vma=False,
    )
```

```python
import jax
import jax.numpy as jnp
from jax import lax
from jax.experimental import pallas as pl
from jax.experimental.pallas import tpu as pltpu
from jax.sharding import PartitionSpec as P

STEP = 10
MESH = pl.DeviceIdType.MESH
BF16, F32 = jnp.bfloat16, jnp.float32
BATCH, CHANS = 4, 128
ROWS = 72
SLAB = 80


def adamw(grad, master_part, first_part, second_part):
    first_new = 0.9 * first_part + 0.1 * grad
    second_new = 0.95 * second_part + 0.05 * grad * grad
    corr_one = 1.0 - 0.9**STEP
    corr_two = 1.0 - 0.95**STEP
    update = first_new / corr_one / (jnp.sqrt(second_new / corr_two) + 1e-08)
    master_new = master_part - 0.001 * (update + 0.1 * master_part)
    return (master_new, first_new, second_new)


def shift_store(src_ref, dst_ref, image):
    edge = jnp.zeros((16, 1, CHANS), BF16)
    for odd in range(2):
        rows = src_ref[image, :, odd]
        place = pl.ds(odd, 16)
        dst_ref[image, 1 - odd, place, :, 0:128] = jnp.concatenate([edge, rows[:, :31]], axis=1)
        dst_ref[image, 1 - odd, place, :, 128:256] = rows
        dst_ref[image, 1 - odd, place, :, 256:384] = jnp.concatenate([rows[:, 1:], edge], axis=1)
    zero = jnp.zeros((32, 3 * CHANS), BF16)
    dst_ref[image, 0, 0] = zero
    dst_ref[image, 1, 16] = zero


def four_rows(ref, image):
    return jnp.concatenate(
        [ref[image, k % 2, pl.ds(k // 2, 16)].reshape(512, 3 * CHANS) for k in range(4)], axis=1
    )


def pair_forward(w_ref, out_ref):
    zero = jnp.zeros((CHANS, CHANS), BF16)
    for k in range(4):
        for tj in range(3):
            rows = pl.ds((k * 3 + tj) * CHANS, CHANS)
            for odd in range(2):
                tap = (k - odd) * 3 + tj
                block = w_ref[0, tap * CHANS : (tap + 1) * CHANS, :] if 0 <= k - odd <= 2 else zero
                out_ref[rows, odd * CHANS : (odd + 1) * CHANS] = block


def pair_backward(w_ref, out_ref):
    zero = jnp.zeros((CHANS, CHANS), BF16)
    for k in range(4):
        for tj in range(3):
            rows = pl.ds((k * 3 + tj) * CHANS, CHANS)
            for odd in range(2):
                tap = (odd - k + 2) * 3 + 2 - tj
                block = w_ref[1, tap * CHANS : (tap + 1) * CHANS, :].T if 0 <= k - odd <= 2 else zero
                out_ref[rows, odd * CHANS : (odd + 1) * CHANS] = block


def put_turned(ref, value, image):
    turned = value.astype(BF16).T
    for odd in range(2):
        start = odd * BATCH * 512 + image * 512
        ref[:, start : start + 512] = turned[odd * CHANS : (odd + 1) * CHANS]


def outer_sum(turned, ref, first, last):
    out = None
    for odd in range(2):
        for image in range(BATCH):
            near = jnp.concatenate(
                [ref[image, (k + odd) % 2, pl.ds((k + odd) // 2, 16)].reshape(512, 3 * CHANS) for k in range(3)], axis=1
            )
            start = odd * BATCH * 512 + image * 512
            part = jnp.dot(
                turned[:, start : start + 512], near[:, first * CHANS : last * CHANS], preferred_element_type=F32
            )
            out = part if out is None else out + part
    return out


def step_kernel(x_hbm, c_hbm, w_hbm, master_hbm, first_hbm, second_hbm,
                gathered_out, totals_out,
                x_ref, c_ref, w_ref, state_ref,
                x3, c3, forward_w, backward_w, act, slope, dpre, grads,
                pair_recv, xy_send, xy_recv, xy_own, z_parts, held, totals, gathered,
                load_s, pair_ss, pair_rs, xy_ss, xy_rs, z_ss, z_rs, held_ss, held_rs, t_ss, t_rs, tot_ss, tot_rs,
                gat_ss, gat_rs, fwd_ss, fwd_rs, put_s):
    grp = lax.axis_index("grp")
    dev = lax.axis_index("dev")
    core = lax.rem(grp, 2)
    y = lax.rem(grp, 8) // 2
    z_hi = grp // 8
    x = lax.rem(dev, 4)
    z_lo = dev // 4
    z = z_hi * 4 + z_lo
    partner = (grp + 1 - 2 * core, dev)

    def xy_peer(kx, ky):
        return (z_hi * 8 + lax.rem(y + ky, 4) * 2 + core, z_lo * 4 + lax.rem(x + kx, 4))

    def z_peer(kz):
        other = lax.rem(z + kz, 8)
        return (other // 4 * 8 + y * 2 + core, lax.rem(other, 4) * 4 + x)

    def held_peer(k):
        return (grp, lax.rem(z_lo + k, 4) * 4 + x)

    def remote(src, dst, ss, rs, target):
        return pltpu.make_async_remote_copy(
            src_ref=src, dst_ref=dst, send_sem=ss, recv_sem=rs, device_id=target, device_id_type=MESH
        )

    loads = [
        pltpu.make_async_copy(src, dst, load_s.at[k])
        for k, (src, dst) in enumerate(
            [(x_hbm, x_ref), (w_hbm, w_ref), (c_hbm, c_ref)]
            + [(ref.at[layer], state_ref.at[layer, k])
               for k, ref in enumerate((master_hbm, first_hbm, second_hbm)) for layer in range(2)]
        )
    ]
    for copy in loads:
        copy.start()
    xy_order = [(kx, ky) for kx in (2, 1, 3, 0) for ky in (2, 1, 3, 0) if kx or ky]
    xy_steps = [(kx, ky) for kx in (0, 1, 3, 2) for ky in (0, 1, 3, 2) if kx or ky]
    z_order = (4, 3, 5, 2, 6, 1, 7)
    peers = [partner] + [xy_peer(*k) for k in xy_steps] + [z_peer(k) for k in z_order]
    barrier = pltpu.get_barrier_semaphore()
    for peer in peers:
        pl.semaphore_signal(barrier, inc=1, device_id=peer, device_id_type=MESH)

    def place(kx, ky):
        return lax.rem(y + ky, 4) * 4 + lax.rem(x + kx, 4)

    def shard_rows(shard):
        start = shard * ROWS
        return pl.ds(start if isinstance(start, int) else pl.multiple_of(start, 8), ROWS)

    def pair_copy(layer, shard):
        src = grads.at[layer, shard_rows(shard), :]
        return remote(src, pair_recv.at[shard], pair_ss.at[shard], pair_rs.at[shard], partner)

    def xy_copy(kx, ky):
        slot = kx * 4 + ky
        return remote(xy_send.at[slot], xy_recv.at[slot], xy_ss.at[slot], xy_rs.at[slot], xy_peer(kx, ky))

    def send_pair(layer, first, last):
        for shard in range(first, last):
            pair_copy(layer, shard).start()

    def sum_pair(layer):
        for kx, ky in xy_order + [(0, 0)]:
            slot, shard = kx * 4 + ky, place(kx, ky)
            pair_copy(layer, shard).wait_recv()
            both = grads[layer, shard_rows(shard), :] + pair_recv[shard]
            if slot:
                xy_send[slot, 0:ROWS, :] = both.astype(BF16)
                xy_copy(kx, ky).start()
            else:
                xy_own[...] = both

    for copy in loads:
        copy.wait()
    pair_forward(w_ref, forward_w)
    shift_store(x_ref, x3, 0)
    for image in range(BATCH):
        pre = jnp.dot(four_rows(x3, image), forward_w[...], preferred_element_type=F32)
        sig = 1.0 / (1.0 + jnp.exp(-pre))
        value = pre * sig
        put_turned(act, value, image)
        slope[image] = sig + value * (1.0 - sig)
        if image < BATCH - 1:
            shift_store(x_ref, x3, image + 1)
        shift_store(c_ref, c3, image)

    pair_backward(w_ref, backward_w)
    out = outer_sum(act, c3, 0, 9)
    for block in range(9):
        tap = 8 - block
        grads[1, tap * CHANS : (tap + 1) * CHANS, :] = out[:, block * CHANS : (block + 1) * CHANS]

    pl.semaphore_wait(barrier, len(peers))

    def held_copy(k, source_ref):
        return remote(source_ref, held, held_ss.at[k], held_rs, held_peer(k))

    @pl.when(z_lo == y)
    def _():
        held[...] = state_ref[core]
        for k in range(1, 4):
            held_copy(k, held).start()

    @pl.when(core == 0)
    def _():
        send_pair(1, 0, 16)

    for image in range(BATCH):
        back = jnp.dot(four_rows(c3, image), backward_w[...], preferred_element_type=F32)
        put_turned(dpre, back * slope[image], image)

    def first_layer(first, last):
        out = outer_sum(dpre, x3, first, last)
        for tap in range(first, last):
            block = out[:, (tap - first) * CHANS : (tap + 1 - first) * CHANS]
            grads[0, tap * CHANS : (tap + 1) * CHANS, :] = block.T

    first_layer(0, 4)

    @pl.when(core == 1)
    def _():
        send_pair(0, 0, 7)

    first_layer(4, 9)

    @pl.when(core == 1)
    def _():
        send_pair(0, 7, 16)
        sum_pair(1)

    @pl.when(core == 0)
    def _():
        sum_pair(0)

    acc = xy_own[...]
    for kx, ky in xy_steps:
        xy_copy(kx, ky).wait_recv()
        acc = acc + xy_recv[kx * 4 + ky, 0:ROWS, :].astype(F32)
    z_parts[z, 0:ROWS, :] = acc.astype(BF16)

    def z_copy(kz, place):
        return remote(z_parts.at[place], z_parts.at[place], z_ss.at[kz], z_rs.at[kz], z_peer(kz))

    for kz in z_order:
        z_copy(kz, z).start()
    for kz in z_order[::-1]:
        z_copy(kz, lax.rem(z + 8 - kz, 8)).wait_recv()
    z_part = [z_parts[k, 0:ROWS, :].astype(F32) for k in range(8)]
    halves = [(z_part[k] + z_part[k + 1]) + (z_part[k + 2] + z_part[k + 3]) for k in (0, 4)]
    whole = halves[0] + halves[1]

    @pl.when(z_lo != y)
    def _():
        held_copy(1, held).wait_recv()

    slab = adamw(whole, held[0], held[1], held[2])[0].astype(BF16)
    gathered[y * 4 + x, 0:ROWS, :] = slab

    def gat_copy(kx, ky, slot):
        ref = gathered.at[slot]
        return remote(ref, ref, gat_ss.at[kx * 4 + ky], gat_rs.at[kx * 4 + ky], xy_peer(kx, ky))

    def source(kx, ky):
        return place(4 - kx, 4 - ky)

    def fwd_copy(layer, kx, ky):
        slot = source(kx, ky)
        k = kx * 4 + ky
        return remote(gathered.at[slot], gathered_out.at[layer, slot], fwd_ss.at[k], fwd_rs.at[k], partner)

    for kx, ky in xy_order:
        gat_copy(kx, ky, source(0, 0)).start()
    fwd_copy(core, 0, 0).start()

    def t_copy(ky):
        return remote(totals, totals, t_ss.at[ky], t_rs, xy_peer(0, ky))

    @pl.when(z_lo == y)
    def _():
        totals[...] = whole
        for ky in (2, 1, 3):
            t_copy(ky).start()

    def forward(steps):
        for kx, ky in steps:
            gat_copy(kx, ky, source(kx, ky)).wait_recv()
            fwd_copy(core, kx, ky).start()

    forward(xy_steps[:3])

    @pl.when(z_lo != y)
    def _():
        t_copy(1).wait_recv()

    tot = remote(totals, totals_out.at[core], tot_ss, tot_rs, partner)
    tot.start()
    puts = [
        pltpu.make_async_copy(totals, totals_out.at[core], put_s.at[0]),
        pltpu.make_async_copy(gathered, gathered_out.at[core], put_s.at[1]),
    ]
    puts[0].start()
    forward(xy_steps[3:])
    puts[1].start()
    remote(totals, totals_out.at[1 - core], tot_ss, tot_rs, partner).wait_recv()
    for kx, ky in xy_steps + [(0, 0)]:
        fwd_copy(1 - core, kx, ky).wait_recv()
    for k in range(16):
        pair_copy(1 - core, k).wait_send()
        fwd_copy(core, k // 4, k % 4).wait_send()
    for kx, ky in xy_steps:
        xy_copy(kx, ky).wait_send()
        gat_copy(kx, ky, source(0, 0)).wait_send()
    for kz in z_order:
        z_copy(kz, z).wait_send()

    @pl.when(z_lo == y)
    def _():
        for k in range(1, 4):
            held_copy(k, held).wait_send()
            t_copy(k).wait_send()

    tot.wait_send()
    for copy in puts:
        copy.wait()


def finish_kernel(gathered_hbm, totals_hbm, master_hbm, first_hbm, second_hbm,
                  weights_hbm, master_out, first_out, second_out,
                  gathered, weights, held, new, load_s, state_s, store_s, new_s):
    loads, stores = [], []
    for k in range(4):
        layer, part = k // 2, pl.ds(k % 2 * 8, 8)
        loads.append(pltpu.make_async_copy(gathered_hbm.at[layer, part], gathered.at[layer, part], load_s.at[k]))
        rows = pl.ds(k % 2 * 8 * ROWS, 8 * ROWS)
        stores.append(pltpu.make_async_copy(weights.at[layer, rows], weights_hbm.at[layer, rows], store_s.at[k]))
    states = [
        pltpu.make_async_copy(src, held.at[k], state_s.at[k])
        for k, src in enumerate((totals_hbm, master_hbm, first_hbm, second_hbm))
    ]
    for copy in states + loads:
        copy.start()
    for copy in states:
        copy.wait()
    for k, value in enumerate(adamw(held[0], held[1], held[2], held[3])):
        new[k] = value
        store = pltpu.make_async_copy(new.at[k], (master_out, first_out, second_out)[k], new_s.at[k])
        store.start()
        stores.append(store)
    for k in range(4):
        loads[k].wait()
        for two in range(k % 2 * 4, k % 2 * 4 + 4):
            both = [gathered[k // 2, 2 * two + odd, 0:ROWS, :].astype(F32) for odd in range(2)]
            weights[k // 2, 2 * ROWS * two : 2 * ROWS * (two + 1), :] = jnp.concatenate(both, axis=0).astype(BF16)
        stores[k].start()
    for copy in stores:
        copy.wait()


def shards(inputs, cotangent, weights, master, first_moment, second_moment):
    far = pl.BlockSpec(memory_space=pltpu.HBM)
    dma = pltpu.SemaphoreType.DMA
    vmem = pltpu.VMEM
    by_pairs = (BATCH, 16, 2, 32, CHANS)
    gathered, totals = pl.pallas_call(
        step_kernel,
        out_shape=(
            jax.ShapeDtypeStruct((2, 16, SLAB, CHANS), BF16),
            jax.ShapeDtypeStruct((2, ROWS, CHANS), F32),
        ),
        in_specs=[far] * 6,
        out_specs=(far, far),
        scratch_shapes=[
            vmem(by_pairs, BF16),
            vmem(by_pairs, BF16),
            vmem(weights.shape, BF16),
            vmem((2, 3, ROWS, CHANS), F32),
            vmem((BATCH, 2, 17, 32, 3 * CHANS), BF16),
            vmem((BATCH, 2, 17, 32, 3 * CHANS), BF16),
            vmem((12 * CHANS, 2 * CHANS), BF16),
            vmem((12 * CHANS, 2 * CHANS), BF16),
            vmem((CHANS, BATCH * 1024), BF16),
            vmem((BATCH, 512, 2 * CHANS), F32),
            vmem((CHANS, BATCH * 1024), BF16),
            vmem((2, 9 * CHANS, CHANS), F32),
            vmem((16, ROWS, CHANS), F32),
            vmem((16, SLAB, CHANS), BF16),
            vmem((16, SLAB, CHANS), BF16),
            vmem((ROWS, CHANS), F32),
            vmem((8, SLAB, CHANS), BF16),
            vmem((3, ROWS, CHANS), F32),
            vmem((ROWS, CHANS), F32),
            vmem((16, SLAB, CHANS), BF16),
            dma((9,)),
            dma((16,)), dma((16,)), dma((16,)), dma((16,)), dma((8,)), dma((8,)), dma((4,)), dma,
            dma((4,)), dma, dma, dma, dma((16,)), dma((16,)), dma((16,)), dma((16,)), dma((2,)),
        ],
        compiler_params=pltpu.CompilerParams(collective_id=0, has_side_effects=True, vmem_limit_bytes=60 * 2**20),
        name="step",
    )(inputs.reshape(by_pairs), cotangent.reshape(by_pairs), weights, master, first_moment, second_moment)
    state = jax.ShapeDtypeStruct(master.shape, F32)
    return pl.pallas_call(
        finish_kernel,
        out_shape=(jax.ShapeDtypeStruct(weights.shape, BF16), state, state, state),
        in_specs=[far] * 5,
        out_specs=(far,) * 4,
        scratch_shapes=[
            vmem((2, 16, SLAB, CHANS), BF16),
            vmem(weights.shape, BF16),
            vmem((4,) + master.shape, F32),
            vmem((3,) + master.shape, F32),
            dma((4,)), dma((4,)), dma((4,)), dma((3,)),
        ],
        compiler_params=pltpu.CompilerParams(vmem_limit_bytes=60 * 2**20),
        name="finish",
    )(gathered, totals, master, first_moment, second_moment)


def solution(mesh):
    placed = (
        P(("grp", "dev"), None, None, None),
        P(("grp", "dev"), None, None, None),
        P(),
        P(None, "dev", None),
        P(None, "dev", None),
        P(None, "dev", None),
    )
    return jax.shard_map(
        shards,
        mesh=mesh,
        in_specs=placed,
        out_specs=(P(), P(None, "dev", None), P(None, "dev", None), P(None, "dev", None)),
        check_vma=False,
    )
```

```python
import jax
import jax.numpy as jnp
from jax import lax
from jax.experimental import pallas as pl
from jax.experimental.pallas import tpu as pltpu
from jax.sharding import PartitionSpec as P

STEP = 10
MESH = pl.DeviceIdType.MESH
BF16, F32 = jnp.bfloat16, jnp.float32
BATCH, CHANS = 4, 128
ROWS = 72
SLAB = 80


def adamw(grad, master_part, first_part, second_part):
    first_new = 0.9 * first_part + 0.1 * grad
    second_new = 0.95 * second_part + 0.05 * grad * grad
    corr_one = 1.0 - 0.9**STEP
    corr_two = 1.0 - 0.95**STEP
    update = first_new / corr_one / (jnp.sqrt(second_new / corr_two) + 1e-08)
    master_new = master_part - 0.001 * (update + 0.1 * master_part)
    return (master_new, first_new, second_new)


def shift_store(src_ref, dst_ref, image):
    edge = jnp.zeros((16, 1, CHANS), BF16)
    for odd in range(2):
        rows = src_ref[image, :, odd]
        place = pl.ds(odd, 16)
        dst_ref[image, 1 - odd, place, :, 0:128] = jnp.concatenate([edge, rows[:, :31]], axis=1)
        dst_ref[image, 1 - odd, place, :, 128:256] = rows
        dst_ref[image, 1 - odd, place, :, 256:384] = jnp.concatenate([rows[:, 1:], edge], axis=1)
    zero = jnp.zeros((32, 3 * CHANS), BF16)
    dst_ref[image, 0, 0] = zero
    dst_ref[image, 1, 16] = zero


def four_rows(ref, image):
    return jnp.concatenate(
        [ref[image, k % 2, pl.ds(k // 2, 16)].reshape(512, 3 * CHANS) for k in range(4)], axis=1
    )


def pair_forward(w_ref, out_ref):
    zero = jnp.zeros((CHANS, CHANS), BF16)
    for k in range(4):
        for tj in range(3):
            rows = pl.ds((k * 3 + tj) * CHANS, CHANS)
            for odd in range(2):
                tap = (k - odd) * 3 + tj
                block = w_ref[0, tap * CHANS : (tap + 1) * CHANS, :] if 0 <= k - odd <= 2 else zero
                out_ref[rows, odd * CHANS : (odd + 1) * CHANS] = block


def pair_backward(w_ref, out_ref):
    zero = jnp.zeros((CHANS, CHANS), BF16)
    for k in range(4):
        for tj in range(3):
            rows = pl.ds((k * 3 + tj) * CHANS, CHANS)
            for odd in range(2):
                tap = (odd - k + 2) * 3 + 2 - tj
                block = w_ref[1, tap * CHANS : (tap + 1) * CHANS, :].T if 0 <= k - odd <= 2 else zero
                out_ref[rows, odd * CHANS : (odd + 1) * CHANS] = block


def put_turned(ref, value, image):
    turned = value.astype(BF16).T
    for odd in range(2):
        start = odd * BATCH * 512 + image * 512
        ref[:, start : start + 512] = turned[odd * CHANS : (odd + 1) * CHANS]


def outer_sum(turned, ref, first, last):
    out = None
    for odd in range(2):
        for image in range(BATCH):
            near = jnp.concatenate(
                [ref[image, (k + odd) % 2, pl.ds((k + odd) // 2, 16)].reshape(512, 3 * CHANS) for k in range(3)], axis=1
            )
            start = odd * BATCH * 512 + image * 512
            part = jnp.dot(
                turned[:, start : start + 512], near[:, first * CHANS : last * CHANS], preferred_element_type=F32
            )
            out = part if out is None else out + part
    return out


def step_kernel(x_hbm, c_hbm, w_hbm, master_hbm, first_hbm, second_hbm,
                gathered_out, totals_out,
                x_ref, c_ref, w_ref, state_ref,
                x3, c3, forward_w, backward_w, act, slope, dpre, grads,
                xy_send, xy_recv, z_parts, held, totals, gathered,
                load_s, xy_ss, xy_rs, z_ss, z_rs, held_ss, held_rs, t_ss, t_rs, tot_ss, tot_rs,
                gat_ss, gat_rs, fwd_ss, fwd_rs, put_s):
    grp = lax.axis_index("grp")
    dev = lax.axis_index("dev")
    core = lax.rem(grp, 2)
    y = lax.rem(grp, 8) // 2
    z_hi = grp // 8
    x = lax.rem(dev, 4)
    z_lo = dev // 4
    z = z_hi * 4 + z_lo
    partner = (grp + 1 - 2 * core, dev)

    def xy_peer(kx, ky, at=core):
        return (z_hi * 8 + lax.rem(y + ky, 4) * 2 + at, z_lo * 4 + lax.rem(x + kx, 4))

    def z_peer(kz):
        other = lax.rem(z + kz, 8)
        return (other // 4 * 8 + y * 2 + core, lax.rem(other, 4) * 4 + x)

    def held_peer(k):
        return (grp, lax.rem(z_lo + k, 4) * 4 + x)

    def remote(src, dst, ss, rs, target):
        return pltpu.make_async_remote_copy(
            src_ref=src, dst_ref=dst, send_sem=ss, recv_sem=rs, device_id=target, device_id_type=MESH
        )

    loads = [
        pltpu.make_async_copy(src, dst, load_s.at[k])
        for k, (src, dst) in enumerate(
            [(x_hbm, x_ref), (w_hbm, w_ref), (c_hbm, c_ref)]
            + [(ref.at[layer], state_ref.at[layer, k])
               for k, ref in enumerate((master_hbm, first_hbm, second_hbm)) for layer in range(2)]
        )
    ]
    for copy in loads:
        copy.start()
    xy_order = [(kx, ky) for kx in (2, 1, 3, 0) for ky in (2, 1, 3, 0) if kx or ky]
    xy_steps = [(kx, ky) for kx in (0, 1, 3, 2) for ky in (0, 1, 3, 2) if kx or ky]
    z_order = (4, 3, 5, 2, 6, 1, 7)
    peers = [partner] + [xy_peer(*k, at) for k in xy_steps for at in range(2)] + [z_peer(k) for k in z_order]
    barrier = pltpu.get_barrier_semaphore()
    for peer in peers:
        pl.semaphore_signal(barrier, inc=1, device_id=peer, device_id_type=MESH)

    def place(kx, ky):
        return lax.rem(y + ky, 4) * 4 + lax.rem(x + kx, 4)

    def shard_rows(shard):
        start = shard * ROWS
        return pl.ds(start if isinstance(start, int) else pl.multiple_of(start, 8), ROWS)

    own = y * 4 + x

    def xy_copy(layer, shard):
        other = 1 - core if layer else core
        kx, ky = lax.rem(shard % 4 + 4 - x, 4), lax.rem(shard // 4 + 4 - y, 4)
        slot = other * 16 + kx * 4 + ky
        target = (z_hi * 8 + shard // 4 * 2 + layer, z_lo * 4 + shard % 4)
        copy = remote(xy_send.at[layer, shard], xy_recv.at[slot], xy_ss.at[layer, shard], xy_rs.at[slot], target)
        return copy, slot > 0

    def send_parts(layer, first, last):
        for shard in range(first, last):
            copy, remote_one = xy_copy(layer, shard)
            pl.when(remote_one)(copy.start)

    def round_parts(layer, first, last):
        for shard in range(first, last):
            xy_send[layer, shard, 0:ROWS, :] = grads[layer, shard_rows(shard), :].astype(BF16)

    for copy in loads:
        copy.wait()
    pair_forward(w_ref, forward_w)
    shift_store(x_ref, x3, 0)
    for image in range(BATCH):
        pre = jnp.dot(four_rows(x3, image), forward_w[...], preferred_element_type=F32)
        sig = 1.0 / (1.0 + jnp.exp(-pre))
        value = pre * sig
        put_turned(act, value, image)
        slope[image] = sig + value * (1.0 - sig)
        if image < BATCH - 1:
            shift_store(x_ref, x3, image + 1)
        shift_store(c_ref, c3, image)

    pair_backward(w_ref, backward_w)
    out = outer_sum(act, c3, 0, 9)
    for block in range(9):
        tap = 8 - block
        grads[1, tap * CHANS : (tap + 1) * CHANS, :] = out[:, block * CHANS : (block + 1) * CHANS]
    round_parts(1, 0, 16)

    pl.semaphore_wait(barrier, len(peers))
    send_parts(1, 0, 16)

    def held_copy(k, source_ref):
        return remote(source_ref, held, held_ss.at[k], held_rs, held_peer(k))

    @pl.when(z_lo == y)
    def _():
        held[...] = state_ref[core]
        for k in range(1, 4):
            held_copy(k, held).start()

    for image in range(BATCH):
        back = jnp.dot(four_rows(c3, image), backward_w[...], preferred_element_type=F32)
        put_turned(dpre, back * slope[image], image)

    def first_layer(first, last):
        out = outer_sum(dpre, x3, first, last)
        for tap in range(first, last):
            block = out[:, (tap - first) * CHANS : (tap + 1 - first) * CHANS]
            grads[0, tap * CHANS : (tap + 1) * CHANS, :] = block.T

    first_layer(0, 4)
    round_parts(0, 0, 7)
    send_parts(0, 0, 7)
    first_layer(4, 9)
    round_parts(0, 7, 16)
    send_parts(0, 7, 16)

    acc = grads[core, shard_rows(own), :]
    for kx, ky in [(0, 0)] + xy_steps:
        for other in range(2):
            slot = other * 16 + kx * 4 + ky
            if slot:
                ref = xy_recv.at[slot]
                remote(ref, ref, xy_ss.at[0, 0], xy_rs.at[slot], partner).wait_recv()
                acc = acc + xy_recv[slot, 0:ROWS, :].astype(F32)
    z_parts[z, 0:ROWS, :] = acc.astype(BF16)

    def z_copy(kz, place):
        return remote(z_parts.at[place], z_parts.at[place], z_ss.at[kz], z_rs.at[kz], z_peer(kz))

    for kz in z_order:
        z_copy(kz, z).start()
    for kz in z_order[::-1]:
        z_copy(kz, lax.rem(z + 8 - kz, 8)).wait_recv()
    z_part = [z_parts[k, 0:ROWS, :].astype(F32) for k in range(8)]
    halves = [(z_part[k] + z_part[k + 1]) + (z_part[k + 2] + z_part[k + 3]) for k in (0, 4)]
    whole = halves[0] + halves[1]

    @pl.when(z_lo != y)
    def _():
        held_copy(1, held).wait_recv()

    slab = adamw(whole, held[0], held[1], held[2])[0].astype(BF16)
    gathered[y * 4 + x, 0:ROWS, :] = slab

    def gat_copy(kx, ky, slot):
        ref = gathered.at[slot]
        return remote(ref, ref, gat_ss.at[kx * 4 + ky], gat_rs.at[kx * 4 + ky], xy_peer(kx, ky))

    def source(kx, ky):
        return place(4 - kx, 4 - ky)

    def fwd_copy(layer, kx, ky):
        slot = source(kx, ky)
        k = kx * 4 + ky
        return remote(gathered.at[slot], gathered_out.at[layer, slot], fwd_ss.at[k], fwd_rs.at[k], partner)

    for kx, ky in xy_order:
        gat_copy(kx, ky, source(0, 0)).start()
    fwd_copy(core, 0, 0).start()

    def t_copy(ky):
        return remote(totals, totals, t_ss.at[ky], t_rs, xy_peer(0, ky))

    @pl.when(z_lo == y)
    def _():
        totals[...] = whole
        for ky in (2, 1, 3):
            t_copy(ky).start()

    def forward(steps):
        for kx, ky in steps:
            gat_copy(kx, ky, source(kx, ky)).wait_recv()
            fwd_copy(core, kx, ky).start()

    forward(xy_steps[:3])

    @pl.when(z_lo != y)
    def _():
        t_copy(1).wait_recv()

    tot = remote(totals, totals_out.at[core], tot_ss, tot_rs, partner)
    tot.start()
    puts = [
        pltpu.make_async_copy(totals, totals_out.at[core], put_s.at[0]),
        pltpu.make_async_copy(gathered, gathered_out.at[core], put_s.at[1]),
    ]
    puts[0].start()
    forward(xy_steps[3:])
    puts[1].start()
    remote(totals, totals_out.at[1 - core], tot_ss, tot_rs, partner).wait_recv()
    for kx, ky in xy_steps + [(0, 0)]:
        fwd_copy(1 - core, kx, ky).wait_recv()
    for k in range(16):
        fwd_copy(core, k // 4, k % 4).wait_send()
        for layer in range(2):
            copy, remote_one = xy_copy(layer, k)
            pl.when(remote_one)(copy.wait_send)
    for kx, ky in xy_steps:
        gat_copy(kx, ky, source(0, 0)).wait_send()
    for kz in z_order:
        z_copy(kz, z).wait_send()

    @pl.when(z_lo == y)
    def _():
        for k in range(1, 4):
            held_copy(k, held).wait_send()
            t_copy(k).wait_send()

    tot.wait_send()
    for copy in puts:
        copy.wait()


def finish_kernel(gathered_hbm, totals_hbm, master_hbm, first_hbm, second_hbm,
                  weights_hbm, master_out, first_out, second_out,
                  gathered, weights, held, new, load_s, state_s, store_s, new_s):
    loads, stores = [], []
    for k in range(4):
        layer, part = k // 2, pl.ds(k % 2 * 8, 8)
        loads.append(pltpu.make_async_copy(gathered_hbm.at[layer, part], gathered.at[layer, part], load_s.at[k]))
        rows = pl.ds(k % 2 * 8 * ROWS, 8 * ROWS)
        stores.append(pltpu.make_async_copy(weights.at[layer, rows], weights_hbm.at[layer, rows], store_s.at[k]))
    states = [
        pltpu.make_async_copy(src, held.at[k], state_s.at[k])
        for k, src in enumerate((totals_hbm, master_hbm, first_hbm, second_hbm))
    ]
    for copy in states + loads:
        copy.start()
    for copy in states:
        copy.wait()
    for k, value in enumerate(adamw(held[0], held[1], held[2], held[3])):
        new[k] = value
        store = pltpu.make_async_copy(new.at[k], (master_out, first_out, second_out)[k], new_s.at[k])
        store.start()
        stores.append(store)
    for k in range(4):
        loads[k].wait()
        for two in range(k % 2 * 4, k % 2 * 4 + 4):
            both = [gathered[k // 2, 2 * two + odd, 0:ROWS, :].astype(F32) for odd in range(2)]
            weights[k // 2, 2 * ROWS * two : 2 * ROWS * (two + 1), :] = jnp.concatenate(both, axis=0).astype(BF16)
        stores[k].start()
    for copy in stores:
        copy.wait()


def shards(inputs, cotangent, weights, master, first_moment, second_moment):
    far = pl.BlockSpec(memory_space=pltpu.HBM)
    dma = pltpu.SemaphoreType.DMA
    vmem = pltpu.VMEM
    by_pairs = (BATCH, 16, 2, 32, CHANS)
    gathered, totals = pl.pallas_call(
        step_kernel,
        out_shape=(
            jax.ShapeDtypeStruct((2, 16, SLAB, CHANS), BF16),
            jax.ShapeDtypeStruct((2, ROWS, CHANS), F32),
        ),
        in_specs=[far] * 6,
        out_specs=(far, far),
        scratch_shapes=[
            vmem(by_pairs, BF16),
            vmem(by_pairs, BF16),
            vmem(weights.shape, BF16),
            vmem((2, 3, ROWS, CHANS), F32),
            vmem((BATCH, 2, 17, 32, 3 * CHANS), BF16),
            vmem((BATCH, 2, 17, 32, 3 * CHANS), BF16),
            vmem((12 * CHANS, 2 * CHANS), BF16),
            vmem((12 * CHANS, 2 * CHANS), BF16),
            vmem((CHANS, BATCH * 1024), BF16),
            vmem((BATCH, 512, 2 * CHANS), F32),
            vmem((CHANS, BATCH * 1024), BF16),
            vmem((2, 9 * CHANS, CHANS), F32),
            vmem((2, 16, SLAB, CHANS), BF16),
            vmem((32, SLAB, CHANS), BF16),
            vmem((8, SLAB, CHANS), BF16),
            vmem((3, ROWS, CHANS), F32),
            vmem((ROWS, CHANS), F32),
            vmem((16, SLAB, CHANS), BF16),
            dma((9,)),
            dma((2, 16)), dma((32,)), dma((8,)), dma((8,)), dma((4,)), dma,
            dma((4,)), dma, dma, dma, dma((16,)), dma((16,)), dma((16,)), dma((16,)), dma((2,)),
        ],
        compiler_params=pltpu.CompilerParams(collective_id=0, has_side_effects=True, vmem_limit_bytes=60 * 2**20),
        name="step",
    )(inputs.reshape(by_pairs), cotangent.reshape(by_pairs), weights, master, first_moment, second_moment)
    state = jax.ShapeDtypeStruct(master.shape, F32)
    return pl.pallas_call(
        finish_kernel,
        out_shape=(jax.ShapeDtypeStruct(weights.shape, BF16), state, state, state),
        in_specs=[far] * 5,
        out_specs=(far,) * 4,
        scratch_shapes=[
            vmem((2, 16, SLAB, CHANS), BF16),
            vmem(weights.shape, BF16),
            vmem((4,) + master.shape, F32),
            vmem((3,) + master.shape, F32),
            dma((4,)), dma((4,)), dma((4,)), dma((3,)),
        ],
        compiler_params=pltpu.CompilerParams(vmem_limit_bytes=60 * 2**20),
        name="finish",
    )(gathered, totals, master, first_moment, second_moment)


def solution(mesh):
    placed = (
        P(("grp", "dev"), None, None, None),
        P(("grp", "dev"), None, None, None),
        P(),
        P(None, "dev", None),
        P(None, "dev", None),
        P(None, "dev", None),
    )
    return jax.shard_map(
        shards,
        mesh=mesh,
        in_specs=placed,
        out_specs=(P(), P(None, "dev", None), P(None, "dev", None), P(None, "dev", None)),
        check_vma=False,
    )
```

```python
import jax
import jax.numpy as jnp
from jax import lax
from jax.experimental import pallas as pl
from jax.experimental.pallas import tpu as pltpu
from jax.sharding import PartitionSpec as P

STEP = 10
MESH = pl.DeviceIdType.MESH
BF16, F32 = jnp.bfloat16, jnp.float32
BATCH, CHANS = 4, 128
ROWS = 72
SLAB = 80


def adamw(grad, master_part, first_part, second_part):
    first_new = 0.9 * first_part + 0.1 * grad
    second_new = 0.95 * second_part + 0.05 * grad * grad
    corr_one = 1.0 - 0.9**STEP
    corr_two = 1.0 - 0.95**STEP
    update = first_new / corr_one / (jnp.sqrt(second_new / corr_two) + 1e-08)
    master_new = master_part - 0.001 * (update + 0.1 * master_part)
    return (master_new, first_new, second_new)


def shift_store(src_ref, dst_ref, image):
    edge = jnp.zeros((16, 1, CHANS), BF16)
    for odd in range(2):
        rows = src_ref[image, :, odd]
        place = pl.ds(odd, 16)
        dst_ref[image, 1 - odd, place, :, 0:128] = jnp.concatenate([edge, rows[:, :31]], axis=1)
        dst_ref[image, 1 - odd, place, :, 128:256] = rows
        dst_ref[image, 1 - odd, place, :, 256:384] = jnp.concatenate([rows[:, 1:], edge], axis=1)
    zero = jnp.zeros((32, 3 * CHANS), BF16)
    dst_ref[image, 0, 0] = zero
    dst_ref[image, 1, 16] = zero


def four_rows(ref, image):
    return jnp.concatenate(
        [ref[image, k % 2, pl.ds(k // 2, 16)].reshape(512, 3 * CHANS) for k in range(4)], axis=1
    )


def pair_forward(w_ref, out_ref):
    zero = jnp.zeros((CHANS, CHANS), BF16)
    for k in range(4):
        for tj in range(3):
            rows = pl.ds((k * 3 + tj) * CHANS, CHANS)
            for odd in range(2):
                tap = (k - odd) * 3 + tj
                block = w_ref[0, tap * CHANS : (tap + 1) * CHANS, :] if 0 <= k - odd <= 2 else zero
                out_ref[rows, odd * CHANS : (odd + 1) * CHANS] = block


def pair_backward(w_ref, out_ref):
    zero = jnp.zeros((CHANS, CHANS), BF16)
    for k in range(4):
        for tj in range(3):
            rows = pl.ds((k * 3 + tj) * CHANS, CHANS)
            for odd in range(2):
                tap = (odd - k + 2) * 3 + 2 - tj
                block = w_ref[1, tap * CHANS : (tap + 1) * CHANS, :].T if 0 <= k - odd <= 2 else zero
                out_ref[rows, odd * CHANS : (odd + 1) * CHANS] = block


def put_turned(ref, value, image):
    turned = value.astype(BF16).T
    for odd in range(2):
        start = odd * BATCH * 512 + image * 512
        ref[:, start : start + 512] = turned[odd * CHANS : (odd + 1) * CHANS]


def outer_sum(turned, ref, first, last):
    out = None
    for odd in range(2):
        for image in range(BATCH):
            near = jnp.concatenate(
                [ref[image, (k + odd) % 2, pl.ds((k + odd) // 2, 16)].reshape(512, 3 * CHANS) for k in range(3)], axis=1
            )
            start = odd * BATCH * 512 + image * 512
            part = jnp.dot(
                turned[:, start : start + 512], near[:, first * CHANS : last * CHANS], preferred_element_type=F32
            )
            out = part if out is None else out + part
    return out


def step_kernel(x_hbm, c_hbm, w_hbm, master_hbm, first_hbm, second_hbm,
                gathered_out, totals_out,
                x_ref, c_ref, w_ref, state_ref,
                x3, c3, forward_w, backward_w, act, slope, dpre, grads,
                xy_send, xy_recv, z_parts, held, totals, gathered,
                load_s, xy_ss, xy_rs, z_ss, z_rs, held_ss, held_rs, t_ss, t_rs, tot_ss, tot_rs,
                gat_ss, gat_rs, fwd_ss, fwd_rs, put_s):
    grp = lax.axis_index("grp")
    dev = lax.axis_index("dev")
    core = lax.rem(grp, 2)
    y = lax.rem(grp, 8) // 2
    z_hi = grp // 8
    x = lax.rem(dev, 4)
    z_lo = dev // 4
    z = z_hi * 4 + z_lo
    partner = (grp + 1 - 2 * core, dev)

    def xy_peer(kx, ky, at=core):
        return (z_hi * 8 + lax.rem(y + ky, 4) * 2 + at, z_lo * 4 + lax.rem(x + kx, 4))

    def z_peer(kz):
        other = lax.rem(z + kz, 8)
        return (other // 4 * 8 + y * 2 + core, lax.rem(other, 4) * 4 + x)

    def held_peer(k):
        return (grp, lax.rem(z_lo + k, 4) * 4 + x)

    def remote(src, dst, ss, rs, target):
        return pltpu.make_async_remote_copy(
            src_ref=src, dst_ref=dst, send_sem=ss, recv_sem=rs, device_id=target, device_id_type=MESH
        )

    loads = [
        pltpu.make_async_copy(src, dst, load_s.at[k])
        for k, (src, dst) in enumerate(
            [(w_hbm.at[0], w_ref.at[0]), (x_hbm, x_ref), (c_hbm, c_ref), (w_hbm.at[1], w_ref.at[1])]
            + [(ref.at[layer], state_ref.at[layer, k])
               for k, ref in enumerate((master_hbm, first_hbm, second_hbm)) for layer in range(2)]
        )
    ]
    for copy in loads[:2]:
        copy.start()
    xy_order = [(kx, ky) for kx in (2, 1, 3, 0) for ky in (2, 1, 3, 0) if kx or ky]
    xy_steps = [(kx, ky) for kx in (0, 1, 3, 2) for ky in (0, 1, 3, 2) if kx or ky]
    z_order = (4, 3, 5, 2, 6, 1, 7)
    peers = [partner] + [xy_peer(*k, at) for k in xy_steps for at in range(2)] + [z_peer(k) for k in z_order]
    barrier = pltpu.get_barrier_semaphore()
    for peer in peers:
        pl.semaphore_signal(barrier, inc=1, device_id=peer, device_id_type=MESH)

    def place(kx, ky):
        return lax.rem(y + ky, 4) * 4 + lax.rem(x + kx, 4)

    def shard_rows(shard):
        start = shard * ROWS
        return pl.ds(start if isinstance(start, int) else pl.multiple_of(start, 8), ROWS)

    own = y * 4 + x

    def xy_copy(layer, shard):
        other = 1 - core if layer else core
        kx, ky = lax.rem(shard % 4 + 4 - x, 4), lax.rem(shard // 4 + 4 - y, 4)
        slot = other * 16 + kx * 4 + ky
        target = (z_hi * 8 + shard // 4 * 2 + layer, z_lo * 4 + shard % 4)
        copy = remote(xy_send.at[layer, shard], xy_recv.at[slot], xy_ss.at[layer, shard], xy_rs.at[slot], target)
        return copy, slot > 0

    def send_parts(layer, first, last):
        for shard in range(first, last):
            copy, remote_one = xy_copy(layer, shard)
            pl.when(remote_one)(copy.start)

    def round_parts(layer, first, last):
        for shard in range(first, last):
            xy_send[layer, shard, 0:ROWS, :] = grads[layer, shard_rows(shard), :].astype(BF16)

    for copy in loads[:2]:
        copy.wait()
    for copy in loads[2:]:
        copy.start()
    pair_forward(w_ref, forward_w)
    shift_store(x_ref, x3, 0)
    for image in range(BATCH):
        pre = jnp.dot(four_rows(x3, image), forward_w[...], preferred_element_type=F32)
        sig = 1.0 / (1.0 + jnp.exp(-pre))
        value = pre * sig
        put_turned(act, value, image)
        slope[image] = sig + value * (1.0 - sig)
        if image < BATCH - 1:
            shift_store(x_ref, x3, image + 1)
    for copy in loads[2:]:
        copy.wait()
    pl.semaphore_wait(barrier, len(peers))
    pair_backward(w_ref, backward_w)
    for image in range(BATCH):
        shift_store(c_ref, c3, image)

    def second_layer(first, last):
        out = outer_sum(act, c3, first, last)
        for block in range(first, last):
            tap = 8 - block
            grads[1, tap * CHANS : (tap + 1) * CHANS, :] = out[:, (block - first) * CHANS : (block - first + 1) * CHANS]

    second_layer(0, 5)
    round_parts(1, 8, 16)
    send_parts(1, 8, 16)
    second_layer(5, 9)
    round_parts(1, 0, 8)
    send_parts(1, 0, 8)

    def held_copy(k, source_ref):
        return remote(source_ref, held, held_ss.at[k], held_rs, held_peer(k))

    @pl.when(z_lo == y)
    def _():
        held[...] = state_ref[core]
        for k in range(1, 4):
            held_copy(k, held).start()

    for image in range(BATCH):
        back = jnp.dot(four_rows(c3, image), backward_w[...], preferred_element_type=F32)
        put_turned(dpre, back * slope[image], image)

    def first_layer(first, last):
        out = outer_sum(dpre, x3, first, last)
        for tap in range(first, last):
            block = out[:, (tap - first) * CHANS : (tap + 1 - first) * CHANS]
            grads[0, tap * CHANS : (tap + 1) * CHANS, :] = block.T

    first_layer(0, 5)
    round_parts(0, 0, 8)
    send_parts(0, 0, 8)
    first_layer(5, 9)
    round_parts(0, 8, 16)
    send_parts(0, 8, 16)

    acc = grads[core, shard_rows(own), :]
    for kx, ky in [(0, 0)] + xy_steps:
        for other in range(2):
            slot = other * 16 + kx * 4 + ky
            if slot:
                ref = xy_recv.at[slot]
                remote(ref, ref, xy_ss.at[0, 0], xy_rs.at[slot], partner).wait_recv()
                acc = acc + xy_recv[slot, 0:ROWS, :].astype(F32)
    z_parts[z, 0:ROWS, :] = acc.astype(BF16)

    parts = (pl.ds(0, 32), pl.ds(32, SLAB - 32))

    def z_copy(kz, place, part):
        ref = z_parts.at[place, parts[part]]
        return remote(ref, ref, z_ss.at[part, kz], z_rs.at[part, kz], z_peer(kz))

    def gat_copy(kx, ky, slot, part):
        ref = gathered.at[slot, parts[part]]
        k = kx * 4 + ky
        return remote(ref, ref, gat_ss.at[part, k], gat_rs.at[part, k], xy_peer(kx, ky))

    for part in range(2):
        for kz in z_order:
            z_copy(kz, z, part).start()

    @pl.when(z_lo != y)
    def _():
        held_copy(1, held).wait_recv()

    for part, rows in enumerate((pl.ds(0, 32), pl.ds(32, ROWS - 32))):
        for kz in z_order[::-1]:
            z_copy(kz, lax.rem(z + 8 - kz, 8), part).wait_recv()
        z_part = [z_parts[k, rows, :].astype(F32) for k in range(8)]
        halves = [(z_part[k] + z_part[k + 1]) + (z_part[k + 2] + z_part[k + 3]) for k in (0, 4)]
        whole = halves[0] + halves[1]

        @pl.when(z_lo == y)
        def _(rows=rows, whole=whole):
            totals[rows, :] = whole

        gathered[own, rows, :] = adamw(whole, held[0, rows, :], held[1, rows, :], held[2, rows, :])[0].astype(BF16)
        for kx, ky in xy_order:
            gat_copy(kx, ky, own, part).start()

    def source(kx, ky):
        return place(4 - kx, 4 - ky)

    def fwd_copy(layer, kx, ky):
        slot = source(kx, ky)
        k = kx * 4 + ky
        return remote(gathered.at[slot], gathered_out.at[layer, slot], fwd_ss.at[k], fwd_rs.at[k], partner)

    fwd_copy(core, 0, 0).start()

    def t_copy(ky):
        return remote(totals, totals, t_ss.at[ky], t_rs, xy_peer(0, ky))

    @pl.when(z_lo == y)
    def _():
        for ky in (2, 1, 3):
            t_copy(ky).start()

    def forward(steps):
        for kx, ky in steps:
            for part in range(2):
                gat_copy(kx, ky, source(kx, ky), part).wait_recv()
            fwd_copy(core, kx, ky).start()

    forward(xy_steps[:3])

    @pl.when(z_lo != y)
    def _():
        t_copy(1).wait_recv()

    tot = remote(totals, totals_out.at[core], tot_ss, tot_rs, partner)
    tot.start()
    puts = [
        pltpu.make_async_copy(totals, totals_out.at[core], put_s.at[0]),
        pltpu.make_async_copy(gathered, gathered_out.at[core], put_s.at[1]),
    ]
    puts[0].start()
    forward(xy_steps[3:])
    puts[1].start()
    remote(totals, totals_out.at[1 - core], tot_ss, tot_rs, partner).wait_recv()
    for kx, ky in xy_steps + [(0, 0)]:
        fwd_copy(1 - core, kx, ky).wait_recv()
    for k in range(16):
        fwd_copy(core, k // 4, k % 4).wait_send()
        for layer in range(2):
            copy, remote_one = xy_copy(layer, k)
            pl.when(remote_one)(copy.wait_send)
    for kx, ky in xy_steps:
        for part in range(2):
            gat_copy(kx, ky, own, part).wait_send()
    for kz in z_order:
        for part in range(2):
            z_copy(kz, z, part).wait_send()

    @pl.when(z_lo == y)
    def _():
        for k in range(1, 4):
            held_copy(k, held).wait_send()
            t_copy(k).wait_send()

    tot.wait_send()
    for copy in puts:
        copy.wait()


def finish_kernel(gathered_hbm, totals_hbm, master_hbm, first_hbm, second_hbm,
                  weights_hbm, master_out, first_out, second_out,
                  gathered, weights, held, new, load_s, state_s, store_s, new_s):
    loads, stores = [], []
    for k in range(4):
        layer, part = k // 2, pl.ds(k % 2 * 8, 8)
        loads.append(pltpu.make_async_copy(gathered_hbm.at[layer, part], gathered.at[layer, part], load_s.at[k]))
        rows = pl.ds(k % 2 * 8 * ROWS, 8 * ROWS)
        stores.append(pltpu.make_async_copy(weights.at[layer, rows], weights_hbm.at[layer, rows], store_s.at[k]))
    states = [
        pltpu.make_async_copy(src, held.at[k], state_s.at[k])
        for k, src in enumerate((totals_hbm, master_hbm, first_hbm, second_hbm))
    ]
    for copy in states + loads:
        copy.start()
    for copy in states:
        copy.wait()
    for k, value in enumerate(adamw(held[0], held[1], held[2], held[3])):
        new[k] = value
        store = pltpu.make_async_copy(new.at[k], (master_out, first_out, second_out)[k], new_s.at[k])
        store.start()
        stores.append(store)
    for k in range(4):
        loads[k].wait()
        for two in range(k % 2 * 4, k % 2 * 4 + 4):
            both = [gathered[k // 2, 2 * two + odd, 0:ROWS, :].astype(F32) for odd in range(2)]
            weights[k // 2, 2 * ROWS * two : 2 * ROWS * (two + 1), :] = jnp.concatenate(both, axis=0).astype(BF16)
        stores[k].start()
    for copy in stores:
        copy.wait()


def shards(inputs, cotangent, weights, master, first_moment, second_moment):
    far = pl.BlockSpec(memory_space=pltpu.HBM)
    dma = pltpu.SemaphoreType.DMA
    vmem = pltpu.VMEM
    by_pairs = (BATCH, 16, 2, 32, CHANS)
    gathered, totals = pl.pallas_call(
        step_kernel,
        out_shape=(
            jax.ShapeDtypeStruct((2, 16, SLAB, CHANS), BF16),
            jax.ShapeDtypeStruct((2, ROWS, CHANS), F32),
        ),
        in_specs=[far] * 6,
        out_specs=(far, far),
        scratch_shapes=[
            vmem(by_pairs, BF16),
            vmem(by_pairs, BF16),
            vmem(weights.shape, BF16),
            vmem((2, 3, ROWS, CHANS), F32),
            vmem((BATCH, 2, 17, 32, 3 * CHANS), BF16),
            vmem((BATCH, 2, 17, 32, 3 * CHANS), BF16),
            vmem((12 * CHANS, 2 * CHANS), BF16),
            vmem((12 * CHANS, 2 * CHANS), BF16),
            vmem((CHANS, BATCH * 1024), BF16),
            vmem((BATCH, 512, 2 * CHANS), F32),
            vmem((CHANS, BATCH * 1024), BF16),
            vmem((2, 9 * CHANS, CHANS), F32),
            vmem((2, 16, SLAB, CHANS), BF16),
            vmem((32, SLAB, CHANS), BF16),
            vmem((8, SLAB, CHANS), BF16),
            vmem((3, ROWS, CHANS), F32),
            vmem((ROWS, CHANS), F32),
            vmem((16, SLAB, CHANS), BF16),
            dma((10,)),
            dma((2, 16)), dma((32,)), dma((2, 8)), dma((2, 8)), dma((4,)), dma,
            dma((4,)), dma, dma, dma, dma((2, 16)), dma((2, 16)), dma((16,)), dma((16,)), dma((2,)),
        ],
        compiler_params=pltpu.CompilerParams(collective_id=0, has_side_effects=True, vmem_limit_bytes=60 * 2**20),
        name="step",
    )(inputs.reshape(by_pairs), cotangent.reshape(by_pairs), weights, master, first_moment, second_moment)
    state = jax.ShapeDtypeStruct(master.shape, F32)
    return pl.pallas_call(
        finish_kernel,
        out_shape=(jax.ShapeDtypeStruct(weights.shape, BF16), state, state, state),
        in_specs=[far] * 5,
        out_specs=(far,) * 4,
        scratch_shapes=[
            vmem((2, 16, SLAB, CHANS), BF16),
            vmem(weights.shape, BF16),
            vmem((4,) + master.shape, F32),
            vmem((3,) + master.shape, F32),
            dma((4,)), dma((4,)), dma((4,)), dma((3,)),
        ],
        compiler_params=pltpu.CompilerParams(vmem_limit_bytes=60 * 2**20),
        name="finish",
    )(gathered, totals, master, first_moment, second_moment)


def solution(mesh):
    placed = (
        P(("grp", "dev"), None, None, None),
        P(("grp", "dev"), None, None, None),
        P(),
        P(None, "dev", None),
        P(None, "dev", None),
        P(None, "dev", None),
    )
    return jax.shard_map(
        shards,
        mesh=mesh,
        in_specs=placed,
        out_specs=(P(), P(None, "dev", None), P(None, "dev", None), P(None, "dev", None)),
        check_vma=False,
    )
```

```python
import jax
import jax.numpy as jnp
from jax import lax
from jax.experimental import pallas as pl
from jax.experimental.pallas import tpu as pltpu
from jax.sharding import PartitionSpec as P

STEP = 10
MESH = pl.DeviceIdType.MESH
BF16, F32 = jnp.bfloat16, jnp.float32
BATCH, CHANS = 4, 128
ROWS = 72
SLAB = 80


def adamw(grad, master_part, first_part, second_part):
    first_new = 0.9 * first_part + 0.1 * grad
    second_new = 0.95 * second_part + 0.05 * grad * grad
    corr_one = 1.0 - 0.9**STEP
    corr_two = 1.0 - 0.95**STEP
    update = first_new / corr_one / (jnp.sqrt(second_new / corr_two) + 1e-08)
    master_new = master_part - 0.001 * (update + 0.1 * master_part)
    return (master_new, first_new, second_new)


def shift_store(src_ref, dst_ref, image):
    edge = jnp.zeros((16, 1, CHANS), BF16)
    for odd in range(2):
        rows = src_ref[image, :, odd]
        place = pl.ds(odd, 16)
        dst_ref[image, 1 - odd, place, :, 0:128] = jnp.concatenate([edge, rows[:, :31]], axis=1)
        dst_ref[image, 1 - odd, place, :, 128:256] = rows
        dst_ref[image, 1 - odd, place, :, 256:384] = jnp.concatenate([rows[:, 1:], edge], axis=1)
    zero = jnp.zeros((32, 3 * CHANS), BF16)
    dst_ref[image, 0, 0] = zero
    dst_ref[image, 1, 16] = zero


def four_rows(ref, image):
    return jnp.concatenate(
        [ref[image, k % 2, pl.ds(k // 2, 16)].reshape(512, 3 * CHANS) for k in range(4)], axis=1
    )


def pair_forward(w_ref, out_ref):
    zero = jnp.zeros((CHANS, CHANS), BF16)
    for k in range(4):
        for tj in range(3):
            rows = pl.ds((k * 3 + tj) * CHANS, CHANS)
            for odd in range(2):
                tap = (k - odd) * 3 + tj
                block = w_ref[0, tap * CHANS : (tap + 1) * CHANS, :] if 0 <= k - odd <= 2 else zero
                out_ref[rows, odd * CHANS : (odd + 1) * CHANS] = block


def pair_backward(w_ref, out_ref):
    zero = jnp.zeros((CHANS, CHANS), BF16)
    for k in range(4):
        for tj in range(3):
            rows = pl.ds((k * 3 + tj) * CHANS, CHANS)
            for odd in range(2):
                tap = (odd - k + 2) * 3 + 2 - tj
                block = w_ref[1, tap * CHANS : (tap + 1) * CHANS, :].T if 0 <= k - odd <= 2 else zero
                out_ref[rows, odd * CHANS : (odd + 1) * CHANS] = block


def put_turned(ref, value, image):
    turned = value.astype(BF16).T
    for odd in range(2):
        start = odd * BATCH * 512 + image * 512
        ref[:, start : start + 512] = turned[odd * CHANS : (odd + 1) * CHANS]


def outer_sum(turned, ref, first, last):
    out = None
    for odd in range(2):
        for image in range(BATCH):
            near = jnp.concatenate(
                [ref[image, (k + odd) % 2, pl.ds((k + odd) // 2, 16)].reshape(512, 3 * CHANS) for k in range(3)], axis=1
            )
            start = odd * BATCH * 512 + image * 512
            part = jnp.dot(
                turned[:, start : start + 512], near[:, first * CHANS : last * CHANS], preferred_element_type=F32
            )
            out = part if out is None else out + part
    return out


def step_kernel(x_hbm, c_hbm, w_hbm, master_hbm, first_hbm, second_hbm,
                gathered_out, totals_out,
                x_ref, c_ref, w_ref, state_ref,
                x3, c3, forward_w, backward_w, act, slope, dpre, grads,
                pair_recv, xy_send, xy_recv, z_parts, held, totals, gathered,
                load_s, pair_ss, pair_rs, xy_ss, xy_rs, z_ss, z_rs, held_ss, held_rs, t_ss, t_rs, tot_ss, tot_rs,
                gat_ss, gat_rs, fwd_ss, fwd_rs, put_s):
    grp = lax.axis_index("grp")
    dev = lax.axis_index("dev")
    core = lax.rem(grp, 2)
    y = lax.rem(grp, 8) // 2
    z_hi = grp // 8
    x = lax.rem(dev, 4)
    z_lo = dev // 4
    z = z_hi * 4 + z_lo
    partner = (grp + 1 - 2 * core, dev)

    def xy_peer(kx, ky, at=core):
        return (z_hi * 8 + lax.rem(y + ky, 4) * 2 + at, z_lo * 4 + lax.rem(x + kx, 4))

    def z_peer(kz):
        other = lax.rem(z + kz, 8)
        return (other // 4 * 8 + y * 2 + core, lax.rem(other, 4) * 4 + x)

    def held_peer(k):
        return (grp, lax.rem(z_lo + k, 4) * 4 + x)

    def remote(src, dst, ss, rs, target):
        return pltpu.make_async_remote_copy(
            src_ref=src, dst_ref=dst, send_sem=ss, recv_sem=rs, device_id=target, device_id_type=MESH
        )

    loads = [
        pltpu.make_async_copy(src, dst, load_s.at[k])
        for k, (src, dst) in enumerate(
            [(x_hbm, x_ref), (w_hbm, w_ref), (c_hbm, c_ref)]
            + [(ref.at[layer], state_ref.at[layer, k])
               for k, ref in enumerate((master_hbm, first_hbm, second_hbm)) for layer in range(2)]
        )
    ]
    for copy in loads:
        copy.start()
    xy_order = [(kx, ky) for kx in (2, 1, 3, 0) for ky in (2, 1, 3, 0) if kx or ky]
    xy_steps = [(kx, ky) for kx in (0, 1, 3, 2) for ky in (0, 1, 3, 2) if kx or ky]
    z_order = (4, 3, 5, 2, 6, 1, 7)
    peers = [partner] + [xy_peer(*k, at) for k in xy_steps for at in range(2)] + [z_peer(k) for k in z_order]
    barrier = pltpu.get_barrier_semaphore()
    for peer in peers:
        pl.semaphore_signal(barrier, inc=1, device_id=peer, device_id_type=MESH)

    def place(kx, ky):
        return lax.rem(y + ky, 4) * 4 + lax.rem(x + kx, 4)

    def shard_rows(shard):
        start = shard * ROWS
        return pl.ds(start if isinstance(start, int) else pl.multiple_of(start, 8), ROWS)

    own = y * 4 + x

    def xy_copy(layer, shard):
        other = 1 - core
        kx, ky = lax.rem(shard % 4 + 4 - x, 4), lax.rem(shard // 4 + 4 - y, 4)
        slot = other * 16 + kx * 4 + ky
        target = (z_hi * 8 + shard // 4 * 2 + layer, z_lo * 4 + shard % 4)
        copy = remote(xy_send.at[layer, shard], xy_recv.at[slot], xy_ss.at[layer, shard], xy_rs.at[slot], target)
        return copy, slot > 0

    def pair_copy(shard):
        return remote(grads.at[0, shard_rows(shard), :], pair_recv.at[shard], pair_ss.at[shard], pair_rs.at[shard], partner)

    def send_pair(first, last):
        for shard in range(first, last):
            pair_copy(shard).start()

    def pair_xy_copy(kx, ky):
        slot, shard = kx * 4 + ky, place(kx, ky)
        target = xy_peer(kx, ky)
        return remote(xy_send.at[0, shard], xy_recv.at[slot], xy_ss.at[0, shard], xy_rs.at[slot], target)

    def sum_pair():
        for kx, ky in xy_order + [(0, 0)]:
            shard = place(kx, ky)
            pair_copy(shard).wait_recv()
            both = grads[0, shard_rows(shard), :] + pair_recv[shard]
            if kx or ky:
                xy_send[0, shard, 0:ROWS, :] = both.astype(BF16)
                pair_xy_copy(kx, ky).start()
            else:
                grads[0, shard_rows(shard), :] = both

    def send_parts(layer, first, last):
        for shard in range(first, last):
            copy, remote_one = xy_copy(layer, shard)
            pl.when(remote_one)(copy.start)

    def round_parts(layer, first, last):
        for shard in range(first, last):
            xy_send[layer, shard, 0:ROWS, :] = grads[layer, shard_rows(shard), :].astype(BF16)

    for copy in loads:
        copy.wait()
    pair_forward(w_ref, forward_w)
    shift_store(x_ref, x3, 0)
    for image in range(BATCH):
        pre = jnp.dot(four_rows(x3, image), forward_w[...], preferred_element_type=F32)
        sig = 1.0 / (1.0 + jnp.exp(-pre))
        value = pre * sig
        put_turned(act, value, image)
        slope[image] = sig + value * (1.0 - sig)
        if image < BATCH - 1:
            shift_store(x_ref, x3, image + 1)
        shift_store(c_ref, c3, image)

    pair_backward(w_ref, backward_w)
    out = outer_sum(act, c3, 0, 9)
    for block in range(9):
        tap = 8 - block
        grads[1, tap * CHANS : (tap + 1) * CHANS, :] = out[:, block * CHANS : (block + 1) * CHANS]
    round_parts(1, 0, 16)

    pl.semaphore_wait(barrier, len(peers))
    send_parts(1, 0, 16)

    def held_copy(k, source_ref):
        return remote(source_ref, held, held_ss.at[k], held_rs, held_peer(k))

    @pl.when(z_lo == y)
    def _():
        held[...] = state_ref[core]
        for k in range(1, 4):
            held_copy(k, held).start()

    for image in range(BATCH):
        back = jnp.dot(four_rows(c3, image), backward_w[...], preferred_element_type=F32)
        put_turned(dpre, back * slope[image], image)

    def first_layer(first, last):
        out = outer_sum(dpre, x3, first, last)
        for tap in range(first, last):
            block = out[:, (tap - first) * CHANS : (tap + 1 - first) * CHANS]
            grads[0, tap * CHANS : (tap + 1) * CHANS, :] = block.T

    first_layer(0, 5)

    @pl.when(core == 1)
    def _():
        send_pair(0, 8)

    first_layer(5, 9)

    @pl.when(core == 1)
    def _():
        send_pair(8, 16)

    @pl.when(core == 0)
    def _():
        sum_pair()

    def sum_parts(layer, others):
        acc = grads[layer, shard_rows(own), :]
        for kx, ky in [(0, 0)] + xy_steps:
            for other in range(others):
                slot = other * 16 + kx * 4 + ky
                if slot:
                    ref = xy_recv.at[slot]
                    remote(ref, ref, xy_ss.at[0, 0], xy_rs.at[slot], partner).wait_recv()
                    acc = acc + xy_recv[slot, 0:ROWS, :].astype(F32)
        z_parts[z, 0:ROWS, :] = acc.astype(BF16)

    @pl.when(core == 0)
    def _():
        sum_parts(0, 1)

    @pl.when(core == 1)
    def _():
        sum_parts(1, 2)

    def z_copy(kz, place):
        return remote(z_parts.at[place], z_parts.at[place], z_ss.at[kz], z_rs.at[kz], z_peer(kz))

    for kz in z_order:
        z_copy(kz, z).start()
    for kz in z_order[::-1]:
        z_copy(kz, lax.rem(z + 8 - kz, 8)).wait_recv()
    z_part = [z_parts[k, 0:ROWS, :].astype(F32) for k in range(8)]
    halves = [(z_part[k] + z_part[k + 1]) + (z_part[k + 2] + z_part[k + 3]) for k in (0, 4)]
    whole = halves[0] + halves[1]

    @pl.when(z_lo != y)
    def _():
        held_copy(1, held).wait_recv()

    slab = adamw(whole, held[0], held[1], held[2])[0].astype(BF16)
    gathered[y * 4 + x, 0:ROWS, :] = slab

    def gat_copy(kx, ky, slot):
        ref = gathered.at[slot]
        return remote(ref, ref, gat_ss.at[kx * 4 + ky], gat_rs.at[kx * 4 + ky], xy_peer(kx, ky))

    def source(kx, ky):
        return place(4 - kx, 4 - ky)

    def fwd_copy(layer, kx, ky):
        slot = source(kx, ky)
        k = kx * 4 + ky
        return remote(gathered.at[slot], gathered_out.at[layer, slot], fwd_ss.at[k], fwd_rs.at[k], partner)

    for kx, ky in xy_order:
        gat_copy(kx, ky, source(0, 0)).start()
    fwd_copy(core, 0, 0).start()

    def t_copy(ky):
        return remote(totals, totals, t_ss.at[ky], t_rs, xy_peer(0, ky))

    @pl.when(z_lo == y)
    def _():
        totals[...] = whole
        for ky in (2, 1, 3):
            t_copy(ky).start()

    def forward(steps):
        for kx, ky in steps:
            gat_copy(kx, ky, source(kx, ky)).wait_recv()
            fwd_copy(core, kx, ky).start()

    forward(xy_steps[:3])

    @pl.when(z_lo != y)
    def _():
        t_copy(1).wait_recv()

    tot = remote(totals, totals_out.at[core], tot_ss, tot_rs, partner)
    tot.start()
    puts = [
        pltpu.make_async_copy(totals, totals_out.at[core], put_s.at[0]),
        pltpu.make_async_copy(gathered, gathered_out.at[core], put_s.at[1]),
    ]
    puts[0].start()
    forward(xy_steps[3:])
    puts[1].start()
    remote(totals, totals_out.at[1 - core], tot_ss, tot_rs, partner).wait_recv()
    for kx, ky in xy_steps + [(0, 0)]:
        fwd_copy(1 - core, kx, ky).wait_recv()
    for k in range(16):
        fwd_copy(core, k // 4, k % 4).wait_send()
        copy, remote_one = xy_copy(1, k)
        pl.when(remote_one)(copy.wait_send)
    for kx, ky in xy_steps:
        gat_copy(kx, ky, source(0, 0)).wait_send()

    @pl.when(core == 0)
    def _():
        for kx, ky in xy_steps:
            pair_xy_copy(kx, ky).wait_send()

    @pl.when(core == 1)
    def _():
        for k in range(16):
            pair_copy(k).wait_send()

    for kz in z_order:
        z_copy(kz, z).wait_send()

    @pl.when(z_lo == y)
    def _():
        for k in range(1, 4):
            held_copy(k, held).wait_send()
            t_copy(k).wait_send()

    tot.wait_send()
    for copy in puts:
        copy.wait()


def finish_kernel(gathered_hbm, totals_hbm, master_hbm, first_hbm, second_hbm,
                  weights_hbm, master_out, first_out, second_out,
                  gathered, weights, held, new, load_s, state_s, store_s, new_s):
    loads, stores = [], []
    for k in range(4):
        layer, part = k // 2, pl.ds(k % 2 * 8, 8)
        loads.append(pltpu.make_async_copy(gathered_hbm.at[layer, part], gathered.at[layer, part], load_s.at[k]))
        rows = pl.ds(k % 2 * 8 * ROWS, 8 * ROWS)
        stores.append(pltpu.make_async_copy(weights.at[layer, rows], weights_hbm.at[layer, rows], store_s.at[k]))
    states = [
        pltpu.make_async_copy(src, held.at[k], state_s.at[k])
        for k, src in enumerate((totals_hbm, master_hbm, first_hbm, second_hbm))
    ]
    for copy in states + loads:
        copy.start()
    for copy in states:
        copy.wait()
    for k, value in enumerate(adamw(held[0], held[1], held[2], held[3])):
        new[k] = value
        store = pltpu.make_async_copy(new.at[k], (master_out, first_out, second_out)[k], new_s.at[k])
        store.start()
        stores.append(store)
    for k in range(4):
        loads[k].wait()
        for two in range(k % 2 * 4, k % 2 * 4 + 4):
            both = [gathered[k // 2, 2 * two + odd, 0:ROWS, :].astype(F32) for odd in range(2)]
            weights[k // 2, 2 * ROWS * two : 2 * ROWS * (two + 1), :] = jnp.concatenate(both, axis=0).astype(BF16)
        stores[k].start()
    for copy in stores:
        copy.wait()


def shards(inputs, cotangent, weights, master, first_moment, second_moment):
    far = pl.BlockSpec(memory_space=pltpu.HBM)
    dma = pltpu.SemaphoreType.DMA
    vmem = pltpu.VMEM
    by_pairs = (BATCH, 16, 2, 32, CHANS)
    gathered, totals = pl.pallas_call(
        step_kernel,
        out_shape=(
            jax.ShapeDtypeStruct((2, 16, SLAB, CHANS), BF16),
            jax.ShapeDtypeStruct((2, ROWS, CHANS), F32),
        ),
        in_specs=[far] * 6,
        out_specs=(far, far),
        scratch_shapes=[
            vmem(by_pairs, BF16),
            vmem(by_pairs, BF16),
            vmem(weights.shape, BF16),
            vmem((2, 3, ROWS, CHANS), F32),
            vmem((BATCH, 2, 17, 32, 3 * CHANS), BF16),
            vmem((BATCH, 2, 17, 32, 3 * CHANS), BF16),
            vmem((12 * CHANS, 2 * CHANS), BF16),
            vmem((12 * CHANS, 2 * CHANS), BF16),
            vmem((CHANS, BATCH * 1024), BF16),
            vmem((BATCH, 512, 2 * CHANS), F32),
            vmem((CHANS, BATCH * 1024), BF16),
            vmem((2, 9 * CHANS, CHANS), F32),
            vmem((16, ROWS, CHANS), F32),
            vmem((2, 16, SLAB, CHANS), BF16),
            vmem((32, SLAB, CHANS), BF16),
            vmem((8, SLAB, CHANS), BF16),
            vmem((3, ROWS, CHANS), F32),
            vmem((ROWS, CHANS), F32),
            vmem((16, SLAB, CHANS), BF16),
            dma((9,)),
            dma((16,)), dma((16,)), dma((2, 16)), dma((32,)), dma((8,)), dma((8,)), dma((4,)), dma,
            dma((4,)), dma, dma, dma, dma((16,)), dma((16,)), dma((16,)), dma((16,)), dma((2,)),
        ],
        compiler_params=pltpu.CompilerParams(collective_id=0, has_side_effects=True, vmem_limit_bytes=60 * 2**20),
        name="step",
    )(inputs.reshape(by_pairs), cotangent.reshape(by_pairs), weights, master, first_moment, second_moment)
    state = jax.ShapeDtypeStruct(master.shape, F32)
    return pl.pallas_call(
        finish_kernel,
        out_shape=(jax.ShapeDtypeStruct(weights.shape, BF16), state, state, state),
        in_specs=[far] * 5,
        out_specs=(far,) * 4,
        scratch_shapes=[
            vmem((2, 16, SLAB, CHANS), BF16),
            vmem(weights.shape, BF16),
            vmem((4,) + master.shape, F32),
            vmem((3,) + master.shape, F32),
            dma((4,)), dma((4,)), dma((4,)), dma((3,)),
        ],
        compiler_params=pltpu.CompilerParams(vmem_limit_bytes=60 * 2**20),
        name="finish",
    )(gathered, totals, master, first_moment, second_moment)


def solution(mesh):
    placed = (
        P(("grp", "dev"), None, None, None),
        P(("grp", "dev"), None, None, None),
        P(),
        P(None, "dev", None),
        P(None, "dev", None),
        P(None, "dev", None),
    )
    return jax.shard_map(
        shards,
        mesh=mesh,
        in_specs=placed,
        out_specs=(P(), P(None, "dev", None), P(None, "dev", None), P(None, "dev", None)),
        check_vma=False,
    )
```

```python
import jax
import jax.numpy as jnp
from jax import lax
from jax.experimental import pallas as pl
from jax.experimental.pallas import tpu as pltpu
from jax.sharding import PartitionSpec as P

STEP = 10
MESH = pl.DeviceIdType.MESH
BF16, F32 = jnp.bfloat16, jnp.float32
BATCH, CHANS = 4, 128
ROWS = 72
SLAB = 80


def adamw(grad, master_part, first_part, second_part):
    first_new = 0.9 * first_part + 0.1 * grad
    second_new = 0.95 * second_part + 0.05 * grad * grad
    corr_one = 1.0 - 0.9**STEP
    corr_two = 1.0 - 0.95**STEP
    update = first_new / corr_one / (jnp.sqrt(second_new / corr_two) + 1e-08)
    master_new = master_part - 0.001 * (update + 0.1 * master_part)
    return (master_new, first_new, second_new)


def shift_store(src_ref, dst_ref, image):
    edge = jnp.zeros((16, 1, CHANS), BF16)
    for odd in range(2):
        rows = src_ref[image, :, odd]
        place = pl.ds(odd, 16)
        dst_ref[image, 1 - odd, place, :, 0:128] = jnp.concatenate([edge, rows[:, :31]], axis=1)
        dst_ref[image, 1 - odd, place, :, 128:256] = rows
        dst_ref[image, 1 - odd, place, :, 256:384] = jnp.concatenate([rows[:, 1:], edge], axis=1)
    zero = jnp.zeros((32, 3 * CHANS), BF16)
    dst_ref[image, 0, 0] = zero
    dst_ref[image, 1, 16] = zero


def four_rows(ref, image):
    return jnp.concatenate(
        [ref[image, k % 2, pl.ds(k // 2, 16)].reshape(512, 3 * CHANS) for k in range(4)], axis=1
    )


def pair_forward(w_ref, out_ref):
    zero = jnp.zeros((CHANS, CHANS), BF16)
    for k in range(4):
        for tj in range(3):
            rows = pl.ds((k * 3 + tj) * CHANS, CHANS)
            for odd in range(2):
                tap = (k - odd) * 3 + tj
                block = w_ref[0, tap * CHANS : (tap + 1) * CHANS, :] if 0 <= k - odd <= 2 else zero
                out_ref[rows, odd * CHANS : (odd + 1) * CHANS] = block


def pair_backward(w_ref, out_ref):
    zero = jnp.zeros((CHANS, CHANS), BF16)
    for k in range(4):
        for tj in range(3):
            rows = pl.ds((k * 3 + tj) * CHANS, CHANS)
            for odd in range(2):
                tap = (odd - k + 2) * 3 + 2 - tj
                block = w_ref[1, tap * CHANS : (tap + 1) * CHANS, :].T if 0 <= k - odd <= 2 else zero
                out_ref[rows, odd * CHANS : (odd + 1) * CHANS] = block


def put_turned(ref, value, image):
    turned = value.astype(BF16).T
    for odd in range(2):
        start = odd * BATCH * 512 + image * 512
        ref[:, start : start + 512] = turned[odd * CHANS : (odd + 1) * CHANS]


def outer_sum(turned, ref, first, last):
    out = None
    for odd in range(2):
        for image in range(BATCH):
            near = jnp.concatenate(
                [ref[image, (k + odd) % 2, pl.ds((k + odd) // 2, 16)].reshape(512, 3 * CHANS) for k in range(3)], axis=1
            )
            start = odd * BATCH * 512 + image * 512
            part = jnp.dot(
                turned[:, start : start + 512], near[:, first * CHANS : last * CHANS], preferred_element_type=F32
            )
            out = part if out is None else out + part
    return out


def step_kernel(x_hbm, c_hbm, w_hbm, master_hbm, first_hbm, second_hbm,
                gathered_out, totals_out,
                x_ref, c_ref, w_ref, state_ref,
                x3, c3, forward_w, backward_w, act, slope, dpre, grads,
                pair_recv, xy_send, xy_recv, z_parts, held, totals, gathered,
                load_s, pair_ss, pair_rs, xy_ss, xy_rs, z_ss, z_rs, held_ss, held_rs, t_ss, t_rs, tot_ss, tot_rs,
                gat_ss, gat_rs, fwd_ss, fwd_rs, put_s):
    grp = lax.axis_index("grp")
    dev = lax.axis_index("dev")
    core = lax.rem(grp, 2)
    y = lax.rem(grp, 8) // 2
    z_hi = grp // 8
    x = lax.rem(dev, 4)
    z_lo = dev // 4
    z = z_hi * 4 + z_lo
    partner = (grp + 1 - 2 * core, dev)

    def xy_peer(kx, ky, at=core):
        return (z_hi * 8 + lax.rem(y + ky, 4) * 2 + at, z_lo * 4 + lax.rem(x + kx, 4))

    def z_peer(kz):
        other = lax.rem(z + kz, 8)
        return (other // 4 * 8 + y * 2 + core, lax.rem(other, 4) * 4 + x)

    def held_peer(k):
        return (grp, lax.rem(z_lo + k, 4) * 4 + x)

    def remote(src, dst, ss, rs, target):
        return pltpu.make_async_remote_copy(
            src_ref=src, dst_ref=dst, send_sem=ss, recv_sem=rs, device_id=target, device_id_type=MESH
        )

    loads = [
        pltpu.make_async_copy(src, dst, load_s.at[k])
        for k, (src, dst) in enumerate(
            [(w_hbm.at[0], w_ref.at[0]), (x_hbm, x_ref), (c_hbm, c_ref), (w_hbm.at[1], w_ref.at[1])]
            + [(ref.at[layer], state_ref.at[layer, k])
               for k, ref in enumerate((master_hbm, first_hbm, second_hbm)) for layer in range(2)]
        )
    ]
    for copy in loads[:2]:
        copy.start()
    xy_order = [(kx, ky) for kx in (2, 1, 3, 0) for ky in (2, 1, 3, 0) if kx or ky]
    xy_steps = [(kx, ky) for kx in (0, 1, 3, 2) for ky in (0, 1, 3, 2) if kx or ky]
    z_order = (4, 3, 5, 2, 6, 1, 7)
    peers = [partner] + [xy_peer(*k, at) for k in xy_steps for at in range(2)] + [z_peer(k) for k in z_order]
    barrier = pltpu.get_barrier_semaphore()
    for peer in peers:
        pl.semaphore_signal(barrier, inc=1, device_id=peer, device_id_type=MESH)

    def place(kx, ky):
        return lax.rem(y + ky, 4) * 4 + lax.rem(x + kx, 4)

    def shard_rows(shard):
        start = shard * ROWS
        return pl.ds(start if isinstance(start, int) else pl.multiple_of(start, 8), ROWS)

    own = y * 4 + x

    def part_copy(kx, ky):
        shard, slot = place(kx, ky), (1 - core) * 16 + kx * 4 + ky
        return remote(xy_send.at[1, shard], xy_recv.at[slot], xy_ss.at[1, shard], xy_rs.at[slot], xy_peer(kx, ky, 1))

    def pair_copy(shard):
        return remote(grads.at[0, shard_rows(shard), :], pair_recv.at[shard], pair_ss.at[shard], pair_rs.at[shard], partner)

    def send_pair(first, last):
        for shard in range(first, last):
            pair_copy(shard).start()

    def pair_xy_copy(kx, ky):
        slot, shard = kx * 4 + ky, place(kx, ky)
        target = xy_peer(kx, ky)
        return remote(xy_send.at[0, shard], xy_recv.at[slot], xy_ss.at[0, shard], xy_rs.at[slot], target)

    def sum_pair():
        for kx, ky in xy_order + [(0, 0)]:
            shard = place(kx, ky)
            pair_copy(shard).wait_recv()
            both = grads[0, shard_rows(shard), :] + pair_recv[shard]
            if kx or ky:
                xy_send[0, shard, 0:ROWS, :] = both.astype(BF16)
                pair_xy_copy(kx, ky).start()
            else:
                grads[0, shard_rows(shard), :] = both

    def send_parts():
        for shard in range(16):
            xy_send[1, shard, 0:ROWS, :] = grads[1, shard_rows(shard), :].astype(BF16)
        for kx, ky in xy_order:
            part_copy(kx, ky).start()
        pl.when(core == 0)(part_copy(0, 0).start)

    for copy in loads[:2]:
        copy.wait()
    for copy in loads[2:]:
        copy.start()
    pair_forward(w_ref, forward_w)
    shift_store(x_ref, x3, 0)
    for image in range(BATCH):
        pre = jnp.dot(four_rows(x3, image), forward_w[...], preferred_element_type=F32)
        sig = 1.0 / (1.0 + jnp.exp(-pre))
        value = pre * sig
        put_turned(act, value, image)
        slope[image] = sig + value * (1.0 - sig)
        if image < BATCH - 1:
            shift_store(x_ref, x3, image + 1)
    for copy in loads[2:]:
        copy.wait()
    for image in range(BATCH):
        shift_store(c_ref, c3, image)

    pair_backward(w_ref, backward_w)
    out = outer_sum(act, c3, 0, 9)
    for block in range(9):
        tap = 8 - block
        grads[1, tap * CHANS : (tap + 1) * CHANS, :] = out[:, block * CHANS : (block + 1) * CHANS]

    pl.semaphore_wait(barrier, len(peers))
    send_parts()

    def held_copy(k, source_ref):
        return remote(source_ref, held, held_ss.at[k], held_rs, held_peer(k))

    @pl.when(z_lo == y)
    def _():
        held[...] = state_ref[core]
        for k in range(1, 4):
            held_copy(k, held).start()

    for image in range(BATCH):
        back = jnp.dot(four_rows(c3, image), backward_w[...], preferred_element_type=F32)
        put_turned(dpre, back * slope[image], image)

    def first_layer(first, last):
        out = outer_sum(dpre, x3, first, last)
        for tap in range(first, last):
            block = out[:, (tap - first) * CHANS : (tap + 1 - first) * CHANS]
            grads[0, tap * CHANS : (tap + 1) * CHANS, :] = block.T

    first_layer(0, 5)

    @pl.when(core == 1)
    def _():
        send_pair(0, 8)

    first_layer(5, 9)

    @pl.when(core == 1)
    def _():
        send_pair(8, 16)

    @pl.when(core == 0)
    def _():
        sum_pair()

    def sum_parts(layer, others):
        acc = grads[layer, shard_rows(own), :]
        for kx, ky in [(0, 0)] + xy_steps:
            for other in range(others):
                slot = other * 16 + kx * 4 + ky
                if slot:
                    ref = xy_recv.at[slot]
                    remote(ref, ref, xy_ss.at[0, 0], xy_rs.at[slot], partner).wait_recv()
                    acc = acc + xy_recv[slot, 0:ROWS, :].astype(F32)
        z_parts[z, 0:ROWS, :] = acc.astype(BF16)

    @pl.when(core == 0)
    def _():
        sum_parts(0, 1)

    @pl.when(core == 1)
    def _():
        sum_parts(1, 2)

    def z_copy(kz, place):
        return remote(z_parts.at[place], z_parts.at[place], z_ss.at[kz], z_rs.at[kz], z_peer(kz))

    for kz in z_order:
        z_copy(kz, z).start()
    for kz in z_order[::-1]:
        z_copy(kz, lax.rem(z + 8 - kz, 8)).wait_recv()
    z_part = [z_parts[k, 0:ROWS, :].astype(F32) for k in range(8)]
    halves = [(z_part[k] + z_part[k + 1]) + (z_part[k + 2] + z_part[k + 3]) for k in (0, 4)]
    whole = halves[0] + halves[1]

    @pl.when(z_lo != y)
    def _():
        held_copy(1, held).wait_recv()

    slab = adamw(whole, held[0], held[1], held[2])[0].astype(BF16)
    gathered[y * 4 + x, 0:ROWS, :] = slab

    def gat_copy(kx, ky, slot):
        ref = gathered.at[slot]
        return remote(ref, ref, gat_ss.at[kx * 4 + ky], gat_rs.at[kx * 4 + ky], xy_peer(kx, ky))

    def source(kx, ky):
        return place(4 - kx, 4 - ky)

    def fwd_copy(layer, kx, ky):
        slot = source(kx, ky)
        k = kx * 4 + ky
        return remote(gathered.at[slot], gathered_out.at[layer, slot], fwd_ss.at[k], fwd_rs.at[k], partner)

    for kx, ky in xy_order:
        gat_copy(kx, ky, source(0, 0)).start()
    fwd_copy(core, 0, 0).start()

    def t_copy(ky):
        return remote(totals, totals, t_ss.at[ky], t_rs, xy_peer(0, ky))

    @pl.when(z_lo == y)
    def _():
        totals[...] = whole
        for ky in (2, 1, 3):
            t_copy(ky).start()

    @pl.when(core == 0)
    def _():
        part_copy(0, 0).wait_send()
        for kx, ky in xy_steps:
            pair_xy_copy(kx, ky).wait_send()

    @pl.when(core == 1)
    def _():
        for k in range(16):
            pair_copy(k).wait_send()

    for kx, ky in xy_steps:
        part_copy(kx, ky).wait_send()
    for kz in z_order:
        z_copy(kz, z).wait_send()

    @pl.when(z_lo == y)
    def _():
        for k in range(1, 4):
            held_copy(k, held).wait_send()

    def forward(steps):
        for kx, ky in steps:
            gat_copy(kx, ky, source(kx, ky)).wait_recv()
            fwd_copy(core, kx, ky).start()

    forward(xy_steps[:3])

    @pl.when(z_lo != y)
    def _():
        t_copy(1).wait_recv()

    tot = remote(totals, totals_out.at[core], tot_ss, tot_rs, partner)
    tot.start()
    puts = [
        pltpu.make_async_copy(totals, totals_out.at[core], put_s.at[0]),
        pltpu.make_async_copy(gathered, gathered_out.at[core], put_s.at[1]),
    ]
    puts[0].start()
    forward(xy_steps[3:])
    puts[1].start()
    for kx, ky in xy_steps:
        gat_copy(kx, ky, source(0, 0)).wait_send()

    @pl.when(z_lo == y)
    def _():
        for k in range(1, 4):
            t_copy(k).wait_send()

    remote(totals, totals_out.at[1 - core], tot_ss, tot_rs, partner).wait_recv()
    for kx, ky in xy_steps + [(0, 0)]:
        fwd_copy(1 - core, kx, ky).wait_recv()
    for k in range(16):
        fwd_copy(core, k // 4, k % 4).wait_send()
    tot.wait_send()
    for copy in puts:
        copy.wait()


def finish_kernel(gathered_hbm, totals_hbm, master_hbm, first_hbm, second_hbm,
                  weights_hbm, master_out, first_out, second_out,
                  gathered, weights, held, new, load_s, state_s, store_s, new_s):
    loads, stores = [], []
    for k in range(4):
        layer, part = k // 2, pl.ds(k % 2 * 8, 8)
        loads.append(pltpu.make_async_copy(gathered_hbm.at[layer, part], gathered.at[layer, part], load_s.at[k]))
        rows = pl.ds(k % 2 * 8 * ROWS, 8 * ROWS)
        stores.append(pltpu.make_async_copy(weights.at[layer, rows], weights_hbm.at[layer, rows], store_s.at[k]))
    states = [
        pltpu.make_async_copy(src, held.at[k], state_s.at[k])
        for k, src in enumerate((totals_hbm, master_hbm, first_hbm, second_hbm))
    ]
    for copy in states + loads:
        copy.start()
    for copy in states:
        copy.wait()
    for k, value in enumerate(adamw(held[0], held[1], held[2], held[3])):
        new[k] = value
        store = pltpu.make_async_copy(new.at[k], (master_out, first_out, second_out)[k], new_s.at[k])
        store.start()
        stores.append(store)
    for k in range(4):
        loads[k].wait()
        for two in range(k % 2 * 4, k % 2 * 4 + 4):
            both = [gathered[k // 2, 2 * two + odd, 0:ROWS, :].astype(F32) for odd in range(2)]
            weights[k // 2, 2 * ROWS * two : 2 * ROWS * (two + 1), :] = jnp.concatenate(both, axis=0).astype(BF16)
        stores[k].start()
    for copy in stores:
        copy.wait()


def shards(inputs, cotangent, weights, master, first_moment, second_moment):
    far = pl.BlockSpec(memory_space=pltpu.HBM)
    dma = pltpu.SemaphoreType.DMA
    vmem = pltpu.VMEM
    by_pairs = (BATCH, 16, 2, 32, CHANS)
    gathered, totals = pl.pallas_call(
        step_kernel,
        out_shape=(
            jax.ShapeDtypeStruct((2, 16, SLAB, CHANS), BF16),
            jax.ShapeDtypeStruct((2, ROWS, CHANS), F32),
        ),
        in_specs=[far] * 6,
        out_specs=(far, far),
        scratch_shapes=[
            vmem(by_pairs, BF16),
            vmem(by_pairs, BF16),
            vmem(weights.shape, BF16),
            vmem((2, 3, ROWS, CHANS), F32),
            vmem((BATCH, 2, 17, 32, 3 * CHANS), BF16),
            vmem((BATCH, 2, 17, 32, 3 * CHANS), BF16),
            vmem((12 * CHANS, 2 * CHANS), BF16),
            vmem((12 * CHANS, 2 * CHANS), BF16),
            vmem((CHANS, BATCH * 1024), BF16),
            vmem((BATCH, 512, 2 * CHANS), F32),
            vmem((CHANS, BATCH * 1024), BF16),
            vmem((2, 9 * CHANS, CHANS), F32),
            vmem((16, ROWS, CHANS), F32),
            vmem((2, 16, SLAB, CHANS), BF16),
            vmem((32, SLAB, CHANS), BF16),
            vmem((8, SLAB, CHANS), BF16),
            vmem((3, ROWS, CHANS), F32),
            vmem((ROWS, CHANS), F32),
            vmem((16, SLAB, CHANS), BF16),
            dma((10,)),
            dma((16,)), dma((16,)), dma((2, 16)), dma((32,)), dma((8,)), dma((8,)), dma((4,)), dma,
            dma((4,)), dma, dma, dma, dma((16,)), dma((16,)), dma((16,)), dma((16,)), dma((2,)),
        ],
        compiler_params=pltpu.CompilerParams(collective_id=0, has_side_effects=True, vmem_limit_bytes=60 * 2**20),
        name="step",
    )(inputs.reshape(by_pairs), cotangent.reshape(by_pairs), weights, master, first_moment, second_moment)
    state = jax.ShapeDtypeStruct(master.shape, F32)
    return pl.pallas_call(
        finish_kernel,
        out_shape=(jax.ShapeDtypeStruct(weights.shape, BF16), state, state, state),
        in_specs=[far] * 5,
        out_specs=(far,) * 4,
        scratch_shapes=[
            vmem((2, 16, SLAB, CHANS), BF16),
            vmem(weights.shape, BF16),
            vmem((4,) + master.shape, F32),
            vmem((3,) + master.shape, F32),
            dma((4,)), dma((4,)), dma((4,)), dma((3,)),
        ],
        compiler_params=pltpu.CompilerParams(vmem_limit_bytes=60 * 2**20),
        name="finish",
    )(gathered, totals, master, first_moment, second_moment)


def solution(mesh):
    placed = (
        P(("grp", "dev"), None, None, None),
        P(("grp", "dev"), None, None, None),
        P(),
        P(None, "dev", None),
        P(None, "dev", None),
        P(None, "dev", None),
    )
    return jax.shard_map(
        shards,
        mesh=mesh,
        in_specs=placed,
        out_specs=(P(), P(None, "dev", None), P(None, "dev", None), P(None, "dev", None)),
        check_vma=False,
    )
```

```python
import jax
import jax.numpy as jnp
from jax import lax
from jax.experimental import pallas as pl
from jax.experimental.pallas import tpu as pltpu
from jax.sharding import PartitionSpec as P

STEP = 10
MESH = pl.DeviceIdType.MESH
BF16, F32 = jnp.bfloat16, jnp.float32
BATCH, CHANS = 4, 128
ROWS = 72
SLAB = 80


def adamw(grad, master_part, first_part, second_part):
    first_new = 0.9 * first_part + 0.1 * grad
    second_new = 0.95 * second_part + 0.05 * grad * grad
    corr_one = 1.0 - 0.9**STEP
    corr_two = 1.0 - 0.95**STEP
    update = first_new / corr_one / (jnp.sqrt(second_new / corr_two) + 1e-08)
    master_new = master_part - 0.001 * (update + 0.1 * master_part)
    return (master_new, first_new, second_new)


def shift_store(src_ref, dst_ref, image):
    edge = jnp.zeros((16, 1, CHANS), BF16)
    for odd in range(2):
        rows = src_ref[image, :, odd]
        place = pl.ds(odd, 16)
        dst_ref[image, 1 - odd, place, :, 0:128] = jnp.concatenate([edge, rows[:, :31]], axis=1)
        dst_ref[image, 1 - odd, place, :, 128:256] = rows
        dst_ref[image, 1 - odd, place, :, 256:384] = jnp.concatenate([rows[:, 1:], edge], axis=1)
    zero = jnp.zeros((32, 3 * CHANS), BF16)
    dst_ref[image, 0, 0] = zero
    dst_ref[image, 1, 16] = zero


def four_rows(ref, image):
    return jnp.concatenate(
        [ref[image, k % 2, pl.ds(k // 2, 16)].reshape(512, 3 * CHANS) for k in range(4)], axis=1
    )


def pair_forward(w_ref, out_ref):
    zero = jnp.zeros((CHANS, CHANS), BF16)
    for k in range(4):
        for tj in range(3):
            rows = pl.ds((k * 3 + tj) * CHANS, CHANS)
            for odd in range(2):
                tap = (k - odd) * 3 + tj
                block = w_ref[0, tap * CHANS : (tap + 1) * CHANS, :] if 0 <= k - odd <= 2 else zero
                out_ref[rows, odd * CHANS : (odd + 1) * CHANS] = block


def pair_backward(w_ref, out_ref):
    zero = jnp.zeros((CHANS, CHANS), BF16)
    for k in range(4):
        for tj in range(3):
            rows = pl.ds((k * 3 + tj) * CHANS, CHANS)
            for odd in range(2):
                tap = (odd - k + 2) * 3 + 2 - tj
                block = w_ref[1, tap * CHANS : (tap + 1) * CHANS, :].T if 0 <= k - odd <= 2 else zero
                out_ref[rows, odd * CHANS : (odd + 1) * CHANS] = block


def put_turned(ref, value, image):
    turned = value.astype(BF16).T
    for odd in range(2):
        start = odd * BATCH * 512 + image * 512
        ref[:, start : start + 512] = turned[odd * CHANS : (odd + 1) * CHANS]


def outer_sum(turned, ref, first, last):
    out = None
    for odd in range(2):
        for image in range(BATCH):
            near = jnp.concatenate(
                [ref[image, (k + odd) % 2, pl.ds((k + odd) // 2, 16)].reshape(512, 3 * CHANS) for k in range(3)], axis=1
            )
            start = odd * BATCH * 512 + image * 512
            part = jnp.dot(
                turned[:, start : start + 512], near[:, first * CHANS : last * CHANS], preferred_element_type=F32
            )
            out = part if out is None else out + part
    return out


def step_kernel(x_hbm, c_hbm, w_hbm, master_hbm, first_hbm, second_hbm,
                gathered_out, totals_out,
                x_ref, c_ref, w_ref, state_ref,
                x3, c3, forward_w, backward_w, act, slope, dpre, grads,
                pair_recv, xy_send, xy_recv, z_parts, held, totals, gathered,
                load_s, pair_ss, pair_rs, xy_ss, xy_rs, z_ss, z_rs, held_ss, held_rs, t_ss, t_rs, tot_ss, tot_rs,
                gat_ss, gat_rs, fwd_ss, fwd_rs, put_s):
    grp = lax.axis_index("grp")
    dev = lax.axis_index("dev")
    core = lax.rem(grp, 2)
    y = lax.rem(grp, 8) // 2
    z_hi = grp // 8
    x = lax.rem(dev, 4)
    z_lo = dev // 4
    z = z_hi * 4 + z_lo
    partner = (grp + 1 - 2 * core, dev)

    def xy_peer(kx, ky, at=core):
        return (z_hi * 8 + lax.rem(y + ky, 4) * 2 + at, z_lo * 4 + lax.rem(x + kx, 4))

    def z_peer(kz):
        other = lax.rem(z + kz, 8)
        return (other // 4 * 8 + y * 2 + core, lax.rem(other, 4) * 4 + x)

    def held_peer(k):
        return (grp, lax.rem(z_lo + k, 4) * 4 + x)

    def remote(src, dst, ss, rs, target):
        return pltpu.make_async_remote_copy(
            src_ref=src, dst_ref=dst, send_sem=ss, recv_sem=rs, device_id=target, device_id_type=MESH
        )

    loads = [
        pltpu.make_async_copy(src, dst, load_s.at[k])
        for k, (src, dst) in enumerate(
            [(w_hbm.at[0], w_ref.at[0]), (x_hbm, x_ref), (c_hbm, c_ref), (w_hbm.at[1], w_ref.at[1])]
            + [(ref.at[layer], state_ref.at[layer, k])
               for k, ref in enumerate((master_hbm, first_hbm, second_hbm)) for layer in range(2)]
        )
    ]
    for copy in loads[:2]:
        copy.start()
    xy_order = [(kx, ky) for kx in (2, 1, 3, 0) for ky in (2, 1, 3, 0) if kx or ky]
    xy_steps = [(kx, ky) for kx in (0, 1, 3, 2) for ky in (0, 1, 3, 2) if kx or ky]
    z_order = (4, 3, 5, 2, 6, 1, 7)
    peers = [partner] + [xy_peer(*k, at) for k in xy_steps for at in range(2)] + [z_peer(k) for k in z_order]
    barrier = pltpu.get_barrier_semaphore()
    for peer in peers:
        pl.semaphore_signal(barrier, inc=1, device_id=peer, device_id_type=MESH)

    def place(kx, ky):
        return lax.rem(y + ky, 4) * 4 + lax.rem(x + kx, 4)

    def shard_rows(shard):
        start = shard * ROWS
        return pl.ds(start if isinstance(start, int) else pl.multiple_of(start, 8), ROWS)

    own = y * 4 + x

    def part_copy(kx, ky):
        shard, slot = place(kx, ky), (1 - core) * 16 + kx * 4 + ky
        return remote(xy_send.at[1, shard], xy_recv.at[slot], xy_ss.at[1, shard], xy_rs.at[slot], xy_peer(kx, ky, 1))

    def pair_copy(shard):
        return remote(grads.at[0, shard_rows(shard), :], pair_recv.at[shard], pair_ss.at[shard], pair_rs.at[shard], partner)

    def send_pair(first, last):
        for shard in range(first, last):
            pair_copy(shard).start()

    def pair_xy_copy(shard):
        slot = lax.rem(shard % 4 + 4 - x, 4) * 4 + lax.rem(shard // 4 + 4 - y, 4)
        target = (z_hi * 8 + shard // 4 * 2 + core, z_lo * 4 + shard % 4)
        copy = remote(xy_send.at[0, shard], xy_recv.at[slot], xy_ss.at[0, shard], xy_rs.at[slot], target)
        return copy, slot > 0

    def sum_pair():
        for shard in range(16):
            pair_copy(shard).wait_recv()
            both = grads[0, shard_rows(shard), :] + pair_recv[shard]
            grads[0, shard_rows(shard), :] = both
            xy_send[0, shard, 0:ROWS, :] = both.astype(BF16)
            copy, away = pair_xy_copy(shard)
            pl.when(away)(copy.start)

    def send_parts():
        for shard in range(16):
            xy_send[1, shard, 0:ROWS, :] = grads[1, shard_rows(shard), :].astype(BF16)
        for kx, ky in xy_order:
            part_copy(kx, ky).start()
        pl.when(core == 0)(part_copy(0, 0).start)

    for copy in loads[:2]:
        copy.wait()
    for copy in loads[2:]:
        copy.start()
    pair_forward(w_ref, forward_w)
    shift_store(x_ref, x3, 0)
    for image in range(BATCH):
        pre = jnp.dot(four_rows(x3, image), forward_w[...], preferred_element_type=F32)
        sig = 1.0 / (1.0 + jnp.exp(-pre))
        value = pre * sig
        put_turned(act, value, image)
        slope[image] = sig + value * (1.0 - sig)
        if image < BATCH - 1:
            shift_store(x_ref, x3, image + 1)
    for copy in loads[2:]:
        copy.wait()
    for image in range(BATCH):
        shift_store(c_ref, c3, image)

    pair_backward(w_ref, backward_w)
    out = outer_sum(act, c3, 0, 9)
    for block in range(9):
        tap = 8 - block
        grads[1, tap * CHANS : (tap + 1) * CHANS, :] = out[:, block * CHANS : (block + 1) * CHANS]

    pl.semaphore_wait(barrier, len(peers))
    send_parts()

    def held_copy(k, source_ref):
        return remote(source_ref, held, held_ss.at[k], held_rs, held_peer(k))

    @pl.when(z_lo == y)
    def _():
        held[...] = state_ref[core]
        for k in range(1, 4):
            held_copy(k, held).start()

    for image in range(BATCH):
        back = jnp.dot(four_rows(c3, image), backward_w[...], preferred_element_type=F32)
        put_turned(dpre, back * slope[image], image)

    def first_layer(first, last):
        out = outer_sum(dpre, x3, first, last)
        for tap in range(first, last):
            block = out[:, (tap - first) * CHANS : (tap + 1 - first) * CHANS]
            grads[0, tap * CHANS : (tap + 1) * CHANS, :] = block.T

    first_layer(0, 5)

    @pl.when(core == 1)
    def _():
        send_pair(0, 8)

    first_layer(5, 9)

    @pl.when(core == 1)
    def _():
        send_pair(8, 16)

    @pl.when(core == 0)
    def _():
        sum_pair()

    def sum_parts(layer, others):
        acc = grads[layer, shard_rows(own), :]
        for kx, ky in [(0, 0)] + xy_steps:
            for other in range(others):
                slot = other * 16 + kx * 4 + ky
                if slot:
                    ref = xy_recv.at[slot]
                    remote(ref, ref, xy_ss.at[0, 0], xy_rs.at[slot], partner).wait_recv()
                    acc = acc + xy_recv[slot, 0:ROWS, :].astype(F32)
        z_parts[z, 0:ROWS, :] = acc.astype(BF16)

    @pl.when(core == 0)
    def _():
        sum_parts(0, 1)

    @pl.when(core == 1)
    def _():
        sum_parts(1, 2)

    def z_copy(kz, place):
        return remote(z_parts.at[place], z_parts.at[place], z_ss.at[kz], z_rs.at[kz], z_peer(kz))

    for kz in z_order:
        z_copy(kz, z).start()
    for kz in z_order[::-1]:
        z_copy(kz, lax.rem(z + 8 - kz, 8)).wait_recv()
    z_part = [z_parts[k, 0:ROWS, :].astype(F32) for k in range(8)]
    halves = [(z_part[k] + z_part[k + 1]) + (z_part[k + 2] + z_part[k + 3]) for k in (0, 4)]
    whole = halves[0] + halves[1]

    @pl.when(z_lo != y)
    def _():
        held_copy(1, held).wait_recv()

    slab = adamw(whole, held[0], held[1], held[2])[0].astype(BF16)
    gathered[y * 4 + x, 0:ROWS, :] = slab

    def gat_copy(kx, ky, slot):
        ref = gathered.at[slot]
        return remote(ref, ref, gat_ss.at[kx * 4 + ky], gat_rs.at[kx * 4 + ky], xy_peer(kx, ky))

    def source(kx, ky):
        return place(4 - kx, 4 - ky)

    def fwd_copy(layer, kx, ky):
        slot = source(kx, ky)
        k = kx * 4 + ky
        return remote(gathered.at[slot], gathered_out.at[layer, slot], fwd_ss.at[k], fwd_rs.at[k], partner)

    for kx, ky in xy_order:
        gat_copy(kx, ky, source(0, 0)).start()
    fwd_copy(core, 0, 0).start()

    def t_copy(ky):
        return remote(totals, totals, t_ss.at[ky], t_rs, xy_peer(0, ky))

    @pl.when(z_lo == y)
    def _():
        totals[...] = whole
        for ky in (2, 1, 3):
            t_copy(ky).start()

    @pl.when(core == 0)
    def _():
        part_copy(0, 0).wait_send()
        for shard in range(16):
            copy, away = pair_xy_copy(shard)
            pl.when(away)(copy.wait_send)

    @pl.when(core == 1)
    def _():
        for k in range(16):
            pair_copy(k).wait_send()

    for kx, ky in xy_steps:
        part_copy(kx, ky).wait_send()
    for kz in z_order:
        z_copy(kz, z).wait_send()

    @pl.when(z_lo == y)
    def _():
        for k in range(1, 4):
            held_copy(k, held).wait_send()

    def forward(steps):
        for kx, ky in steps:
            gat_copy(kx, ky, source(kx, ky)).wait_recv()
            fwd_copy(core, kx, ky).start()

    forward(xy_steps[:3])

    @pl.when(z_lo != y)
    def _():
        t_copy(1).wait_recv()

    tot = remote(totals, totals_out.at[core], tot_ss, tot_rs, partner)
    tot.start()
    puts = [
        pltpu.make_async_copy(totals, totals_out.at[core], put_s.at[0]),
        pltpu.make_async_copy(gathered, gathered_out.at[core], put_s.at[1]),
    ]
    puts[0].start()
    forward(xy_steps[3:])
    puts[1].start()
    for kx, ky in xy_steps:
        gat_copy(kx, ky, source(0, 0)).wait_send()

    @pl.when(z_lo == y)
    def _():
        for k in range(1, 4):
            t_copy(k).wait_send()

    remote(totals, totals_out.at[1 - core], tot_ss, tot_rs, partner).wait_recv()
    for kx, ky in xy_steps + [(0, 0)]:
        fwd_copy(1 - core, kx, ky).wait_recv()
    for k in range(16):
        fwd_copy(core, k // 4, k % 4).wait_send()
    tot.wait_send()
    for copy in puts:
        copy.wait()


def finish_kernel(gathered_hbm, totals_hbm, master_hbm, first_hbm, second_hbm,
                  weights_hbm, master_out, first_out, second_out,
                  gathered, weights, held, new, load_s, state_s, store_s, new_s):
    loads, stores = [], []
    for k in range(4):
        layer, part = k // 2, pl.ds(k % 2 * 8, 8)
        loads.append(pltpu.make_async_copy(gathered_hbm.at[layer, part], gathered.at[layer, part], load_s.at[k]))
        rows = pl.ds(k % 2 * 8 * ROWS, 8 * ROWS)
        stores.append(pltpu.make_async_copy(weights.at[layer, rows], weights_hbm.at[layer, rows], store_s.at[k]))
    states = [
        pltpu.make_async_copy(src, held.at[k], state_s.at[k])
        for k, src in enumerate((totals_hbm, master_hbm, first_hbm, second_hbm))
    ]
    for copy in states + loads:
        copy.start()
    for copy in states:
        copy.wait()
    for k, value in enumerate(adamw(held[0], held[1], held[2], held[3])):
        new[k] = value
        store = pltpu.make_async_copy(new.at[k], (master_out, first_out, second_out)[k], new_s.at[k])
        store.start()
        stores.append(store)
    for k in range(4):
        loads[k].wait()
        for two in range(k % 2 * 4, k % 2 * 4 + 4):
            both = [gathered[k // 2, 2 * two + odd, 0:ROWS, :].astype(F32) for odd in range(2)]
            weights[k // 2, 2 * ROWS * two : 2 * ROWS * (two + 1), :] = jnp.concatenate(both, axis=0).astype(BF16)
        stores[k].start()
    for copy in stores:
        copy.wait()


def shards(inputs, cotangent, weights, master, first_moment, second_moment):
    far = pl.BlockSpec(memory_space=pltpu.HBM)
    dma = pltpu.SemaphoreType.DMA
    vmem = pltpu.VMEM
    by_pairs = (BATCH, 16, 2, 32, CHANS)
    gathered, totals = pl.pallas_call(
        step_kernel,
        out_shape=(
            jax.ShapeDtypeStruct((2, 16, SLAB, CHANS), BF16),
            jax.ShapeDtypeStruct((2, ROWS, CHANS), F32),
        ),
        in_specs=[far] * 6,
        out_specs=(far, far),
        scratch_shapes=[
            vmem(by_pairs, BF16),
            vmem(by_pairs, BF16),
            vmem(weights.shape, BF16),
            vmem((2, 3, ROWS, CHANS), F32),
            vmem((BATCH, 2, 17, 32, 3 * CHANS), BF16),
            vmem((BATCH, 2, 17, 32, 3 * CHANS), BF16),
            vmem((12 * CHANS, 2 * CHANS), BF16),
            vmem((12 * CHANS, 2 * CHANS), BF16),
            vmem((CHANS, BATCH * 1024), BF16),
            vmem((BATCH, 512, 2 * CHANS), F32),
            vmem((CHANS, BATCH * 1024), BF16),
            vmem((2, 9 * CHANS, CHANS), F32),
            vmem((16, ROWS, CHANS), F32),
            vmem((2, 16, SLAB, CHANS), BF16),
            vmem((32, SLAB, CHANS), BF16),
            vmem((8, SLAB, CHANS), BF16),
            vmem((3, ROWS, CHANS), F32),
            vmem((ROWS, CHANS), F32),
            vmem((16, SLAB, CHANS), BF16),
            dma((10,)),
            dma((16,)), dma((16,)), dma((2, 16)), dma((32,)), dma((8,)), dma((8,)), dma((4,)), dma,
            dma((4,)), dma, dma, dma, dma((16,)), dma((16,)), dma((16,)), dma((16,)), dma((2,)),
        ],
        compiler_params=pltpu.CompilerParams(collective_id=0, has_side_effects=True, vmem_limit_bytes=60 * 2**20),
        name="step",
    )(inputs.reshape(by_pairs), cotangent.reshape(by_pairs), weights, master, first_moment, second_moment)
    state = jax.ShapeDtypeStruct(master.shape, F32)
    return pl.pallas_call(
        finish_kernel,
        out_shape=(jax.ShapeDtypeStruct(weights.shape, BF16), state, state, state),
        in_specs=[far] * 5,
        out_specs=(far,) * 4,
        scratch_shapes=[
            vmem((2, 16, SLAB, CHANS), BF16),
            vmem(weights.shape, BF16),
            vmem((4,) + master.shape, F32),
            vmem((3,) + master.shape, F32),
            dma((4,)), dma((4,)), dma((4,)), dma((3,)),
        ],
        compiler_params=pltpu.CompilerParams(vmem_limit_bytes=60 * 2**20),
        name="finish",
    )(gathered, totals, master, first_moment, second_moment)


def solution(mesh):
    placed = (
        P(("grp", "dev"), None, None, None),
        P(("grp", "dev"), None, None, None),
        P(),
        P(None, "dev", None),
        P(None, "dev", None),
        P(None, "dev", None),
    )
    return jax.shard_map(
        shards,
        mesh=mesh,
        in_specs=placed,
        out_specs=(P(), P(None, "dev", None), P(None, "dev", None), P(None, "dev", None)),
        check_vma=False,
    )
```

```python
import jax
import jax.numpy as jnp
from jax import lax
from jax.experimental import pallas as pl
from jax.experimental.pallas import tpu as pltpu
from jax.sharding import PartitionSpec as P

STEP = 10
MESH = pl.DeviceIdType.MESH
BF16, F32 = jnp.bfloat16, jnp.float32
BATCH, CHANS = 4, 128
ROWS = 72
SLAB = 80


def adamw(grad, master_part, first_part, second_part):
    first_new = 0.9 * first_part + 0.1 * grad
    second_new = 0.95 * second_part + 0.05 * grad * grad
    corr_one = 1.0 - 0.9**STEP
    corr_two = 1.0 - 0.95**STEP
    update = first_new / corr_one / (jnp.sqrt(second_new / corr_two) + 1e-08)
    master_new = master_part - 0.001 * (update + 0.1 * master_part)
    return (master_new, first_new, second_new)


def shift_store(src_ref, dst_ref, image):
    edge = jnp.zeros((16, 1, CHANS), BF16)
    for odd in range(2):
        rows = src_ref[image, :, odd]
        place = pl.ds(odd, 16)
        dst_ref[image, 1 - odd, place, :, 0:128] = jnp.concatenate([edge, rows[:, :31]], axis=1)
        dst_ref[image, 1 - odd, place, :, 128:256] = rows
        dst_ref[image, 1 - odd, place, :, 256:384] = jnp.concatenate([rows[:, 1:], edge], axis=1)
    zero = jnp.zeros((32, 3 * CHANS), BF16)
    dst_ref[image, 0, 0] = zero
    dst_ref[image, 1, 16] = zero


def four_rows(ref, image):
    return jnp.concatenate(
        [ref[image, k % 2, pl.ds(k // 2, 16)].reshape(512, 3 * CHANS) for k in range(4)], axis=1
    )


def pair_forward(w_ref, out_ref):
    zero = jnp.zeros((CHANS, CHANS), BF16)
    for k in range(4):
        for tj in range(3):
            rows = pl.ds((k * 3 + tj) * CHANS, CHANS)
            for odd in range(2):
                tap = (k - odd) * 3 + tj
                block = w_ref[0, tap * CHANS : (tap + 1) * CHANS, :] if 0 <= k - odd <= 2 else zero
                out_ref[rows, odd * CHANS : (odd + 1) * CHANS] = block


def pair_backward(w_ref, out_ref):
    zero = jnp.zeros((CHANS, CHANS), BF16)
    for k in range(4):
        for tj in range(3):
            rows = pl.ds((k * 3 + tj) * CHANS, CHANS)
            for odd in range(2):
                tap = (odd - k + 2) * 3 + 2 - tj
                block = w_ref[1, tap * CHANS : (tap + 1) * CHANS, :].T if 0 <= k - odd <= 2 else zero
                out_ref[rows, odd * CHANS : (odd + 1) * CHANS] = block


def put_turned(ref, value, image):
    turned = value.astype(BF16).T
    for odd in range(2):
        start = odd * BATCH * 512 + image * 512
        ref[:, start : start + 512] = turned[odd * CHANS : (odd + 1) * CHANS]


def outer_sum(turned, ref, first, last):
    out = None
    for odd in range(2):
        for image in range(BATCH):
            near = jnp.concatenate(
                [ref[image, (k + odd) % 2, pl.ds((k + odd) // 2, 16)].reshape(512, 3 * CHANS) for k in range(3)], axis=1
            )
            start = odd * BATCH * 512 + image * 512
            part = jnp.dot(
                turned[:, start : start + 512], near[:, first * CHANS : last * CHANS], preferred_element_type=F32
            )
            out = part if out is None else out + part
    return out


def step_kernel(x_hbm, c_hbm, w_hbm, master_hbm, first_hbm, second_hbm,
                gathered_out, totals_out,
                x_ref, c_ref, w_ref, state_ref,
                x3, c3, forward_w, backward_w, act, slope, dpre, grads,
                pair_recv, xy_send, xy_recv, z_parts, held, totals, gathered,
                load_s, pair_ss, pair_rs, xy_ss, xy_rs, z_ss, z_rs, held_ss, held_rs, t_ss, t_rs, tot_ss, tot_rs,
                gat_ss, gat_rs, fwd_ss, fwd_rs, put_s):
    grp = lax.axis_index("grp")
    dev = lax.axis_index("dev")
    core = lax.rem(grp, 2)
    y = lax.rem(grp, 8) // 2
    z_hi = grp // 8
    x = lax.rem(dev, 4)
    z_lo = dev // 4
    z = z_hi * 4 + z_lo
    partner = (grp + 1 - 2 * core, dev)

    def xy_peer(kx, ky, at=core):
        return (z_hi * 8 + lax.rem(y + ky, 4) * 2 + at, z_lo * 4 + lax.rem(x + kx, 4))

    def z_peer(kz):
        other = lax.rem(z + kz, 8)
        return (other // 4 * 8 + y * 2 + core, lax.rem(other, 4) * 4 + x)

    def held_peer(k):
        return (grp, lax.rem(z_lo + k, 4) * 4 + x)

    def remote(src, dst, ss, rs, target):
        return pltpu.make_async_remote_copy(
            src_ref=src, dst_ref=dst, send_sem=ss, recv_sem=rs, device_id=target, device_id_type=MESH
        )

    loads = [
        pltpu.make_async_copy(src, dst, load_s.at[k])
        for k, (src, dst) in enumerate(
            [(w_hbm.at[0], w_ref.at[0]), (x_hbm, x_ref), (c_hbm, c_ref), (w_hbm.at[1], w_ref.at[1])]
            + [(ref.at[layer], state_ref.at[layer, k])
               for k, ref in enumerate((master_hbm, first_hbm, second_hbm)) for layer in range(2)]
        )
    ]
    for copy in loads[:2]:
        copy.start()
    xy_order = [(kx, ky) for kx in (2, 1, 3, 0) for ky in (2, 1, 3, 0) if kx or ky]
    xy_steps = [(kx, ky) for kx in (0, 1, 3, 2) for ky in (0, 1, 3, 2) if kx or ky]
    z_order = (4, 3, 5, 2, 6, 1, 7)
    peers = [partner] + [xy_peer(*k, at) for k in xy_steps for at in range(2)] + [z_peer(k) for k in z_order]
    barrier = pltpu.get_barrier_semaphore()
    for peer in peers:
        pl.semaphore_signal(barrier, inc=1, device_id=peer, device_id_type=MESH)

    def place(kx, ky):
        return lax.rem(y + ky, 4) * 4 + lax.rem(x + kx, 4)

    def shard_rows(shard):
        start = shard * ROWS
        return pl.ds(start if isinstance(start, int) else pl.multiple_of(start, 8), ROWS)

    own = y * 4 + x

    def part_copy(kx, ky):
        shard, slot = place(kx, ky), (1 - core) * 16 + kx * 4 + ky
        return remote(xy_send.at[1, shard], xy_recv.at[slot], xy_ss.at[1, shard], xy_rs.at[slot], xy_peer(kx, ky, 1))

    def pair_copy(shard):
        return remote(grads.at[0, shard_rows(shard), :], pair_recv.at[shard], pair_ss.at[shard], pair_rs.at[shard], partner)

    def send_pair(first, last):
        for shard in range(first, last):
            pair_copy(shard).start()

    def pair_xy_copy(shard):
        slot = lax.rem(shard % 4 + 4 - x, 4) * 4 + lax.rem(shard // 4 + 4 - y, 4)
        target = (z_hi * 8 + shard // 4 * 2 + core, z_lo * 4 + shard % 4)
        copy = remote(xy_send.at[0, shard], xy_recv.at[slot], xy_ss.at[0, shard], xy_rs.at[slot], target)
        return copy, slot > 0

    def sum_pair():
        for shard in range(16):
            pair_copy(shard).wait_recv()
            both = grads[0, shard_rows(shard), :] + pair_recv[shard]
            grads[0, shard_rows(shard), :] = both
            xy_send[0, shard, 0:ROWS, :] = both.astype(BF16)
            copy, away = pair_xy_copy(shard)
            pl.when(away)(copy.start)

    def send_parts():
        for shard in range(16):
            xy_send[1, shard, 0:ROWS, :] = grads[1, shard_rows(shard), :].astype(BF16)
        for kx, ky in xy_order:
            part_copy(kx, ky).start()
        pl.when(core == 0)(part_copy(0, 0).start)

    for copy in loads[:2]:
        copy.wait()
    for copy in loads[2:]:
        copy.start()
    pair_forward(w_ref, forward_w)
    shift_store(x_ref, x3, 0)
    for image in range(BATCH):
        pre = jnp.dot(four_rows(x3, image), forward_w[...], preferred_element_type=F32)
        sig = 1.0 / (1.0 + jnp.exp(-pre))
        value = pre * sig
        put_turned(act, value, image)
        slope[image] = sig + value * (1.0 - sig)
        if image < BATCH - 1:
            shift_store(x_ref, x3, image + 1)
    for copy in loads[2:]:
        copy.wait()
    for image in range(BATCH):
        shift_store(c_ref, c3, image)

    pair_backward(w_ref, backward_w)
    out = outer_sum(act, c3, 0, 9)
    for block in range(9):
        tap = 8 - block
        grads[1, tap * CHANS : (tap + 1) * CHANS, :] = out[:, block * CHANS : (block + 1) * CHANS]

    pl.semaphore_wait(barrier, len(peers))
    send_parts()

    def held_copy(k, source_ref):
        return remote(source_ref, held, held_ss.at[k], held_rs, held_peer(k))

    @pl.when(z_lo == y)
    def _():
        held[...] = state_ref[core]
        for k in range(1, 4):
            held_copy(k, held).start()

    for image in range(BATCH):
        back = jnp.dot(four_rows(c3, image), backward_w[...], preferred_element_type=F32)
        put_turned(dpre, back * slope[image], image)

    def first_layer(first, last):
        out = outer_sum(dpre, x3, first, last)
        for tap in range(first, last):
            block = out[:, (tap - first) * CHANS : (tap + 1 - first) * CHANS]
            grads[0, tap * CHANS : (tap + 1) * CHANS, :] = block.T

    first_layer(0, 5)

    @pl.when(core == 1)
    def _():
        send_pair(0, 8)

    first_layer(5, 7)

    @pl.when(core == 1)
    def _():
        send_pair(8, 12)

    first_layer(7, 9)

    @pl.when(core == 1)
    def _():
        send_pair(12, 16)

    @pl.when(core == 0)
    def _():
        sum_pair()

    def sum_parts(layer, others):
        acc = grads[layer, shard_rows(own), :]
        for kx, ky in [(0, 0)] + xy_steps:
            for other in range(others):
                slot = other * 16 + kx * 4 + ky
                if slot:
                    ref = xy_recv.at[slot]
                    remote(ref, ref, xy_ss.at[0, 0], xy_rs.at[slot], partner).wait_recv()
                    acc = acc + xy_recv[slot, 0:ROWS, :].astype(F32)
        z_parts[z, 0:ROWS, :] = acc.astype(BF16)

    @pl.when(core == 0)
    def _():
        sum_parts(0, 1)

    @pl.when(core == 1)
    def _():
        sum_parts(1, 2)

    def z_copy(kz, place):
        return remote(z_parts.at[place], z_parts.at[place], z_ss.at[kz], z_rs.at[kz], z_peer(kz))

    for kz in z_order:
        z_copy(kz, z).start()
    for kz in z_order[::-1]:
        z_copy(kz, lax.rem(z + 8 - kz, 8)).wait_recv()
    z_part = [z_parts[k, 0:ROWS, :].astype(F32) for k in range(8)]
    halves = [(z_part[k] + z_part[k + 1]) + (z_part[k + 2] + z_part[k + 3]) for k in (0, 4)]
    whole = halves[0] + halves[1]

    @pl.when(z_lo != y)
    def _():
        held_copy(1, held).wait_recv()

    slab = adamw(whole, held[0], held[1], held[2])[0].astype(BF16)
    gathered[y * 4 + x, 0:ROWS, :] = slab

    def gat_copy(kx, ky, slot):
        ref = gathered.at[slot]
        return remote(ref, ref, gat_ss.at[kx * 4 + ky], gat_rs.at[kx * 4 + ky], xy_peer(kx, ky))

    def source(kx, ky):
        return place(4 - kx, 4 - ky)

    def fwd_copy(layer, kx, ky):
        slot = source(kx, ky)
        k = kx * 4 + ky
        return remote(gathered.at[slot], gathered_out.at[layer, slot], fwd_ss.at[k], fwd_rs.at[k], partner)

    for kx, ky in xy_order:
        gat_copy(kx, ky, source(0, 0)).start()
    fwd_copy(core, 0, 0).start()

    def t_copy(ky):
        return remote(totals, totals, t_ss.at[ky], t_rs, xy_peer(0, ky))

    @pl.when(z_lo == y)
    def _():
        totals[...] = whole
        for ky in (2, 1, 3):
            t_copy(ky).start()

    @pl.when(core == 0)
    def _():
        part_copy(0, 0).wait_send()
        for shard in range(16):
            copy, away = pair_xy_copy(shard)
            pl.when(away)(copy.wait_send)

    @pl.when(core == 1)
    def _():
        for k in range(16):
            pair_copy(k).wait_send()

    for kx, ky in xy_steps:
        part_copy(kx, ky).wait_send()
    for kz in z_order:
        z_copy(kz, z).wait_send()

    @pl.when(z_lo == y)
    def _():
        for k in range(1, 4):
            held_copy(k, held).wait_send()

    def forward(steps):
        for kx, ky in steps:
            gat_copy(kx, ky, source(kx, ky)).wait_recv()
            fwd_copy(core, kx, ky).start()

    forward(xy_steps[:3])

    @pl.when(z_lo != y)
    def _():
        t_copy(1).wait_recv()

    tot = remote(totals, totals_out.at[core], tot_ss, tot_rs, partner)
    tot.start()
    puts = [
        pltpu.make_async_copy(totals, totals_out.at[core], put_s.at[0]),
        pltpu.make_async_copy(gathered, gathered_out.at[core], put_s.at[1]),
    ]
    puts[0].start()
    forward(xy_steps[3:])
    puts[1].start()
    for kx, ky in xy_steps:
        gat_copy(kx, ky, source(0, 0)).wait_send()

    @pl.when(z_lo == y)
    def _():
        for k in range(1, 4):
            t_copy(k).wait_send()

    remote(totals, totals_out.at[1 - core], tot_ss, tot_rs, partner).wait_recv()
    for kx, ky in xy_steps + [(0, 0)]:
        fwd_copy(1 - core, kx, ky).wait_recv()
    for k in range(16):
        fwd_copy(core, k // 4, k % 4).wait_send()
    tot.wait_send()
    for copy in puts:
        copy.wait()


def finish_kernel(gathered_hbm, totals_hbm, master_hbm, first_hbm, second_hbm,
                  weights_hbm, master_out, first_out, second_out,
                  gathered, weights, held, new, load_s, state_s, store_s, new_s):
    loads, stores = [], []
    for k in range(4):
        layer, part = k // 2, pl.ds(k % 2 * 8, 8)
        loads.append(pltpu.make_async_copy(gathered_hbm.at[layer, part], gathered.at[layer, part], load_s.at[k]))
        rows = pl.ds(k % 2 * 8 * ROWS, 8 * ROWS)
        stores.append(pltpu.make_async_copy(weights.at[layer, rows], weights_hbm.at[layer, rows], store_s.at[k]))
    states = [
        pltpu.make_async_copy(src, held.at[k], state_s.at[k])
        for k, src in enumerate((totals_hbm, master_hbm, first_hbm, second_hbm))
    ]
    for copy in states + loads:
        copy.start()
    for copy in states:
        copy.wait()
    for k, value in enumerate(adamw(held[0], held[1], held[2], held[3])):
        new[k] = value
        store = pltpu.make_async_copy(new.at[k], (master_out, first_out, second_out)[k], new_s.at[k])
        store.start()
        stores.append(store)
    for k in range(4):
        loads[k].wait()
        for two in range(k % 2 * 4, k % 2 * 4 + 4):
            both = [gathered[k // 2, 2 * two + odd, 0:ROWS, :].astype(F32) for odd in range(2)]
            weights[k // 2, 2 * ROWS * two : 2 * ROWS * (two + 1), :] = jnp.concatenate(both, axis=0).astype(BF16)
        stores[k].start()
    for copy in stores:
        copy.wait()


def shards(inputs, cotangent, weights, master, first_moment, second_moment):
    far = pl.BlockSpec(memory_space=pltpu.HBM)
    dma = pltpu.SemaphoreType.DMA
    vmem = pltpu.VMEM
    by_pairs = (BATCH, 16, 2, 32, CHANS)
    gathered, totals = pl.pallas_call(
        step_kernel,
        out_shape=(
            jax.ShapeDtypeStruct((2, 16, SLAB, CHANS), BF16),
            jax.ShapeDtypeStruct((2, ROWS, CHANS), F32),
        ),
        in_specs=[far] * 6,
        out_specs=(far, far),
        scratch_shapes=[
            vmem(by_pairs, BF16),
            vmem(by_pairs, BF16),
            vmem(weights.shape, BF16),
            vmem((2, 3, ROWS, CHANS), F32),
            vmem((BATCH, 2, 17, 32, 3 * CHANS), BF16),
            vmem((BATCH, 2, 17, 32, 3 * CHANS), BF16),
            vmem((12 * CHANS, 2 * CHANS), BF16),
            vmem((12 * CHANS, 2 * CHANS), BF16),
            vmem((CHANS, BATCH * 1024), BF16),
            vmem((BATCH, 512, 2 * CHANS), F32),
            vmem((CHANS, BATCH * 1024), BF16),
            vmem((2, 9 * CHANS, CHANS), F32),
            vmem((16, ROWS, CHANS), F32),
            vmem((2, 16, SLAB, CHANS), BF16),
            vmem((32, SLAB, CHANS), BF16),
            vmem((8, SLAB, CHANS), BF16),
            vmem((3, ROWS, CHANS), F32),
            vmem((ROWS, CHANS), F32),
            vmem((16, SLAB, CHANS), BF16),
            dma((10,)),
            dma((16,)), dma((16,)), dma((2, 16)), dma((32,)), dma((8,)), dma((8,)), dma((4,)), dma,
            dma((4,)), dma, dma, dma, dma((16,)), dma((16,)), dma((16,)), dma((16,)), dma((2,)),
        ],
        compiler_params=pltpu.CompilerParams(collective_id=0, has_side_effects=True, vmem_limit_bytes=60 * 2**20),
        name="step",
    )(inputs.reshape(by_pairs), cotangent.reshape(by_pairs), weights, master, first_moment, second_moment)
    state = jax.ShapeDtypeStruct(master.shape, F32)
    return pl.pallas_call(
        finish_kernel,
        out_shape=(jax.ShapeDtypeStruct(weights.shape, BF16), state, state, state),
        in_specs=[far] * 5,
        out_specs=(far,) * 4,
        scratch_shapes=[
            vmem((2, 16, SLAB, CHANS), BF16),
            vmem(weights.shape, BF16),
            vmem((4,) + master.shape, F32),
            vmem((3,) + master.shape, F32),
            dma((4,)), dma((4,)), dma((4,)), dma((3,)),
        ],
        compiler_params=pltpu.CompilerParams(vmem_limit_bytes=60 * 2**20),
        name="finish",
    )(gathered, totals, master, first_moment, second_moment)


def solution(mesh):
    placed = (
        P(("grp", "dev"), None, None, None),
        P(("grp", "dev"), None, None, None),
        P(),
        P(None, "dev", None),
        P(None, "dev", None),
        P(None, "dev", None),
    )
    return jax.shard_map(
        shards,
        mesh=mesh,
        in_specs=placed,
        out_specs=(P(), P(None, "dev", None), P(None, "dev", None), P(None, "dev", None)),
        check_vma=False,
    )
```

```python
import jax
import jax.numpy as jnp
from jax import lax
from jax.experimental import pallas as pl
from jax.experimental.pallas import tpu as pltpu
from jax.sharding import PartitionSpec as P

STEP = 10
MESH = pl.DeviceIdType.MESH
BF16, F32 = jnp.bfloat16, jnp.float32
BATCH, CHANS = 4, 128
ROWS = 72
SLAB = 80


def adamw(grad, master_part, first_part, second_part):
    first_new = 0.9 * first_part + 0.1 * grad
    second_new = 0.95 * second_part + 0.05 * grad * grad
    corr_one = 1.0 - 0.9**STEP
    corr_two = 1.0 - 0.95**STEP
    update = first_new / corr_one / (jnp.sqrt(second_new / corr_two) + 1e-08)
    master_new = master_part - 0.001 * (update + 0.1 * master_part)
    return (master_new, first_new, second_new)


def shift_store(src_ref, dst_ref, image):
    edge = jnp.zeros((16, 1, CHANS), BF16)
    for odd in range(2):
        rows = src_ref[image, :, odd]
        place = pl.ds(odd, 16)
        dst_ref[image, 1 - odd, place, :, 0:128] = jnp.concatenate([edge, rows[:, :31]], axis=1)
        dst_ref[image, 1 - odd, place, :, 128:256] = rows
        dst_ref[image, 1 - odd, place, :, 256:384] = jnp.concatenate([rows[:, 1:], edge], axis=1)
    zero = jnp.zeros((32, 3 * CHANS), BF16)
    dst_ref[image, 0, 0] = zero
    dst_ref[image, 1, 16] = zero


def four_rows(ref, image):
    return jnp.concatenate(
        [ref[image, k % 2, pl.ds(k // 2, 16)].reshape(512, 3 * CHANS) for k in range(4)], axis=1
    )


def pair_forward(w_ref, out_ref):
    zero = jnp.zeros((CHANS, CHANS), BF16)
    for k in range(4):
        for tj in range(3):
            rows = pl.ds((k * 3 + tj) * CHANS, CHANS)
            for odd in range(2):
                tap = (k - odd) * 3 + tj
                block = w_ref[0, tap * CHANS : (tap + 1) * CHANS, :] if 0 <= k - odd <= 2 else zero
                out_ref[rows, odd * CHANS : (odd + 1) * CHANS] = block


def pair_backward(w_ref, out_ref):
    zero = jnp.zeros((CHANS, CHANS), BF16)
    for k in range(4):
        for tj in range(3):
            rows = pl.ds((k * 3 + tj) * CHANS, CHANS)
            for odd in range(2):
                tap = (odd - k + 2) * 3 + 2 - tj
                block = w_ref[1, tap * CHANS : (tap + 1) * CHANS, :].T if 0 <= k - odd <= 2 else zero
                out_ref[rows, odd * CHANS : (odd + 1) * CHANS] = block


def put_turned(ref, value, image):
    turned = value.astype(BF16).T
    for odd in range(2):
        start = odd * BATCH * 512 + image * 512
        ref[:, start : start + 512] = turned[odd * CHANS : (odd + 1) * CHANS]


def outer_sum(turned, ref, first, last):
    out = None
    for odd in range(2):
        for image in range(BATCH):
            near = jnp.concatenate(
                [ref[image, (k + odd) % 2, pl.ds((k + odd) // 2, 16)].reshape(512, 3 * CHANS) for k in range(3)], axis=1
            )
            start = odd * BATCH * 512 + image * 512
            part = jnp.dot(
                turned[:, start : start + 512], near[:, first * CHANS : last * CHANS], preferred_element_type=F32
            )
            out = part if out is None else out + part
    return out


def step_kernel(x_hbm, c_hbm, w_hbm, master_hbm, first_hbm, second_hbm,
                gathered_out, totals_out,
                x_ref, c_ref, w_ref, state_ref,
                x3, c3, forward_w, backward_w, act, slope, dpre, grads,
                pair_recv, xy_send, xy_recv, z_parts, held, totals, gathered,
                load_s, pair_ss, pair_rs, xy_ss, xy_rs, z_ss, z_rs, held_ss, held_rs, t_ss, t_rs, tot_ss, tot_rs,
                gat_ss, gat_rs, fwd_ss, fwd_rs, put_s):
    grp = lax.axis_index("grp")
    dev = lax.axis_index("dev")
    core = lax.rem(grp, 2)
    y = lax.rem(grp, 8) // 2
    z_hi = grp // 8
    x = lax.rem(dev, 4)
    z_lo = dev // 4
    z = z_hi * 4 + z_lo
    partner = (grp + 1 - 2 * core, dev)

    def xy_peer(kx, ky, at=core):
        return (z_hi * 8 + lax.rem(y + ky, 4) * 2 + at, z_lo * 4 + lax.rem(x + kx, 4))

    def z_peer(kz):
        other = lax.rem(z + kz, 8)
        return (other // 4 * 8 + y * 2 + core, lax.rem(other, 4) * 4 + x)

    def held_peer(k):
        return (grp, lax.rem(z_lo + k, 4) * 4 + x)

    def remote(src, dst, ss, rs, target):
        return pltpu.make_async_remote_copy(
            src_ref=src, dst_ref=dst, send_sem=ss, recv_sem=rs, device_id=target, device_id_type=MESH
        )

    loads = [
        pltpu.make_async_copy(src, dst, load_s.at[k])
        for k, (src, dst) in enumerate(
            [(w_hbm.at[0], w_ref.at[0]), (x_hbm, x_ref), (c_hbm, c_ref), (w_hbm.at[1], w_ref.at[1])]
            + [(ref.at[layer], state_ref.at[layer, k])
               for k, ref in enumerate((master_hbm, first_hbm, second_hbm)) for layer in range(2)]
        )
    ]
    for copy in loads[:2]:
        copy.start()
    xy_order = [(kx, ky) for kx in (2, 1, 3, 0) for ky in (2, 1, 3, 0) if kx or ky]
    xy_steps = [(kx, ky) for kx in (0, 1, 3, 2) for ky in (0, 1, 3, 2) if kx or ky]
    z_order = (4, 3, 5, 2, 6, 1, 7)
    peers = [partner] + [xy_peer(*k, at) for k in xy_steps for at in range(2)] + [z_peer(k) for k in z_order]
    barrier = pltpu.get_barrier_semaphore()
    for peer in peers:
        pl.semaphore_signal(barrier, inc=1, device_id=peer, device_id_type=MESH)

    def place(kx, ky):
        return lax.rem(y + ky, 4) * 4 + lax.rem(x + kx, 4)

    def shard_rows(shard):
        start = shard * ROWS
        return pl.ds(start if isinstance(start, int) else pl.multiple_of(start, 8), ROWS)

    own = y * 4 + x

    def part_copy(kx, ky):
        shard, slot = place(kx, ky), (1 - core) * 16 + kx * 4 + ky
        return remote(xy_send.at[1, shard], xy_recv.at[slot], xy_ss.at[1, shard], xy_rs.at[slot], xy_peer(kx, ky, 1))

    def pair_copy(shard):
        return remote(grads.at[0, shard_rows(shard), :], pair_recv.at[shard], pair_ss.at[shard], pair_rs.at[shard], partner)

    def send_pair(first, last):
        for shard in range(first, last):
            pair_copy(shard).start()

    def pair_xy_copy(shard):
        slot = lax.rem(shard % 4 + 4 - x, 4) * 4 + lax.rem(shard // 4 + 4 - y, 4)
        target = (z_hi * 8 + shard // 4 * 2 + core, z_lo * 4 + shard % 4)
        copy = remote(xy_send.at[0, shard], xy_recv.at[slot], xy_ss.at[0, shard], xy_rs.at[slot], target)
        return copy, slot > 0

    def sum_pair():
        for shard in range(16):
            pair_copy(shard).wait_recv()
            both = grads[0, shard_rows(shard), :] + pair_recv[shard]
            grads[0, shard_rows(shard), :] = both
            xy_send[0, shard, 0:ROWS, :] = both.astype(BF16)
            copy, away = pair_xy_copy(shard)
            pl.when(away)(copy.start)

    def send_parts():
        for shard in range(16):
            xy_send[1, shard, 0:ROWS, :] = grads[1, shard_rows(shard), :].astype(BF16)
        for kx, ky in xy_order:
            part_copy(kx, ky).start()
        pl.when(core == 0)(part_copy(0, 0).start)

    for copy in loads[:2]:
        copy.wait()
    for copy in loads[2:]:
        copy.start()
    pair_forward(w_ref, forward_w)
    shift_store(x_ref, x3, 0)
    for image in range(BATCH):
        pre = jnp.dot(four_rows(x3, image), forward_w[...], preferred_element_type=F32)
        sig = 1.0 / (1.0 + jnp.exp(-pre))
        value = pre * sig
        put_turned(act, value, image)
        slope[image] = sig + value * (1.0 - sig)
        if image < BATCH - 1:
            shift_store(x_ref, x3, image + 1)
    for copy in loads[2:]:
        copy.wait()
    for image in range(BATCH):
        shift_store(c_ref, c3, image)

    pair_backward(w_ref, backward_w)
    out = outer_sum(act, c3, 0, 9)
    for block in range(9):
        tap = 8 - block
        grads[1, tap * CHANS : (tap + 1) * CHANS, :] = out[:, block * CHANS : (block + 1) * CHANS]

    pl.semaphore_wait(barrier, len(peers))
    send_parts()

    def held_copy(k, source_ref):
        return remote(source_ref, held, held_ss.at[k], held_rs, held_peer(k))

    @pl.when(z_lo == y)
    def _():
        held[...] = state_ref[core]
        for k in range(1, 4):
            held_copy(k, held).start()

    for image in range(BATCH):
        back = jnp.dot(four_rows(c3, image), backward_w[...], preferred_element_type=F32)
        put_turned(dpre, back * slope[image], image)

    def first_layer(first, last):
        out = outer_sum(dpre, x3, first, last)
        for tap in range(first, last):
            block = out[:, (tap - first) * CHANS : (tap + 1 - first) * CHANS]
            grads[0, tap * CHANS : (tap + 1) * CHANS, :] = block.T

    first_layer(0, 6)

    @pl.when(core == 1)
    def _():
        send_pair(0, 10)

    first_layer(6, 9)

    @pl.when(core == 1)
    def _():
        send_pair(10, 16)

    @pl.when(core == 0)
    def _():
        sum_pair()

    def sum_parts(layer, others):
        acc = grads[layer, shard_rows(own), :]
        for kx, ky in [(0, 0)] + xy_steps:
            for other in range(others):
                slot = other * 16 + kx * 4 + ky
                if slot:
                    ref = xy_recv.at[slot]
                    remote(ref, ref, xy_ss.at[0, 0], xy_rs.at[slot], partner).wait_recv()
                    acc = acc + xy_recv[slot, 0:ROWS, :].astype(F32)
        z_parts[z, 0:ROWS, :] = acc.astype(BF16)

    @pl.when(core == 0)
    def _():
        sum_parts(0, 1)

    @pl.when(core == 1)
    def _():
        sum_parts(1, 2)

    def z_copy(kz, place):
        return remote(z_parts.at[place], z_parts.at[place], z_ss.at[kz], z_rs.at[kz], z_peer(kz))

    for kz in z_order:
        z_copy(kz, z).start()
    for kz in z_order[::-1]:
        z_copy(kz, lax.rem(z + 8 - kz, 8)).wait_recv()
    z_part = [z_parts[k, 0:ROWS, :].astype(F32) for k in range(8)]
    halves = [(z_part[k] + z_part[k + 1]) + (z_part[k + 2] + z_part[k + 3]) for k in (0, 4)]
    whole = halves[0] + halves[1]

    @pl.when(z_lo != y)
    def _():
        held_copy(1, held).wait_recv()

    slab = adamw(whole, held[0], held[1], held[2])[0].astype(BF16)
    gathered[y * 4 + x, 0:ROWS, :] = slab

    def gat_copy(kx, ky, slot):
        ref = gathered.at[slot]
        return remote(ref, ref, gat_ss.at[kx * 4 + ky], gat_rs.at[kx * 4 + ky], xy_peer(kx, ky))

    def source(kx, ky):
        return place(4 - kx, 4 - ky)

    def fwd_copy(layer, kx, ky):
        slot = source(kx, ky)
        k = kx * 4 + ky
        return remote(gathered.at[slot], gathered_out.at[layer, slot], fwd_ss.at[k], fwd_rs.at[k], partner)

    for kx, ky in xy_order:
        gat_copy(kx, ky, source(0, 0)).start()
    fwd_copy(core, 0, 0).start()

    def t_copy(ky):
        return remote(totals, totals, t_ss.at[ky], t_rs, xy_peer(0, ky))

    @pl.when(z_lo == y)
    def _():
        totals[...] = whole
        for ky in (2, 1, 3):
            t_copy(ky).start()

    @pl.when(core == 0)
    def _():
        part_copy(0, 0).wait_send()
        for shard in range(16):
            copy, away = pair_xy_copy(shard)
            pl.when(away)(copy.wait_send)

    @pl.when(core == 1)
    def _():
        for k in range(16):
            pair_copy(k).wait_send()

    for kx, ky in xy_steps:
        part_copy(kx, ky).wait_send()
    for kz in z_order:
        z_copy(kz, z).wait_send()

    @pl.when(z_lo == y)
    def _():
        for k in range(1, 4):
            held_copy(k, held).wait_send()

    def forward(steps):
        for kx, ky in steps:
            gat_copy(kx, ky, source(kx, ky)).wait_recv()
            fwd_copy(core, kx, ky).start()

    forward(xy_steps[:3])

    @pl.when(z_lo != y)
    def _():
        t_copy(1).wait_recv()

    tot = remote(totals, totals_out.at[core], tot_ss, tot_rs, partner)
    tot.start()
    puts = [
        pltpu.make_async_copy(totals, totals_out.at[core], put_s.at[0]),
        pltpu.make_async_copy(gathered, gathered_out.at[core], put_s.at[1]),
    ]
    puts[0].start()
    forward(xy_steps[3:])
    puts[1].start()
    for kx, ky in xy_steps:
        gat_copy(kx, ky, source(0, 0)).wait_send()

    @pl.when(z_lo == y)
    def _():
        for k in range(1, 4):
            t_copy(k).wait_send()

    remote(totals, totals_out.at[1 - core], tot_ss, tot_rs, partner).wait_recv()
    for kx, ky in xy_steps + [(0, 0)]:
        fwd_copy(1 - core, kx, ky).wait_recv()
    for k in range(16):
        fwd_copy(core, k // 4, k % 4).wait_send()
    tot.wait_send()
    for copy in puts:
        copy.wait()


def finish_kernel(gathered_hbm, totals_hbm, master_hbm, first_hbm, second_hbm,
                  weights_hbm, master_out, first_out, second_out,
                  gathered, weights, held, new, load_s, state_s, store_s, new_s):
    loads, stores = [], []
    for k in range(4):
        layer, part = k // 2, pl.ds(k % 2 * 8, 8)
        loads.append(pltpu.make_async_copy(gathered_hbm.at[layer, part], gathered.at[layer, part], load_s.at[k]))
        rows = pl.ds(k % 2 * 8 * ROWS, 8 * ROWS)
        stores.append(pltpu.make_async_copy(weights.at[layer, rows], weights_hbm.at[layer, rows], store_s.at[k]))
    states = [
        pltpu.make_async_copy(src, held.at[k], state_s.at[k])
        for k, src in enumerate((totals_hbm, master_hbm, first_hbm, second_hbm))
    ]
    for copy in states + loads:
        copy.start()
    for copy in states:
        copy.wait()
    for k, value in enumerate(adamw(held[0], held[1], held[2], held[3])):
        new[k] = value
        store = pltpu.make_async_copy(new.at[k], (master_out, first_out, second_out)[k], new_s.at[k])
        store.start()
        stores.append(store)
    for k in range(4):
        loads[k].wait()
        for two in range(k % 2 * 4, k % 2 * 4 + 4):
            both = [gathered[k // 2, 2 * two + odd, 0:ROWS, :].astype(F32) for odd in range(2)]
            weights[k // 2, 2 * ROWS * two : 2 * ROWS * (two + 1), :] = jnp.concatenate(both, axis=0).astype(BF16)
        stores[k].start()
    for copy in stores:
        copy.wait()


def shards(inputs, cotangent, weights, master, first_moment, second_moment):
    far = pl.BlockSpec(memory_space=pltpu.HBM)
    dma = pltpu.SemaphoreType.DMA
    vmem = pltpu.VMEM
    by_pairs = (BATCH, 16, 2, 32, CHANS)
    gathered, totals = pl.pallas_call(
        step_kernel,
        out_shape=(
            jax.ShapeDtypeStruct((2, 16, SLAB, CHANS), BF16),
            jax.ShapeDtypeStruct((2, ROWS, CHANS), F32),
        ),
        in_specs=[far] * 6,
        out_specs=(far, far),
        scratch_shapes=[
            vmem(by_pairs, BF16),
            vmem(by_pairs, BF16),
            vmem(weights.shape, BF16),
            vmem((2, 3, ROWS, CHANS), F32),
            vmem((BATCH, 2, 17, 32, 3 * CHANS), BF16),
            vmem((BATCH, 2, 17, 32, 3 * CHANS), BF16),
            vmem((12 * CHANS, 2 * CHANS), BF16),
            vmem((12 * CHANS, 2 * CHANS), BF16),
            vmem((CHANS, BATCH * 1024), BF16),
            vmem((BATCH, 512, 2 * CHANS), F32),
            vmem((CHANS, BATCH * 1024), BF16),
            vmem((2, 9 * CHANS, CHANS), F32),
            vmem((16, ROWS, CHANS), F32),
            vmem((2, 16, SLAB, CHANS), BF16),
            vmem((32, SLAB, CHANS), BF16),
            vmem((8, SLAB, CHANS), BF16),
            vmem((3, ROWS, CHANS), F32),
            vmem((ROWS, CHANS), F32),
            vmem((16, SLAB, CHANS), BF16),
            dma((10,)),
            dma((16,)), dma((16,)), dma((2, 16)), dma((32,)), dma((8,)), dma((8,)), dma((4,)), dma,
            dma((4,)), dma, dma, dma, dma((16,)), dma((16,)), dma((16,)), dma((16,)), dma((2,)),
        ],
        compiler_params=pltpu.CompilerParams(collective_id=0, has_side_effects=True, vmem_limit_bytes=60 * 2**20),
        name="step",
    )(inputs.reshape(by_pairs), cotangent.reshape(by_pairs), weights, master, first_moment, second_moment)
    state = jax.ShapeDtypeStruct(master.shape, F32)
    return pl.pallas_call(
        finish_kernel,
        out_shape=(jax.ShapeDtypeStruct(weights.shape, BF16), state, state, state),
        in_specs=[far] * 5,
        out_specs=(far,) * 4,
        scratch_shapes=[
            vmem((2, 16, SLAB, CHANS), BF16),
            vmem(weights.shape, BF16),
            vmem((4,) + master.shape, F32),
            vmem((3,) + master.shape, F32),
            dma((4,)), dma((4,)), dma((4,)), dma((3,)),
        ],
        compiler_params=pltpu.CompilerParams(vmem_limit_bytes=60 * 2**20),
        name="finish",
    )(gathered, totals, master, first_moment, second_moment)


def solution(mesh):
    placed = (
        P(("grp", "dev"), None, None, None),
        P(("grp", "dev"), None, None, None),
        P(),
        P(None, "dev", None),
        P(None, "dev", None),
        P(None, "dev", None),
    )
    return jax.shard_map(
        shards,
        mesh=mesh,
        in_specs=placed,
        out_specs=(P(), P(None, "dev", None), P(None, "dev", None), P(None, "dev", None)),
        check_vma=False,
    )
```
